128 devices in a mesh: hd: 4 (over z), blk: 32 (over x, y, core).
Axes of the slice: x: 4, y: 4, z: 4, core: 2. Of those that a mesh axis runs over, the one named last changes fastest.
Arguments:
- hidden_in: bfloat16 [4, 4096, 1024], P('hd', 'blk'), may hold values from -6 to 6
- seg_start: int32 [4, 4096], P('hd', 'blk'), may hold values from 0 to 4095, as said below
- norm1_gain: bfloat16 [1024], P('blk'), may hold values from 0.5 to 1.5
- qkv_weight: bfloat16 [1024, 3072], P('blk'), may hold values from -0.1875 to 0.1875
- out_weight: bfloat16 [1024, 1024], P('blk'), may hold values from -0.75 to 0.75
- norm2_gain: bfloat16 [1024], P('blk'), may hold values from 0.5 to 1.5
- in_weight: bfloat16 [1024, 5248], P('blk'), may hold values from -0.1875 to 0.1875
- mlp_weight: bfloat16 [2624, 1024], P('blk'), may hold values from -0.125 to 0.125
- out_cotangent: bfloat16 [4, 4096, 1024], P('hd', 'blk'), may hold values from -6 to 6
Outputs:
- hidden_out: bfloat16 [4, 4096, 1024], P('hd', 'blk')
- input_grad: bfloat16 [4, 4096, 1024], P('hd', 'blk')
- qkv_grad: float32 [1024, 3072], P('blk')
- out_proj_grad: float32 [1024, 1024], P('blk')
- in_proj_grad: float32 [1024, 5248], P('blk')
- mlp_out_grad: float32 [2624, 1024], P('blk')
- norm1_grad: float32 [1024], P('blk')
- norm2_grad: float32 [1024], P('blk')
The draws below stay inside these ranges and needn't reach their ends.
Inputs may be any that keep to these rules, and one draw needn't show every extreme that they name: `seg_start`: each row never falls along the positions; a token whose value equals its own position begins a document. In every draw one row, drawn from the seed, is a single document; in every other row the last token is a document of its own.
All inputs are finite; a program needn't handle non-finite values.
Results may differ from the reference program's by a relative error of at most 0.029.
Values may be sent and summed in bfloat16 or wider, within the bound.
No kernel may reach another device: no remote copies, remote signals or barrier semaphores. Data moves between devices by JAX's collectives and lax.ppermute only.
A program may use at most 128 MiB of HBM per device.

```python
import jax
import jax.numpy as jnp
from jax import lax

D = 1024
HEADS = 16
HDIM = 64
FF = 2624
SEQS = 4
LEN = 4096


def draw_seg_start(key, part):
    key = jax.random.fold_in(key, 7)
    first, second, third = jax.random.split(key, 3)
    long_row = jax.random.randint(first, (), 0, SEQS)
    exponents = jax.random.randint(second, (SEQS, 1), 3, 11)
    rates = jnp.left_shift(jnp.ones((SEQS, 1), jnp.int32), exponents)
    marks = jax.random.randint(third, (SEQS, LEN), 0, 1 << 30) % rates == 0
    places = jnp.arange(LEN, dtype=jnp.int32)[None, :]
    row_ids = jnp.arange(SEQS, dtype=jnp.int32)[:, None]
    marks = marks | (places == 0) | (places == LEN - 1) & (row_ids != long_row)
    marks = marks & ((row_ids != long_row) | (places == 0))
    starts = jnp.where(marks, places, 0)
    return lax.cummax(starts, axis=1)


def steps_of(own_key, dims, cuts, least, high):
    loudness, own = 1.0, jax.random.fold_in(own_key, 6)
    for dim, blocks in cuts:
        heights = jnp.exp(jax.random.uniform(jax.random.fold_in(own, dim), (blocks,), jnp.float32, least / len(cuts), high / len(cuts)))
        loudness = loudness * jnp.repeat(heights, dims[dim] // blocks).reshape([-1 if axis == dim else 1 for axis in range(len(dims))])
    return loudness


def gaussian(stream_key, shape, scale, most, shards=(), kind=jnp.bfloat16):
    loudness = steps_of(stream_key, shape, shards, -0.22, 0.18) if shards else 1.0
    array = jax.random.normal(stream_key, shape, jnp.float32) * scale * loudness
    return jnp.minimum(jnp.maximum(array, -most), most).astype(kind)


def setup_inputs(seed: int = 0) -> dict:
    arg_keys = jax.random.split(jax.random.key(seed), 10)
    hidden_in = gaussian(arg_keys[0], (SEQS, LEN, D), 1.0, 6.0, ((0, 4), (1, 32)))
    seg_start = draw_seg_start(jax.random.fold_in(arg_keys[9], 71), 0)
    norm1_gain = jnp.clip(1.0 + 0.1 * jax.random.normal(arg_keys[2], (D,), jnp.float32), 0.5, 1.5).astype(jnp.bfloat16)
    qkv_weight = gaussian(arg_keys[3], (D, 3 * D), D ** -0.5, 0.1875, ((0, 32),))
    out_weight = gaussian(arg_keys[4], (D, D), (D // 16) ** -0.5, 0.75, ((0, 32),))
    norm2_gain = jnp.clip(1.0 + 0.1 * jax.random.normal(arg_keys[5], (D,), jnp.float32), 0.5, 1.5).astype(jnp.bfloat16)
    in_weight = gaussian(arg_keys[6], (D, 2 * FF), D ** -0.5, 0.1875, ((0, 32),))
    mlp_weight = gaussian(arg_keys[7], (FF, D), FF ** -0.5, 0.125, ((0, 32),))
    out_cotangent = gaussian(arg_keys[8], (SEQS, LEN, D), 1.0, 6.0, ((0, 4), (1, 32)))
    return {"hidden_in": hidden_in, "seg_start": seg_start, "norm1_gain": norm1_gain, "qkv_weight": qkv_weight, "out_weight": out_weight, "norm2_gain": norm2_gain, "in_weight": in_weight, "mlp_weight": mlp_weight, "out_cotangent": out_cotangent}


@jax.custom_vjp
def low(v):
    return lax.optimization_barrier(v.astype(jnp.bfloat16)).astype(jnp.float32)

@jax.custom_vjp
def low_back(v):
    return v

def low_keep(v):
    return (low(v), None)

def low_pass(kept, grad):
    return (grad,)

def back_keep(v):
    return (v, None)

def back_low(kept, grad):
    return (low(grad),)
low.defvjp(low_keep, low_pass)
low_back.defvjp(back_keep, back_low)
EPS = 1e-05
THETA = 160000.0
NEG = -1e+30
HIGH = lax.Precision.HIGHEST

def norm_rows(values, gains):
    average = lax.optimization_barrier(jnp.mean(values, axis=-1, keepdims=True))
    centred = values - average
    spread = lax.optimization_barrier(jnp.mean(centred * centred, axis=-1, keepdims=True))
    return centred * lax.rsqrt(spread + EPS) * gains

def rotate(values, cosine, sine):
    middle = values.shape[-1] // 2
    turned = jnp.concatenate([-values[..., middle:], values[..., :middle]], axis=-1)
    return values * cosine + turned * sine

def tables(positions):
    exponents = jnp.arange(0, HDIM, 2).astype(jnp.float32) / HDIM
    inverse = THETA ** (-exponents)
    angles = positions.astype(jnp.float32)[:, None] * inverse[None, :]
    angles = jnp.concatenate([angles, angles], axis=-1)
    return (jnp.cos(angles), jnp.sin(angles))

def attend(queries, keys_all, values_all, segments):
    length = queries.shape[0]
    rows = min(512, length)
    factor = HDIM ** (-0.5)

    def one_block(offset):
        query_blk = lax.dynamic_slice_in_dim(queries, offset, rows, 0)
        seg_blk = lax.dynamic_slice_in_dim(segments, offset, rows, 0)
        scores = low_back(jnp.einsum('thd,uhd->htu', query_blk, keys_all, precision=HIGH) * factor)
        same = seg_blk[:, None] == segments[None, :]
        scores = jnp.where(same[None], scores, NEG)
        highest = lax.optimization_barrier(jnp.max(scores, axis=-1, keepdims=True))
        expos = jnp.where(same[None], jnp.exp(scores - highest), 0.0)
        probs = low(expos / lax.optimization_barrier(jnp.sum(expos, axis=-1, keepdims=True)))
        return jnp.einsum('htu,uhd->thd', probs, values_all, precision=HIGH)
    offsets = jnp.arange(0, length, rows).astype(jnp.int32)
    blocks = lax.map(jax.checkpoint(one_block), offsets)
    return blocks.reshape(length, HEADS, HDIM)

def one_sequence(values, segments, gain_one, w_qkv, w_out, gain_two, w_in, w_mlp):
    length = values.shape[0]
    normed_one = low(norm_rows(values, gain_one))
    projected = low_back(jnp.dot(normed_one, w_qkv, precision=HIGH))
    positions = jnp.arange(length).astype(jnp.int32) - segments
    cosine, sine = tables(positions)
    cosine = cosine[:, None, :]
    sine = sine[:, None, :]
    queries = projected[:, :D].reshape(length, HEADS, HDIM)
    keys_all = projected[:, D:2 * D].reshape(length, HEADS, HDIM)
    values_all = projected[:, 2 * D:].reshape(length, HEADS, HDIM)
    queries = low(low_back(rotate(queries, cosine, sine)))
    keys_all = low(low_back(rotate(keys_all, cosine, sine)))
    values_all = low(low_back(values_all))
    attended = attend(queries, keys_all, values_all, segments)
    attended = low(low_back(attended.reshape(length, D)))
    branch = low_back(jnp.dot(attended, w_out, precision=HIGH))
    middle = values + branch
    normed_two = low(norm_rows(middle, gain_two))
    up_proj = low_back(jnp.dot(normed_two, w_in, precision=HIGH))
    activated = low(jax.nn.gelu(up_proj[:, :FF], approximate=False) * up_proj[:, FF:])
    return middle + jnp.dot(activated, w_mlp, precision=HIGH)

def reference(hidden_in, seg_start, norm1_gain, qkv_weight, out_weight, norm2_gain, in_weight, mlp_weight, out_cotangent):

    def forward(values, gain_one, w_qkv, w_out, gain_two, w_in, w_mlp):

        def scan_step(carry, pair):
            return (carry, one_sequence(pair[0], pair[1], gain_one, w_qkv, w_out, gain_two, w_in, w_mlp))
        _, outputs = lax.scan(scan_step, jnp.zeros((), jnp.float32), (values, seg_start))
        return outputs
    outputs, pullback = jax.vjp(forward, hidden_in.astype(jnp.float32), norm1_gain.astype(jnp.float32), qkv_weight.astype(jnp.float32), out_weight.astype(jnp.float32), norm2_gain.astype(jnp.float32), in_weight.astype(jnp.float32), mlp_weight.astype(jnp.float32))
    grads = pullback(out_cotangent.astype(jnp.float32))
    return (outputs.astype(jnp.bfloat16), grads[0].astype(jnp.bfloat16), grads[2], grads[3], grads[5], grads[6], grads[1], grads[4])
```

```python
import functools

import jax
import jax.numpy as jnp
from jax import lax
from jax.experimental import pallas as pl
from jax.experimental.pallas import tpu as pltpu
from jax.sharding import Mesh
from jax.sharding import PartitionSpec as P

HEADS = 16
HDIM = 64
EPS = 1e-05
THETA = 160000.0
NEG = -1e30
FLOOR = -1e29
ROWS = 128
FQ = 656
FP = 768
bf16 = jnp.bfloat16
f32 = jnp.float32
XY = ("x", "y")
XYC = ("x", "y", "c")
SMEM = pl.BlockSpec(memory_space=pltpu.SMEM)
VMEM = pl.BlockSpec(memory_space=pltpu.VMEM)


def dot_nn(a, b):
    return lax.dot_general(a, b, (((1,), (0,)), ((), ())), preferred_element_type=f32)


def dot_nt(a, b):
    return lax.dot_general(a, b, (((1,), (1,)), ((), ())), preferred_element_type=f32)


def dot_tn(a, b):
    return lax.dot_general(a, b, (((0,), (0,)), ((), ())), preferred_element_type=f32)


def fwd_kernel(tq, tk, qlo, qhi, klo, khi, q_ref, own_ref, oth_ref, sq_ref, sk_ref,
               o_ref, lse_ref, v_own, v_oth, m_ref, acc_ref):
    n = q_ref.shape[0]
    low = lax.broadcasted_iota(jnp.int32, (n, 128), 1) < HDIM
    v_own[...] = jnp.where(low, own_ref[...], jnp.ones((), bf16))
    v_oth[...] = jnp.where(low, oth_ref[...], jnp.ones((), bf16))

    def q_step(i, _):
        qs = pl.ds(pl.multiple_of(i * tq, tq), tq)
        q = q_ref[qs, :]
        m_ref[...] = jnp.full_like(m_ref, FLOOR)
        acc_ref[...] = jnp.zeros_like(acc_ref)

        def tile(j, masked):
            ks = pl.ds(pl.multiple_of(j * tk, tk), tk)
            sa = dot_nt(q, own_ref[ks, :])
            sb = dot_nt(q, oth_ref[ks, :])
            if masked:
                seg = sq_ref[qs, :]
                sa = jnp.where(seg == sk_ref[0:1, ks], sa, NEG)
                sb = jnp.where(seg == sk_ref[1:2, ks], sb, NEG)
            old = m_ref[...]
            high = jnp.maximum(
                jnp.max(sa, axis=1, keepdims=True), jnp.max(sb, axis=1, keepdims=True)
            )
            new = jnp.maximum(old, high)
            pa = jnp.exp(sa - new[:, :1]).astype(bf16)
            pb = jnp.exp(sb - new[:, :1]).astype(bf16)
            m_ref[...] = new
            acc_ref[...] = (
                acc_ref[...] * jnp.exp(old - new)
                + dot_nn(pa, v_own[ks, :])
                + dot_nn(pb, v_oth[ks, :])
            )

        def k_step(j, _):
            a, b, c, d = qlo[i], qhi[i], klo[j], khi[j]
            plain = (a == b) & (c == d) & (a == c)
            meet = (a <= d) & (c <= b)
            pl.when(plain)(lambda: tile(j, False))
            pl.when(meet & jnp.logical_not(plain))(lambda: tile(j, True))
            return 0

        lax.fori_loop(0, n // tk, k_step, 0)
        acc = acc_ref[...]
        turned = pltpu.roll(acc, HDIM, 1)
        left = lax.broadcasted_iota(jnp.int32, (tq, 128), 1) < HDIM
        o_ref[qs, :] = acc / turned
        lse_ref[qs, :] = m_ref[...] + jnp.log(jnp.where(left, turned, acc))
        return 0

    lax.fori_loop(0, n // tq, q_step, 0)


def attn_fwd(tq, tk, ranges, q, own, oth, sq, sk):
    n = q.shape[0]
    return pl.pallas_call(
        functools.partial(fwd_kernel, tq, tk),
        out_shape=(jax.ShapeDtypeStruct((n, 128), f32), jax.ShapeDtypeStruct((n, 128), f32)),
        in_specs=[SMEM] * 4 + [VMEM] * 5,
        out_specs=(VMEM, VMEM),
        scratch_shapes=[
            pltpu.VMEM((n, 128), bf16),
            pltpu.VMEM((n, 128), bf16),
            pltpu.VMEM((tq, 128), f32),
            pltpu.VMEM((tq, 128), f32),
        ],
        compiler_params=pltpu.CompilerParams(vmem_limit_bytes=48 << 20),
        cost_estimate=pl.CostEstimate(
            flops=8 * n * n * 128, bytes_accessed=1 << 22, transcendentals=2 * n * n
        ),
        name="attn_fwd",
    )(*ranges, q, own, oth, sq, sk)


def bwd_kernel(tq, tk, qlo, qhi, klo, khi, q_ref, own_ref, oth_ref, do_ref, o_ref, lse_ref,
               sq_ref, sk_ref, dq_ref, dk_ref, lrow, drow, dkacc):
    n = q_ref.shape[0]
    low = lax.broadcasted_iota(jnp.int32, (128, 128), 1) < HDIM
    for b in range(n // 128):
        s = pl.ds(b * 128, 128)
        lrow[0:1, s] = lse_ref[s, :].T[0:1, :]
        mixed = jnp.where(low, do_ref[s, :].astype(f32) * o_ref[s, :], 0.0)
        delta = jnp.sum(mixed, axis=1, keepdims=True)
        drow[0:1, s] = jnp.broadcast_to(delta, (128, 128)).T[0:1, :]
    dq_ref[...] = jnp.zeros_like(dq_ref)
    for half, k_ref in ((0, own_ref), (1, oth_ref)):

        def k_step(j, _, half=half, k_ref=k_ref):
            ks = pl.ds(pl.multiple_of(j * tk, tk), tk)
            dkacc[...] = jnp.zeros_like(dkacc)

            def tile(i, masked):
                qs = pl.ds(pl.multiple_of(i * tq, tq), tq)
                keys = k_ref[ks, :]
                q = q_ref[qs, :]
                do = do_ref[qs, :]
                s = dot_nt(keys, q)
                dp = dot_nt(keys, do)
                p = jnp.exp(s - lrow[0:1, qs])
                if masked:
                    p = jnp.where(sk_ref[half, ks, :] == sq_ref[0:1, qs], p, 0.0)
                ds = (p * (dp - drow[0:1, qs])).astype(bf16)
                dkacc[...] += dot_nn(p.astype(bf16), do) + dot_nn(ds, q)
                dq_ref[qs, :] += dot_tn(ds, keys)

            def q_step(i, _):
                a, b, c, d = qlo[i], qhi[i], klo[half, j], khi[half, j]
                plain = (a == b) & (c == d) & (a == c)
                meet = (a <= d) & (c <= b)
                pl.when(plain)(lambda: tile(i, False))
                pl.when(meet & jnp.logical_not(plain))(lambda: tile(i, True))
                return 0

            lax.fori_loop(0, n // tq, q_step, 0)
            dk_ref[half, ks, :] = dkacc[...]
            return 0

        lax.fori_loop(0, n // tk, k_step, 0)


def attn_bwd(tq, tk, ranges, q, own, oth, do, o, lse, sq, sk):
    n = q.shape[0]
    return pl.pallas_call(
        functools.partial(bwd_kernel, tq, tk),
        out_shape=(jax.ShapeDtypeStruct((n, 128), f32), jax.ShapeDtypeStruct((2, n, 128), f32)),
        in_specs=[SMEM] * 4 + [VMEM] * 8,
        out_specs=(VMEM, VMEM),
        scratch_shapes=[
            pltpu.VMEM((8, n), f32),
            pltpu.VMEM((8, n), f32),
            pltpu.VMEM((tk, 128), f32),
        ],
        compiler_params=pltpu.CompilerParams(vmem_limit_bytes=56 << 20),
        cost_estimate=pl.CostEstimate(
            flops=20 * n * n * 128, bytes_accessed=1 << 23, transcendentals=2 * n * n
        ),
        name="attn_bwd",
    )(*ranges, q, own, oth, do, o, lse, sq, sk)


def qkv_kernel(x_ref, gain_ref, w_ref, cos_ref, sin_ref, n_ref, q_ref, k_ref):
    x = x_ref[...].astype(f32)
    mid = x - jnp.mean(x, axis=1, keepdims=True)
    spread = jnp.mean(mid * mid, axis=1, keepdims=True)
    normed = (mid * lax.rsqrt(spread + EPS) * gain_ref[...]).astype(bf16)
    n_ref[...] = normed
    both = dot_nn(normed, w_ref[...])
    lane = lax.broadcasted_iota(jnp.int32, q_ref.shape, 1)

    def turn(t):
        other = jnp.where(lane < 96, pltpu.roll(t, 96, 1), pltpu.roll(t, 32, 1))
        return t * cos_ref[...] + other * sin_ref[...]

    first, second = both[:, :128], both[:, 128:]
    q_ref[...] = jnp.where(lane < HDIM, 0.0, turn(first) * HDIM**-0.5).astype(bf16)
    k_ref[...] = jnp.where(lane < HDIM, first, turn(second)).astype(bf16)


def qkv(x, gain, w, cos, sin):
    n, width = x.shape
    rows = 256
    return pl.pallas_call(
        qkv_kernel,
        grid=(n // rows,),
        out_shape=(
            jax.ShapeDtypeStruct((n, width), bf16),
            jax.ShapeDtypeStruct((n, 128), bf16),
            jax.ShapeDtypeStruct((n, 128), bf16),
        ),
        in_specs=[
            pl.BlockSpec((rows, width), lambda i: (i, 0)),
            pl.BlockSpec((1, width), lambda i: (0, 0)),
            pl.BlockSpec((width, 256), lambda i: (0, 0)),
            pl.BlockSpec((rows, 128), lambda i: (i, 0)),
            pl.BlockSpec((rows, 128), lambda i: (i, 0)),
        ],
        out_specs=(
            pl.BlockSpec((rows, width), lambda i: (i, 0)),
            pl.BlockSpec((rows, 128), lambda i: (i, 0)),
            pl.BlockSpec((rows, 128), lambda i: (i, 0)),
        ),
        compiler_params=pltpu.CompilerParams(vmem_limit_bytes=48 << 20),
        cost_estimate=pl.CostEstimate(
            flops=2 * n * width * 256, bytes_accessed=n * width * 4, transcendentals=n
        ),
        name="qkv",
    )(x, gain, w, cos, sin)


def shift(value, axis, steps):
    count = lax.axis_size(axis)
    return lax.ppermute(value, axis, [(i, (i + steps) % count) for i in range(count)])


def from_planes(value):
    return [value] + [shift(value, "z", k) for k in (1, 3, 2)]


def back_to_planes(pieces):
    return [pieces[0]] + [shift(p, "z", -k) for p, k in zip(pieces[1:], (1, 3, 2))]


def exchange(value, axes):
    return lax.all_to_all(value, axes, split_axis=0, concat_axis=0, tiled=True)


def norm_parts(values):
    mid = values - jnp.mean(values, axis=-1, keepdims=True)
    scale = lax.rsqrt(jnp.mean(mid * mid, axis=-1, keepdims=True) + EPS)
    return mid * scale, scale


def norm_back(e, z, scale):
    return (
        e - jnp.mean(e, axis=-1, keepdims=True) - z * jnp.mean(e * z, axis=-1, keepdims=True)
    ) * scale


def halves_out(rows):
    return rows.reshape(2, 64, HEADS, HDIM).transpose(2, 1, 0, 3).reshape(HEADS, 64, 128)


def halves_in(packed):
    return packed.reshape(HEADS, 64, 2, HDIM).transpose(2, 1, 0, 3).reshape(128, HEADS * HDIM)


def turned_back(t, cos, sin):
    lane = lax.broadcasted_iota(jnp.int32, t.shape, 1)
    other = jnp.where(lane < 96, jnp.roll(t, -32, 1), jnp.roll(t, 32, 1))
    return t * cos - other * sin


def shards(hidden_in, seg_start, norm1_gain, qkv_weight, out_weight, norm2_gain, in_weight,
           mlp_weight, out_cotangent):
    plane = lax.axis_index("z")
    core = lax.axis_index("c")
    x_own = hidden_in[0]
    width = x_own.shape[1]
    rows = qkv_weight.shape[0]

    parts = qkv_weight.reshape(rows, 3, HEADS, HDIM)
    starts = seg_start.astype(jnp.int32).reshape(2, HDIM)
    misc = jnp.concatenate(
        [
            jnp.concatenate([norm1_gain, norm2_gain])[None],
            (starts // 64).astype(bf16),
            (starts % 64).astype(bf16),
            jnp.zeros((rows - 5, HDIM), bf16),
        ]
    )
    sent = jnp.concatenate(
        [parts[:, 2], parts[:, 0], jnp.broadcast_to(misc[:, None], (rows, HEADS, HDIM)), parts[:, 1]],
        axis=-1,
    )
    sent = jnp.broadcast_to(sent.transpose(1, 0, 2)[:, None], (HEADS, 2, rows, 256))
    got = exchange(sent.reshape(2 * HEADS, rows, 256), XYC)
    w_head = got.reshape(width, 256)
    gain_one = got[:, 0, 128:160].reshape(1, width).astype(f32)
    gain_two = got[:, 0, 160:192].reshape(1, width).astype(f32)
    seg_all = (got[:, 1:3, 128:192].astype(jnp.int32) * 64 + got[:, 3:5, 128:192].astype(jnp.int32)).reshape(
        HEADS, 2, ROWS
    )
    seg_own = jnp.where(core == 0, seg_all[:, 0], seg_all[:, 1]).reshape(-1)
    seg_oth = jnp.where(core == 0, seg_all[:, 1], seg_all[:, 0]).reshape(-1)
    tokens = seg_own.shape[0]
    places = (jnp.arange(HEADS)[:, None] * 2 + core) * ROWS + jnp.arange(ROWS)[None]
    exponents = jnp.arange(0, HDIM, 2).astype(f32) / HDIM
    inverse = THETA ** (-exponents)
    angles = (places.reshape(-1) - seg_own).astype(f32)[:, None] * inverse[None]
    cosine, sine = jnp.cos(angles), jnp.sin(angles)
    cosine = jnp.concatenate([cosine] * 4, axis=1)
    sine = jnp.concatenate([-sine, sine, -sine, sine], axis=1)

    x_all = lax.all_gather(x_own, XY, axis=0, tiled=True)

    def unit_columns(half):
        wide = in_weight.reshape(rows, 2, 4, FQ)[:, half]
        mine = lax.dynamic_index_in_dim(wide, plane, 1, keepdims=False)
        return jnp.pad(mine, ((0, 0), (0, FP - FQ)))

    win_own = jnp.concatenate([unit_columns(0), unit_columns(1)], axis=1)
    quarters = jnp.pad(mlp_weight, ((0, 14), (0, 0))).reshape(4, 24, width)
    quarter = lax.dynamic_index_in_dim(quarters, plane, 0, keepdims=False)
    swap = [(a * 4 + b, b * 4 + a) for a in range(4) for b in range(4)]
    quarter = lax.ppermute(quarter, ("z", "x"), swap)
    bundle = jnp.concatenate(
        [
            win_own.reshape(rows, 3, 512).transpose(1, 0, 2).reshape(96, 512),
            quarter.reshape(24, 2, 512).transpose(1, 0, 2).reshape(48, 512),
            out_weight.reshape(rows, 2, 512).transpose(1, 0, 2).reshape(64, 512),
        ]
    )
    bundle, x_all = lax.optimization_barrier((bundle, x_all))
    bundles = lax.all_gather(bundle, XYC, axis=0, tiled=False)
    win = bundles[:, :96].reshape(32, 3, rows, 512).transpose(0, 2, 1, 3).reshape(width, 2 * FP)
    wout = bundles[:, 144:].reshape(32, 2, rows, 512).transpose(0, 2, 1, 3).reshape(width, width)
    wmlp = bundles[:, 96:144].reshape(4, 8, 2, 24, 512).transpose(1, 0, 3, 2, 4)
    wmlp = wmlp.reshape(8, 96, width)[:, :82].reshape(FQ, width)
    wmlp = jnp.pad(wmlp, ((0, FP - FQ), (0, 0)))
    wqkv_own = jnp.concatenate(
        [
            jnp.concatenate([parts[:, 2], parts[:, 0]], axis=-1).reshape(rows, 2 * width),
            parts[:, 1].reshape(rows, width),
        ],
        axis=1,
    )
    wqkv_own, bundles_done = lax.optimization_barrier((wqkv_own, bundles))
    wqkv = lax.all_gather(wqkv_own, XYC, axis=0, tiled=True)

    cot = out_cotangent[0]
    cot_all = jnp.concatenate(from_planes(cot))

    normed_one, queries, keys = qkv(x_all, gain_one, w_head, cosine, sine)
    keys_oth = shift(keys, "c", 1)

    def bounds(seg, size):
        tiles = seg.reshape(-1, size)
        return tiles[:, 0], tiles[:, -1]

    def first_last(size, sizek):
        qlo, qhi = bounds(seg_own, size)
        olo, ohi = bounds(seg_own, sizek)
        tlo, thi = bounds(seg_oth, sizek)
        return qlo, qhi, olo, ohi, tlo, thi

    qlo, qhi, olo, ohi, tlo, thi = first_last(512, 1024)
    ranges_f = (qlo, qhi, jnp.minimum(olo, tlo), jnp.maximum(ohi, thi))
    o, lse = attn_fwd(
        512, 1024, ranges_f, queries, keys, keys_oth, seg_own[:, None], jnp.stack([seg_own, seg_oth])
    )
    o_heads = o[:, :HDIM].astype(bf16).reshape(HEADS, 2, 64, HDIM).transpose(0, 2, 1, 3)
    o_tok = halves_in(exchange(o_heads.reshape(HEADS, 64, 128), XY))

    middle = x_own.astype(f32) + dot_nn(o_tok, wout)
    z_two, scale_two = norm_parts(middle)
    normed_two = (z_two * gain_two).astype(bf16)
    normed_all = jnp.concatenate(from_planes(normed_two))
    up = dot_nn(normed_all, win)
    first, second = up[:, :FP], up[:, FP:]
    cdf = 0.5 * (1.0 + lax.erf(first * (0.5**0.5)))
    slope = cdf + first * jnp.exp(-0.5 * first * first) * (1.0 / (2.0 * jnp.pi) ** 0.5)
    gated = first * cdf
    act = (gated * second).astype(bf16)
    d_act = dot_nt(cot_all, wmlp)
    d_up = jnp.concatenate([d_act * second * slope, d_act * gated], axis=1).astype(bf16)
    d_normed = dot_nt(d_up, win).astype(bf16)
    d_normed = back_to_planes([d_normed[i * ROWS : (i + 1) * ROWS] for i in range(4)])
    d_normed = sum(d.astype(f32) for d in d_normed)
    d_mid = cot.astype(f32) + norm_back(d_normed * gain_two, z_two, scale_two)
    d_mid_low = d_mid.astype(bf16)
    d_o = dot_nt(d_mid_low, wout).astype(bf16)
    do_heads = exchange(halves_out(d_o), XY)
    do_rows = do_heads.reshape(HEADS, 64, 2, HDIM).transpose(0, 2, 1, 3).reshape(tokens, HDIM)
    do_rows = jnp.pad(do_rows, ((0, 0), (0, HDIM)))

    out = dot_nn(act, wmlp).astype(bf16)
    out = back_to_planes([out[i * ROWS : (i + 1) * ROWS] for i in range(4)])
    hidden_out = (middle + sum(p.astype(f32) for p in out)).astype(bf16)

    g_in = dot_tn(normed_all, d_up).astype(bf16)
    g_mlp = dot_tn(act, cot_all).astype(bf16)[:FQ]
    g_out = dot_tn(o_tok, d_mid_low).astype(bf16)
    g_mlp = jnp.pad(g_mlp.reshape(8, 82, width), ((0, 0), (0, 14), (0, 0)))
    g_mlp = g_mlp.reshape(8, 4, 24, 2, 512).transpose(1, 0, 3, 2, 4).reshape(32, 48, 512)
    g_all = jnp.concatenate(
        [
            g_in.reshape(32, rows, 3, 512).transpose(0, 2, 1, 3).reshape(32, 96, 512),
            g_mlp,
            g_out.reshape(32, rows, 2, 512).transpose(0, 2, 1, 3).reshape(32, 64, 512),
        ],
        axis=1,
    )
    g_sum = lax.psum_scatter(g_all, XYC, scatter_dimension=0, tiled=True)[0]
    g_swapped = lax.ppermute(g_sum[96:144], ("z", "x"), swap)
    g_sum = jnp.concatenate([g_sum[:96], g_swapped, g_sum[144:]])
    g_planes = from_planes(g_sum)
    order = [(plane - k) % 4 for k in (0, 1, 3, 2)]

    def by_plane(part):
        stacked = jnp.zeros((4, *part[0].shape), part[0].dtype)
        for piece, place in zip(part, order):
            stacked = lax.dynamic_update_index_in_dim(stacked, piece, place, 0)
        return stacked

    gi = by_plane([g[:96] for g in g_planes]).reshape(4, 3, rows, 512).transpose(2, 0, 1, 3)
    gi = gi.reshape(rows, 4, 2, FP)[..., :FQ].transpose(0, 2, 1, 3).reshape(rows, 8 * FQ).astype(f32)
    gm = by_plane([g[96:144] for g in g_planes]).reshape(4, 2, 24, 512).transpose(0, 2, 1, 3)
    gm = gm.reshape(96, width)[:82].astype(f32)
    go = sum(g[144:].astype(f32) for g in g_planes).reshape(2, rows, 512).transpose(1, 0, 2)
    go = go.reshape(rows, width)
    grad_two = jnp.sum(gi * in_weight.astype(f32), axis=1) / norm2_gain.astype(f32)

    qlo, qhi, olo, ohi, tlo, thi = first_last(1024, 1024)
    ranges_b = (qlo, qhi, jnp.stack([olo, tlo]), jnp.stack([ohi, thi]))
    dq, dk = attn_bwd(
        1024, 1024, ranges_b, queries, keys, keys_oth, do_rows, o, lse,
        seg_own[None], jnp.stack([seg_own, seg_oth])[:, :, None],
    )
    dk = dk[0] + shift(dk[1].astype(bf16), "c", 1).astype(f32)
    lane = lax.broadcasted_iota(jnp.int32, dk.shape, 1)
    d_first = jnp.where(lane < HDIM, dk, turned_back(dq * HDIM**-0.5, cosine, sine)).astype(bf16)
    d_second = turned_back(dk, cosine, sine).astype(bf16)
    d_keys = d_second[:, HDIM:].reshape(HEADS, 2, 64, HDIM).transpose(0, 2, 1, 3)
    d_sent = jnp.concatenate([d_first.reshape(HEADS, ROWS, 128), d_keys.reshape(HEADS, 64, 128)], axis=1)
    d_got = exchange(d_sent, XY)
    d_proj = jnp.concatenate(
        [
            d_got[:, :ROWS].transpose(1, 0, 2).reshape(ROWS, 2 * width),
            halves_in(d_got[:, ROWS:]),
        ],
        axis=1,
    )
    d_normed_one = dot_nt(d_proj, wqkv)
    z_one, scale_one = norm_parts(x_own.astype(f32))
    input_grad = (d_mid + norm_back(d_normed_one * gain_one, z_one, scale_one)).astype(bf16)

    g_head = dot_tn(normed_one, jnp.concatenate([d_first, d_second], axis=1)).astype(bf16)
    g_got = exchange(g_head.reshape(32, rows, 256), XYC).reshape(HEADS, 2, rows, 256)
    g_got = (g_got[:, 0].astype(f32) + g_got[:, 1].astype(f32)).astype(bf16)
    g_got = jnp.concatenate([g_got[:, :, :128], g_got[:, :, 192:]], axis=2)
    g_qkv = sum(g.astype(f32) for g in from_planes(g_got)).transpose(1, 0, 2)
    g_qkv = jnp.concatenate(
        [
            g_qkv[:, :, 64:128].reshape(rows, width),
            g_qkv[:, :, 128:].reshape(rows, width),
            g_qkv[:, :, :64].reshape(rows, width),
        ],
        axis=1,
    )
    grad_one = jnp.sum(g_qkv * qkv_weight.astype(f32), axis=1) / norm1_gain.astype(f32)
    return hidden_out[None], input_grad[None], g_qkv, go, gi, gm, grad_one, grad_two


def solution(mesh):
    fine = Mesh(mesh.devices.reshape(4, 4, 4, 2), ("z", "x", "y", "c"))
    blk = ("x", "y", "c")
    return jax.shard_map(
        shards,
        mesh=fine,
        in_specs=(
            P("z", blk, None),
            P("z", blk),
            P(blk),
            P(blk, None),
            P(blk, None),
            P(blk),
            P(blk, None),
            P(blk, None),
            P("z", blk, None),
        ),
        out_specs=(
            P("z", blk, None),
            P("z", blk, None),
            P(blk, None),
            P(blk, None),
            P(blk, None),
            P(blk, None),
            P(blk),
            P(blk),
        ),
        check_vma=False,
    )
```

```python
import functools

import jax
import jax.numpy as jnp
import numpy as np
from jax import lax
from jax.experimental import pallas as pl
from jax.experimental.pallas import tpu as pltpu
from jax.sharding import Mesh
from jax.sharding import PartitionSpec as P

HEADS = 16
HDIM = 64
EPS = 1e-05
THETA = 160000.0
NEG = -1e30
FLOOR = -1e29
ROWS = 128
UNITS = 656
BLOCK = 82
SLOT = 96
WIDE = 8 * SLOT
bf16 = jnp.bfloat16
f32 = jnp.float32
XY = ("x", "y")
YC = ("y", "c")
XYC = ("x", "y", "c")
SMEM = pl.BlockSpec(memory_space=pltpu.SMEM)
VMEM = pl.BlockSpec(memory_space=pltpu.VMEM)
SHIFTS = (0, 1, 3, 2)


def dot_nn(a, b):
    return lax.dot_general(a, b, (((1,), (0,)), ((), ())), preferred_element_type=f32)


def dot_nt(a, b):
    return lax.dot_general(a, b, (((1,), (1,)), ((), ())), preferred_element_type=f32)


def dot_tn(a, b):
    return lax.dot_general(a, b, (((0,), (0,)), ((), ())), preferred_element_type=f32)


def shape(dims, dtype):
    return jax.ShapeDtypeStruct(dims, dtype)


def limits(mib):
    return pltpu.CompilerParams(vmem_limit_bytes=mib << 20)


def cost(us):
    return pl.CostEstimate(flops=int(us * 1.1e9), bytes_accessed=int(us * 3.4e6), transcendentals=0)


def weight_part(rows, first, blocks=32):
    return pl.BlockSpec((blocks, rows, 256), lambda i: (0, first // rows, 0))


def whole(*dims):
    return pl.BlockSpec(dims, lambda i: (0,) * len(dims))


def left_lanes(dims):
    return lax.broadcasted_iota(jnp.int32, dims, len(dims) - 1) < HDIM


def swapped(v):
    return pltpu.roll(v, HDIM, 1)


def norm_parts(values):
    mid = values - jnp.mean(values, axis=-1, keepdims=True)
    scale = lax.rsqrt(jnp.mean(mid * mid, axis=-1, keepdims=True) + EPS)
    return mid * scale, scale


def norm_back(e, z, scale):
    return (
        e - jnp.mean(e, axis=-1, keepdims=True) - z * jnp.mean(e * z, axis=-1, keepdims=True)
    ) * scale


def unpack_pair(even, odd):
    left = left_lanes(even.shape)
    top = jnp.where(left, even, swapped(odd))
    bottom = jnp.where(left, swapped(even), odd)
    return jnp.concatenate([top, bottom], axis=0)


def pack_pair(rows):
    top, bottom = rows[:64], rows[64:]
    left = left_lanes(top.shape)
    return jnp.where(left, top, swapped(bottom)), jnp.where(left, swapped(top), bottom)


def columns(rows_ref, cols_ref, k):
    for b in range(rows_ref.shape[1] // ROWS):
        s = pl.ds(b * ROWS, ROWS)
        cols_ref[s, :] = jnp.broadcast_to(rows_ref[k : k + 1, s], (ROWS, ROWS)).T


def fwd_kernel(tq, tk, qlo, qhi, klo, khi, q_ref, own_ref, oth_ref, seg_ref,
               pack_ref, o_ref, lse_ref, v_own, v_oth, m_ref, acc_ref, sq_ref):
    n = q_ref.shape[0]
    low = left_lanes((n, 128))
    v_own[...] = jnp.where(low, own_ref[...], jnp.ones((), bf16))
    v_oth[...] = jnp.where(low, oth_ref[...], jnp.ones((), bf16))
    pl.when(qlo[0] != qhi[n // tq - 1])(lambda: columns(seg_ref, sq_ref, 0))

    def q_step(i, _):
        qs = pl.ds(pl.multiple_of(i * tq, tq), tq)
        q = q_ref[qs, :]
        m_ref[...] = jnp.full_like(m_ref, FLOOR)
        acc_ref[...] = jnp.zeros_like(acc_ref)

        def tile(j, masked):
            ks = pl.ds(pl.multiple_of(j * tk, tk), tk)
            sa = dot_nt(q, own_ref[ks, :])
            sb = dot_nt(q, oth_ref[ks, :])
            if masked:
                seg = sq_ref[qs, 0:1]
                sa = jnp.where(seg == seg_ref[0:1, ks], sa, NEG)
                sb = jnp.where(seg == seg_ref[1:2, ks], sb, NEG)
            old = m_ref[...]
            high = jnp.maximum(
                jnp.max(sa, axis=1, keepdims=True), jnp.max(sb, axis=1, keepdims=True)
            )
            new = jnp.maximum(old, high)
            pa = jnp.exp(sa - new[:, :1]).astype(bf16)
            pb = jnp.exp(sb - new[:, :1]).astype(bf16)
            m_ref[...] = new
            acc_ref[...] = (
                acc_ref[...] * jnp.exp(old - new)
                + dot_nn(pa, v_own[ks, :])
                + dot_nn(pb, v_oth[ks, :])
            )

        def k_step(j, _):
            a, b, c, d = qlo[i], qhi[i], klo[j], khi[j]
            plain = (a == b) & (c == d) & (a == c)
            meet = (a <= d) & (c <= b)
            pl.when(plain)(lambda: tile(j, False))
            pl.when(meet & jnp.logical_not(plain))(lambda: tile(j, True))
            return 0

        lax.fori_loop(0, n // tk, k_step, 0)
        acc = acc_ref[...]
        turned = swapped(acc)
        left = left_lanes((tq, 128))
        o = jnp.where(left, acc / turned, 0.0)
        o_ref[qs, :] = o.astype(bf16)
        lse = m_ref[...] + jnp.log(jnp.where(left, turned, acc))
        half = left_lanes((64, 128))
        for b in range(tq // ROWS):
            block = slice(b * ROWS, (b + 1) * ROWS)
            lse_ref[0:1, pl.ds(pl.multiple_of(i * tq + b * ROWS, ROWS), ROWS)] = lse[block].T[0:1]
            upper, lower = o[block][:64], swapped(o[block][64:])
            pack_ref[i * (tq // ROWS) + b] = jnp.where(half, upper, lower).astype(bf16)
        return 0

    lax.fori_loop(0, n // tq, q_step, 0)


def attn_fwd(tq, tk, ranges, q, own, oth, seg):
    n = q.shape[0]
    return pl.pallas_call(
        functools.partial(fwd_kernel, tq, tk),
        out_shape=(shape((n // ROWS, 64, 128), bf16), shape((n, 128), bf16), shape((1, n), f32)),
        in_specs=[SMEM] * 4 + [VMEM] * 4,
        out_specs=(VMEM, VMEM, VMEM),
        scratch_shapes=[
            pltpu.VMEM((n, 128), bf16),
            pltpu.VMEM((n, 128), bf16),
            pltpu.VMEM((tq, 128), f32),
            pltpu.VMEM((tq, 128), f32),
            pltpu.VMEM((n, 128), f32),
        ],
        compiler_params=limits(24),
        cost_estimate=cost(22),
        name="attn_fwd",
    )(*ranges, q, own, oth, seg)


def bwd_kernel(tq, tk, qlo, qhi, klo, khi, q_ref, own_ref, oth_ref, pack_ref, o_ref, lrow,
               seg_ref, dq_out, dk_own, dk_oth, do_ref, drow, dkacc, dq_ref, sk_own, sk_oth):
    n = q_ref.shape[0]
    low = left_lanes((ROWS, 128))

    @pl.when(qlo[0] != qhi[n // tq - 1])
    def _():
        columns(seg_ref, sk_own, 0)
        columns(seg_ref, sk_oth, 1)

    for b in range(n // ROWS):
        s = pl.ds(b * ROWS, ROWS)
        packed = pack_ref[b].astype(f32)
        do = jnp.where(low, jnp.concatenate([packed, swapped(packed)], axis=0), 0.0)
        do_ref[s, :] = do.astype(bf16)
        delta = jnp.sum(do * o_ref[s, :].astype(f32), axis=1, keepdims=True)
        drow[0:1, s] = jnp.broadcast_to(delta, (ROWS, 128)).T[0:1, :]
    dq_ref[...] = jnp.zeros_like(dq_ref)
    sides = ((1, oth_ref, dk_oth, sk_oth), (0, own_ref, dk_own, sk_own))
    for half, k_ref, dk_ref, sk_ref in sides:

        def k_step(j, _, half=half, k_ref=k_ref, dk_ref=dk_ref, sk_ref=sk_ref):
            ks = pl.ds(pl.multiple_of(j * tk, tk), tk)
            dkacc[...] = jnp.zeros_like(dkacc)

            def tile(i, masked):
                qs = pl.ds(pl.multiple_of(i * tq, tq), tq)
                keys = k_ref[ks, :]
                q = q_ref[qs, :]
                do = do_ref[qs, :]
                s = dot_nt(keys, q)
                dp = dot_nt(keys, do)
                p = jnp.exp(s - lrow[0:1, qs])
                if masked:
                    p = jnp.where(sk_ref[ks, 0:1] == seg_ref[0:1, qs], p, 0.0)
                ds = (p * (dp - drow[0:1, qs])).astype(bf16)
                dkacc[...] += dot_nn(p.astype(bf16), do) + dot_nn(ds, q)
                dq_ref[qs, :] += dot_tn(ds, keys)

            def q_step(i, _):
                a, b, c, d = qlo[i], qhi[i], klo[half, j], khi[half, j]
                plain = (a == b) & (c == d) & (a == c)
                meet = (a <= d) & (c <= b)
                pl.when(plain)(lambda: tile(i, False))
                pl.when(meet & jnp.logical_not(plain))(lambda: tile(i, True))
                return 0

            lax.fori_loop(0, n // tq, q_step, 0)
            dk_ref[ks, :] = dkacc[...].astype(dk_ref.dtype)
            return 0

        lax.fori_loop(0, n // tk, k_step, 0)
    dq_out[...] = (dq_ref[...] * HDIM**-0.5).astype(bf16)


def attn_bwd(tq, tk, ranges, q, own, oth, pack, o, lse, seg):
    n = q.shape[0]
    return pl.pallas_call(
        functools.partial(bwd_kernel, tq, tk),
        out_shape=(shape((n, 128), bf16), shape((n, 128), f32), shape((n, 128), bf16)),
        grid=(1,),
        in_specs=[SMEM] * 4
        + [whole(*a.shape) for a in (q, own, oth, pack, o, lse, seg)],
        out_specs=(whole(n, 128), whole(n, 128), whole(n, 128)),
        scratch_shapes=[
            pltpu.VMEM((n, 128), bf16),
            pltpu.VMEM((8, n), f32),
            pltpu.VMEM((tk, 128), f32),
            pltpu.VMEM((n, 128), f32),
            pltpu.VMEM((n, 128), f32),
            pltpu.VMEM((n, 128), f32),
        ],
        compiler_params=limits(60),
        cost_estimate=cost(120),
        name="attn_bwd",
    )(*ranges, q, own, oth, pack, o, lse, seg)


def heads_kernel(w_ref, gains_ref, seg_ref, sent_ref, wqkv_ref):
    left = left_lanes((32, 128))
    row = lax.broadcasted_iota(jnp.int32, (32, 128), 0)
    seg = jnp.broadcast_to(seg_ref[...], (32, 128))
    high, rest = (seg >> 6).astype(f32), (seg & 63).astype(f32)
    misc = jnp.broadcast_to(gains_ref[...], (32, 128))
    for k, part in enumerate((high, swapped(high), rest, swapped(rest))):
        misc = jnp.where(row == k + 1, part, misc)
    for p in range(HEADS // 2):
        q, k, v = (
            w_ref[:, 1024 * i + 128 * p : 1024 * i + 128 * (p + 1)].astype(f32) for i in range(3)
        )
        even = jnp.where(left, v, swapped(q)).astype(bf16)
        odd = jnp.where(left, swapped(v), q).astype(bf16)
        even_k = jnp.where(left, misc, swapped(k)).astype(bf16)
        odd_k = jnp.where(left, misc, k).astype(bf16)
        for c in range(2):
            sent_ref[4 * p + c, :, :128] = even
            sent_ref[4 * p + c, :, 128:] = even_k
            sent_ref[4 * p + 2 + c, :, :128] = odd
            sent_ref[4 * p + 2 + c, :, 128:] = odd_k
        wqkv_ref[:, 256 * p : 256 * p + 128] = even
        wqkv_ref[:, 256 * p + 128 : 256 * (p + 1)] = odd
        wqkv_ref[:, 2048 + 128 * p : 2048 + 128 * (p + 1)] = k.astype(bf16)


def heads_out(w, gains, seg):
    return pl.pallas_call(
        heads_kernel,
        out_shape=(shape((32, 32, 256), bf16), shape((32, 3072), bf16)),
        in_specs=[VMEM] * 3,
        out_specs=(VMEM, VMEM),
        compiler_params=limits(16),
        cost_estimate=cost(1),
        name="heads_out",
    )(w, gains, seg)


def bundle_kernel(plane_ref, in_ref, spread_ref, quarter_ref, out_ref, bundle_ref):
    for z in range(4):

        @pl.when(plane_ref[0] == z)
        def _(z=z):
            for half in range(2):
                part = in_ref[:, (4 * half + z) * UNITS : (4 * half + z + 1) * UNITS]
                units = dot_nn(part, spread_ref[...]).astype(bf16)
                for j in range(3):
                    bundle_ref[96 * half + 32 * j : 96 * half + 32 * (j + 1), :] = units[
                        :, 256 * j : 256 * (j + 1)
                    ]

    bundle_ref[192:OUT_FIRST, :] = quarter_ref[...]
    for j in range(4):
        bundle_ref[OUT_FIRST + 32 * j : OUT_FIRST + 32 * (j + 1), :] = out_ref[
            :, 256 * j : 256 * (j + 1)
        ]


def bundle_out(plane, w_in, spread, quarter, w_out):
    return pl.pallas_call(
        bundle_kernel,
        out_shape=shape((416, 256), bf16),
        in_specs=[SMEM] + [VMEM] * 4,
        out_specs=VMEM,
        compiler_params=limits(16),
        cost_estimate=cost(1),
        name="bundle_out",
    )(plane, w_in, spread, quarter, w_out)


def qkv_kernel(sizes, *refs):
    place = refs[0]
    pieces = refs[1 : 1 + len(sizes)]
    gain_ref, w_ref, cos_ref, sin_ref, n_ref, q_ref, k_ref = refs[1 + len(sizes) :]
    gain = gain_ref[...]
    w = w_ref[...]
    group = 0
    for piece, size in zip(pieces, sizes):
        z, _ = norm_parts(piece[...].astype(f32))
        normed = (z * gain).astype(bf16)
        both = dot_nn(normed, w)
        for g in range(size // 64):
            to = pl.ds(pl.multiple_of(place[group] * 64, 64), 64)
            group += 1
            mine = slice(g * 64, (g + 1) * 64)
            cos, sin = cos_ref[to, :], sin_ref[to, :]
            lane = lax.broadcasted_iota(jnp.int32, (64, 128), 1)

            def turn(t):
                other = jnp.where(lane < 96, pltpu.roll(t, 96, 1), pltpu.roll(t, 32, 1))
                return t * cos + other * sin

            first, second = both[mine, :128], both[mine, 128:]
            q_ref[to, :] = jnp.where(lane < HDIM, 0.0, turn(first) * HDIM**-0.5).astype(bf16)
            n_ref[to, :] = normed[mine]
            k_ref[to, :] = jnp.where(lane < HDIM, first, turn(second)).astype(bf16)


def qkv(place, pieces, gain, w, cos, sin):
    n, width = cos.shape[0], pieces[0].shape[1]
    sizes = tuple(p.shape[0] for p in pieces)
    return pl.pallas_call(
        functools.partial(qkv_kernel, sizes),
        out_shape=(shape((n, width), bf16), shape((n, 128), bf16), shape((n, 128), bf16)),
        in_specs=[SMEM] + [VMEM] * (len(pieces) + 4),
        out_specs=(VMEM, VMEM, VMEM),
        compiler_params=limits(24),
        cost_estimate=cost(6),
        name="qkv",
    )(place, *pieces, gain, w, cos, sin)


OUT_FIRST = 288
OUT_PARTS = [weight_part(32, OUT_FIRST + 32 * j) for j in range(4)]


def proj_kernel(pack_ref, x_ref, gain_ref, w0, w1, w2, w3, n_ref, h_ref, o_ref):
    for p in range(HEADS // 2):
        both = unpack_pair(pack_ref[2 * p].astype(f32), pack_ref[2 * p + 1].astype(f32))
        o_ref[:, p * 128 : (p + 1) * 128] = both.astype(bf16)
    o = o_ref[...]
    for j, w in enumerate((w0, w1, w2, w3)):
        cols = slice(256 * j, 256 * (j + 1))
        h_ref[:, cols] = x_ref[:, cols].astype(f32) + dot_nn(o, w[...].reshape(1024, 256))
    z, _ = norm_parts(h_ref[...])
    n_ref[...] = (z * gain_ref[...]).astype(bf16)


def proj(pack, x, gain, bundle):
    n, width = x.shape
    return pl.pallas_call(
        proj_kernel,
        grid=(1,),
        out_shape=(shape((n, width), bf16), shape((n, width), f32), shape((n, width), bf16)),
        in_specs=[whole(*pack.shape), whole(n, width), whole(1, width), *OUT_PARTS],
        out_specs=(whole(n, width), whole(n, width), whole(n, width)),
        compiler_params=limits(60),
        cost_estimate=cost(3),
        name="proj",
    )(pack, x, gain, bundle, bundle, bundle, bundle)


def units_kernel(*refs):
    n_refs, g_refs = refs[:4], refs[4:8]
    win_ref, wmlp_ref, act_ref, dup_ref, n_all, g_all = refs[8:14]
    d_refs = refs[14:]
    for i in range(4):
        n_all[i * ROWS : (i + 1) * ROWS, :] = n_refs[i][...]
        g_all[i * ROWS : (i + 1) * ROWS, :] = g_refs[i][...]
    normed = n_all[...]
    g = g_all[...]

    def win(j):
        return win_ref[:, 32 * j : 32 * (j + 1), :].reshape(1024, 256)

    def wmlp(a):
        return wmlp_ref[8 * a : 8 * (a + 1)].reshape(WIDE, 256)

    for j in range(3):
        cols = slice(256 * j, 256 * (j + 1))
        first = dot_nn(normed, win(j))
        second = dot_nn(normed, win(j + 3))
        d_act = sum(
            dot_nt(g[:, 256 * a : 256 * (a + 1)], wmlp(a)[cols]) for a in range(4)
        )
        cdf = 0.5 * (1.0 + lax.erf(first * (0.5**0.5)))
        slope = cdf + first * (jnp.exp(-0.5 * first * first) * (1.0 / (2.0 * jnp.pi) ** 0.5))
        gated = first * cdf
        act_ref[:, cols] = (gated * second).astype(bf16)
        dup_ref[:, cols] = (d_act * second * slope).astype(bf16)
        dup_ref[:, WIDE + 256 * j : WIDE + 256 * (j + 1)] = (d_act * gated).astype(bf16)
    total = sum(dot_nt(dup_ref[:, 256 * j : 256 * (j + 1)], win(j)) for j in range(6))
    for i in range(4):
        d_refs[i][...] = total[i * ROWS : (i + 1) * ROWS].astype(bf16)


def units(normed, cots, bundle):
    n, width = normed[0].shape
    tokens = 4 * n
    return pl.pallas_call(
        units_kernel,
        grid=(1,),
        out_shape=(
            shape((tokens, WIDE), bf16),
            shape((tokens, 2 * WIDE), bf16),
            shape((tokens, width), bf16),
            shape((tokens, width), bf16),
            *[shape((n, width), bf16)] * 4,
        ),
        in_specs=[whole(n, width)] * 8 + [weight_part(192, 0), weight_part(SLOT, 192)],
        out_specs=(
            whole(tokens, WIDE),
            whole(tokens, 2 * WIDE),
            whole(tokens, width),
            whole(tokens, width),
            *[whole(n, width)] * 4,
        ),
        compiler_params=limits(56),
        cost_estimate=cost(11),
        name="units",
    )(*normed, *cots, bundle, bundle)


def unit_grads_kernel(act_ref, dup_ref, n_all, g_all, out_hbm, out_ref, sem):
    act = act_ref[...].T
    for a in range(4):
        cols = slice(256 * a, 256 * (a + 1))
        grad = dot_nn(act, g_all[:, cols]).astype(bf16)
        for i in range(8):
            out_ref[i * 4 + a, 192:OUT_FIRST, :] = grad[SLOT * i : SLOT * (i + 1)]
    normed = n_all[...].T
    for j in range(6):
        grad = dot_nn(normed, dup_ref[:, 256 * j : 256 * (j + 1)]).astype(bf16)
        for b in range(32):
            out_ref[(b % 8) * 4 + b // 8, 32 * j : 32 * (j + 1), :] = grad[32 * b : 32 * (b + 1)]
    copy = pltpu.make_async_copy(out_ref, out_hbm.at[:, pl.ds(0, OUT_FIRST)], sem)
    copy.start()
    copy.wait()


HBM = pl.BlockSpec(memory_space=pltpu.HBM)


def unit_grads(act, dup, n_all, g_all):
    tokens, width = n_all.shape
    return pl.pallas_call(
        unit_grads_kernel,
        out_shape=shape((32, 416, 256), bf16),
        grid=(1,),
        in_specs=[whole(*a.shape) for a in (act, dup, n_all, g_all)],
        out_specs=HBM,
        scratch_shapes=[pltpu.VMEM((32, OUT_FIRST, 256), bf16), pltpu.SemaphoreType.DMA],
        compiler_params=limits(60),
        cost_estimate=cost(2),
        name="unit_grads",
    )(act, dup, n_all, g_all)


def out_grad_kernel(o_ref, da_ref, in_hbm, out_hbm, out_ref, sem):
    del in_hbm
    grad = dot_tn(o_ref[...], da_ref[...]).astype(bf16)
    for b in range(32):
        for j in range(4):
            out_ref[(b % 8) * 4 + b // 8, 32 * j : 32 * (j + 1), :] = grad[
                32 * b : 32 * (b + 1), 256 * j : 256 * (j + 1)
            ]
    copy = pltpu.make_async_copy(out_ref, out_hbm.at[:, pl.ds(OUT_FIRST, 128)], sem)
    copy.start()
    copy.wait()


def out_grad(o, da, grads):
    return pl.pallas_call(
        out_grad_kernel,
        out_shape=shape(grads.shape, bf16),
        grid=(1,),
        in_specs=[whole(*o.shape), whole(*da.shape), HBM],
        out_specs=HBM,
        scratch_shapes=[pltpu.VMEM((32, 128, 256), bf16), pltpu.SemaphoreType.DMA],
        input_output_aliases={2: 0},
        compiler_params=limits(60),
        cost_estimate=cost(1),
        name="out_grad",
    )(o, da, grads)


def unit_out_kernel(act_ref, wmlp_ref, p0, p1, p2, p3):
    act = act_ref[...]
    for a in range(4):
        cols = slice(256 * a, 256 * (a + 1))
        part = dot_nn(act, wmlp_ref[8 * a : 8 * (a + 1)].reshape(WIDE, 256)).astype(bf16)
        for i, p in enumerate((p0, p1, p2, p3)):
            p[:, cols] = part[i * ROWS : (i + 1) * ROWS]


def unit_out(act, bundle):
    return pl.pallas_call(
        unit_out_kernel,
        grid=(1,),
        out_shape=[shape((ROWS, 1024), bf16)] * 4,
        in_specs=[whole(*act.shape), weight_part(SLOT, 192)],
        out_specs=[whole(ROWS, 1024)] * 4,
        compiler_params=limits(60),
        cost_estimate=cost(0.5),
        name="unit_out",
    )(act, bundle)


def proj_back_kernel(d0, d1, d2, d3, h_ref, gain_ref, cot_ref, w0, w1, w2, w3,
                     pack_ref, dh_ref, da_ref):
    total = d0[...].astype(f32) + d1[...].astype(f32) + d2[...].astype(f32) + d3[...].astype(f32)
    z, scale = norm_parts(h_ref[...])
    dh = cot_ref[...].astype(f32) + norm_back(total * gain_ref[...], z, scale)
    dh_ref[...] = dh
    da_ref[...] = dh.astype(bf16)
    do = sum(
        dot_nt(da_ref[:, 256 * j : 256 * (j + 1)], w[...].reshape(1024, 256))
        for j, w in enumerate((w0, w1, w2, w3))
    )
    for p in range(HEADS // 2):
        even, odd = pack_pair(do[:, p * 128 : (p + 1) * 128])
        pack_ref[2 * p] = even.astype(bf16)
        pack_ref[2 * p + 1] = odd.astype(bf16)


def proj_back(ds, h, gain, cot, bundle):
    n, width = h.shape
    return pl.pallas_call(
        proj_back_kernel,
        grid=(1,),
        out_shape=(shape((HEADS, 64, 128), bf16), shape((n, width), f32), shape((n, width), bf16)),
        in_specs=[whole(n, width)] * 5 + [whole(1, width), whole(n, width), *OUT_PARTS],
        out_specs=(whole(HEADS, 64, 128), whole(n, width), whole(n, width)),
        compiler_params=limits(60),
        cost_estimate=cost(3),
        name="proj_back",
    )(*ds, h, gain, cot, bundle, bundle, bundle, bundle)


def turn_back_kernel(dq_ref, own_ref, oth_ref, cos_ref, sin_ref, n_ref, sent_ref, grad_ref, d_ref):
    for b in range(dq_ref.shape[0] // ROWS):
        s = slice(b * ROWS, (b + 1) * ROWS)
        cos, sin = cos_ref[s, :], sin_ref[s, :]
        lane = lax.broadcasted_iota(jnp.int32, (ROWS, 128), 1)

        def turn(t):
            other = jnp.where(lane < 96, pltpu.roll(t, 96, 1), pltpu.roll(t, 32, 1))
            return t * cos - other * sin

        dk = own_ref[s, :] + oth_ref[s, :].astype(f32)
        first = jnp.where(lane < HDIM, dk, turn(dq_ref[s, :].astype(f32)))
        second = jnp.where(lane < HDIM, 0.0, turn(dk))
        d_ref[s, :128] = first.astype(bf16)
        d_ref[s, 128:] = second.astype(bf16)
        sent_ref[b, :ROWS, :] = first.astype(bf16)
        packed = jnp.where(left_lanes((64, 128)), swapped(second[:64]), second[64:])
        sent_ref[b, ROWS:, :] = packed.astype(bf16)
    grad = dot_tn(d_ref[...], n_ref[...]).T
    grad_ref[...] = grad.astype(bf16).reshape(grad_ref.shape)


def turn_back(dq, own, oth, cos, sin, normed):
    n = dq.shape[0]
    return pl.pallas_call(
        turn_back_kernel,
        out_shape=(shape((n // ROWS, 192, 128), bf16), shape((32, 32, 256), bf16)),
        grid=(1,),
        in_specs=[whole(*a.shape) for a in (dq, own, oth, cos, sin, normed)],
        out_specs=(whole(n // ROWS, 192, 128), whole(32, 32, 256)),
        scratch_shapes=[pltpu.VMEM((n, 256), bf16)],
        compiler_params=limits(60),
        cost_estimate=cost(5),
        name="turn_back",
    )(dq, own, oth, cos, sin, normed)


def input_kernel(got_ref, w_ref, x_ref, gain_ref, dh_ref, out_ref, d_ref, acc_ref):
    step = pl.program_id(0)

    @pl.when(step == 0)
    def _():
        for h in range(HEADS):
            d_ref[h // 4, :, 128 * (h % 4) : 128 * (h % 4 + 1)] = got_ref[h, :ROWS, :]
        for p in range(HEADS // 2):
            both = unpack_pair(
                got_ref[2 * p, ROWS:, :].astype(f32), got_ref[2 * p + 1, ROWS:, :].astype(f32)
            )
            d_ref[4 + p // 4, :, 128 * (p % 4) : 128 * (p % 4 + 1)] = both.astype(bf16)
        acc_ref[...] = jnp.zeros_like(acc_ref)

    acc_ref[...] += dot_nt(d_ref[step], w_ref[...])

    @pl.when(step == pl.num_programs(0) - 1)
    def _():
        z, scale = norm_parts(x_ref[...].astype(f32))
        back = norm_back(acc_ref[...] * gain_ref[...], z, scale)
        out_ref[...] = (dh_ref[...] + back).astype(bf16)


def input_back(got, w, x, gain, dh):
    n, width = x.shape
    return pl.pallas_call(
        input_kernel,
        grid=(6,),
        out_shape=shape((n, width), bf16),
        in_specs=[
            whole(*got.shape),
            pl.BlockSpec((width, 512), lambda i: (0, i)),
            whole(n, width),
            whole(1, width),
            whole(n, width),
        ],
        out_specs=whole(n, width),
        scratch_shapes=[pltpu.VMEM((6, n, 512), bf16), pltpu.VMEM((n, width), f32)],
        compiler_params=limits(32),
        cost_estimate=cost(4),
        name="input_back",
    )(got, w, x, gain, dh)


def gather_kernel(head_ref, sum_ref):
    for p in range(HEADS // 2):
        even = head_ref[4 * p].astype(f32) + head_ref[4 * p + 1].astype(f32)
        odd = head_ref[4 * p + 2].astype(f32) + head_ref[4 * p + 3].astype(f32)
        left = left_lanes((32, 128))
        cols = slice(p * 128, (p + 1) * 128)
        q = jnp.where(left, swapped(even[:, :128]), odd[:, :128])
        k = jnp.where(left, swapped(even[:, 128:]), odd[:, 128:])
        v = jnp.where(left, even[:, :128], swapped(odd[:, :128]))
        for i, part in enumerate((q, k, v)):
            sum_ref[:, 1024 * i + 128 * p : 1024 * i + 128 * (p + 1)] = part.astype(bf16)


def gather_rows(head):
    return pl.pallas_call(
        gather_kernel,
        out_shape=shape((32, 3072), bf16),
        in_specs=[VMEM],
        out_specs=VMEM,
        compiler_params=limits(32),
        cost_estimate=cost(1),
        name="gather_rows",
    )(head)


def planes_kernel(a, b, c, d, w_ref, gain_ref, qkv_ref, norm_ref):
    total = (a[...].astype(f32) + b[...].astype(f32)) + (c[...].astype(f32) + d[...].astype(f32))
    qkv_ref[...] = total
    norm = jnp.sum(total * w_ref[...].astype(f32), axis=1, keepdims=True)
    norm_ref[...] = norm / gain_ref[...]


def add_planes(parts, w, gain):
    return pl.pallas_call(
        planes_kernel,
        out_shape=(shape((32, 3072), f32), shape((32, 1), f32)),
        in_specs=[VMEM] * 6,
        out_specs=(VMEM, VMEM),
        compiler_params=limits(32),
        cost_estimate=cost(1),
        name="add_planes",
    )(*parts, w, gain)


def unit_rows_kernel(plane_ref, got_ref, m0, m1, m2, m3, spread_ref, w_ref, gain_ref,
                     in_ref, mlp_ref, out_ref, norm_ref):
    spread = spread_ref[...]
    norm = jnp.zeros((32, 1), f32)
    for half in range(2):
        for z in range(4):
            chunks = [got_ref[z, 96 * half + 32 * j : 96 * half + 32 * (j + 1), :] for j in range(3)]
            grad = dot_nt(jnp.concatenate(chunks, axis=1), spread)
            cols = slice((4 * half + z) * UNITS, (4 * half + z + 1) * UNITS)
            in_ref[:, cols] = grad
            norm += jnp.sum(grad * w_ref[:, cols].astype(f32), axis=1, keepdims=True)
    for a in range(4):
        cols = slice(256 * a, 256 * (a + 1))
        part = slice(192 + 32 * a, 192 + 32 * (a + 1))
        out_ref[:, cols] = sum(got_ref[z, part, :].astype(f32) for z in range(4))
    for k, m in enumerate((m0, m1, m2, m3)):
        a = lax.rem(plane_ref[0] + k, 4)
        mlp_ref[:, pl.ds(pl.multiple_of(a * 256, 256), 256)] = m[...].astype(f32)[:BLOCK]
    norm_ref[...] = norm / gain_ref[...]


def unit_rows(plane, got, mlp, spread, w, gain):
    return pl.pallas_call(
        unit_rows_kernel,
        out_shape=(
            shape((32, 8 * UNITS), f32),
            shape((BLOCK, 1024), f32),
            shape((32, 1024), f32),
            shape((32, 1), f32),
        ),
        in_specs=[SMEM] + [VMEM] * 8,
        out_specs=(VMEM, VMEM, VMEM, VMEM),
        compiler_params=limits(32),
        cost_estimate=cost(2),
        name="unit_rows",
    )(plane, got, *mlp, spread, w, gain)


def shift(value, axis, steps):
    count = lax.axis_size(axis)
    return lax.ppermute(value, axis, [(i, (i + steps) % count) for i in range(count)])


def from_planes(value):
    return [value] + [shift(value, "z", k) for k in SHIFTS[1:]]


def back_to_planes(pieces):
    return [pieces[0]] + [shift(p, "z", -k) for p, k in zip(pieces[1:], SHIFTS[1:])]


def far(value, near, axis):
    half = value.shape[0] // 2
    behind, ahead = near
    return [value, behind, ahead, shift(behind[:half], axis, 1), shift(ahead[half:], axis, 3)]


def exchange(value, axes):
    return lax.all_to_all(value, axes, split_axis=0, concat_axis=0, tiled=True)


def shards(hidden_in, seg_start, norm1_gain, qkv_weight, out_weight, norm2_gain, in_weight,
           mlp_weight, out_cotangent):
    plane, core = lax.axis_index("z"), lax.axis_index("c")
    mine = (lax.axis_index("x"), lax.axis_index("y"))
    x_own = hidden_in[0]
    cot = out_cotangent[0]
    width = x_own.shape[1]
    rows = qkv_weight.shape[0]

    upper, lower = x_own[:64], x_own[64:]
    upper = [upper] + [shift(upper, "x", k) for k in SHIFTS[1:]]
    lower = [lower] + [shift(lower, "y", k) for k in SHIFTS[1:]]
    upper, lower = jnp.concatenate(upper), jnp.concatenate(lower)

    gains = jnp.pad(jnp.concatenate([norm1_gain, norm2_gain]), (0, HDIM)).astype(f32)[None]
    sent, wqkv = heads_out(qkv_weight, gains, seg_start)
    got = exchange(sent, XYC)
    upper, lower, got = lax.optimization_barrier((upper, lower, got))
    pieces = [upper] + [shift(upper, "y", k) for k in SHIFTS[1:]]
    pieces += [lower] + [shift(lower, "x", k) for k in SHIFTS[1:]]
    place = []
    for half in (0, 1):
        for outer in SHIFTS:
            for inner in SHIFTS:
                sx, sy = (inner, outer) if half == 0 else (outer, inner)
                place.append((((mine[0] - sx) % 4) * 4 + (mine[1] - sy) % 4) * 2 + half)
    place = jnp.stack(place).astype(jnp.int32)
    w_head = got.reshape(width, 256)
    gain_one = got[:, 0, 128:160].reshape(1, width).astype(f32)
    gain_two = got[:, 0, 160:192].reshape(1, width).astype(f32)
    high, rest = got[:, 1:3, 128:192].astype(jnp.int32), got[:, 3:5, 128:192].astype(jnp.int32)
    seg_all = (high * 64 + rest).reshape(HEADS, 2, ROWS)
    seg_own = jnp.where(core == 0, seg_all[:, 0], seg_all[:, 1]).reshape(-1)
    seg_oth = jnp.where(core == 0, seg_all[:, 1], seg_all[:, 0]).reshape(-1)
    places = (jnp.arange(HEADS)[:, None] * 2 + core) * ROWS + jnp.arange(ROWS)[None]
    exponents = jnp.arange(0, HDIM, 2).astype(f32) / HDIM
    inverse = THETA ** (-exponents)
    angles = (places.reshape(-1) - seg_own).astype(f32)[:, None] * inverse[None]
    cosine, sine = jnp.cos(angles), jnp.sin(angles)
    cosine = jnp.concatenate([cosine] * 4, axis=1)
    sine = jnp.concatenate([-sine, sine, -sine, sine], axis=1)

    unit = np.arange(UNITS)
    spread = (unit // BLOCK * SLOT + unit % BLOCK)[:, None] == np.arange(WIDE)[None]
    spread = jnp.asarray(spread, bf16)
    quarter = lax.dynamic_slice_in_dim(mlp_weight, plane * 256, 256, 1)
    quarter = jnp.pad(quarter, ((0, SLOT - BLOCK), (0, 0)))
    swap = [(a * 4 + b, b * 4 + a) for a in range(4) for b in range(4)]
    quarter = lax.ppermute(quarter, ("z", "x"), swap)
    bundle = bundle_out(plane.astype(jnp.int32)[None], in_weight, spread, quarter, out_weight)
    bundle, pieces, cosine, sine = lax.optimization_barrier((bundle, pieces, cosine, sine))
    bundle = lax.all_gather(bundle, XYC, axis=0, tiled=False)
    cots = from_planes(cot)

    normed_one, queries, keys = qkv(place, pieces, gain_one, w_head, cosine, sine)
    keys_oth = shift(keys, "c", 1)

    def bounds(seg, size):
        tiles = seg.reshape(-1, size)
        return tiles[:, 0], tiles[:, -1]

    (qlo, qhi), (olo, ohi), (tlo, thi) = bounds(seg_own, 256), bounds(seg_own, 1024), bounds(seg_oth, 1024)
    both_segs = jnp.stack([seg_own, seg_oth]).astype(f32)
    o_pack, o, lse = attn_fwd(
        256, 1024, (qlo, qhi, jnp.minimum(olo, tlo), jnp.maximum(ohi, thi)),
        queries, keys, keys_oth, both_segs,
    )
    wqkv, o_pack = lax.optimization_barrier((wqkv, o_pack))
    wqkv = lax.all_gather(wqkv, XYC, axis=0, tiled=True)
    o_got = exchange(o_pack, XY)

    normed_two, middle, o_tok = proj(o_got, x_own, gain_two, bundle)
    act, dup, n_all, g_all, *d_parts = units(from_planes(normed_two), cots, bundle)
    d_parts = back_to_planes(d_parts)
    g_sum = unit_grads(act, dup, n_all, g_all)
    d_parts, g_sum = lax.optimization_barrier((d_parts, g_sum))
    do_pack, d_mid, d_attn = proj_back(d_parts, middle, gain_two, cot, bundle)
    do_got = exchange(do_pack, XY)
    g_sum = out_grad(o_tok, d_attn, g_sum)
    act, d_attn = lax.optimization_barrier((act, d_attn))
    out_parts = unit_out(act, bundle)
    g_sum, wqkv = lax.optimization_barrier((g_sum, wqkv))
    do_got, g_sum, out_parts = lax.optimization_barrier((do_got, g_sum, out_parts))
    g_sum = lax.psum_scatter(g_sum.reshape(8, 4 * 416, 256), YC, scatter_dimension=0, tiled=False)
    out_parts = back_to_planes(out_parts)

    ranges = (olo, ohi, jnp.stack([olo, tlo]), jnp.stack([ohi, thi]))
    dq, dk_own, dk_oth = attn_bwd(1024, 1024, ranges, queries, keys, keys_oth, do_got, o, lse, both_segs)
    dk_oth, out_parts = lax.optimization_barrier((dk_oth, out_parts))
    hidden_out = (middle + sum(p.astype(f32) for p in out_parts)).astype(bf16)
    d_sent, g_head = turn_back(dq, dk_own, shift(dk_oth, "c", 1), cosine, sine, normed_one)

    g_sum, g_head = lax.optimization_barrier((g_sum, g_head))
    g_sum = lax.psum_scatter(g_sum.reshape(4, 416, 256), "x", scatter_dimension=0, tiled=False)
    g_head = exchange(g_head, XYC)
    g_head, d_sent = lax.optimization_barrier((g_head, d_sent))
    g_rows = from_planes(gather_rows(g_head))
    d_got = exchange(d_sent, XY)
    g_rows, d_got, g_sum = lax.optimization_barrier((g_rows, d_got, g_sum))

    g_mlp = []
    for k in range(4):
        pairs = [(a * 4 + b, (b - k) % 4 * 4 + a) for a in range(4) for b in range(4)]
        g_mlp.append(lax.ppermute(g_sum[192:OUT_FIRST], ("z", "x"), pairs))
    g_rest = jnp.concatenate([g_sum[:192], g_sum[OUT_FIRST:]])
    g_rest = exchange(jnp.broadcast_to(g_rest[None], (4, *g_rest.shape)), "z")
    input_grad = input_back(d_got, wqkv, x_own, gain_one, d_mid)
    gain_column = norm1_gain.astype(f32)[:, None]
    g_qkv, grad_one = add_planes(g_rows, qkv_weight, gain_column)
    g_rest, g_mlp, g_qkv, input_grad = lax.optimization_barrier((g_rest, g_mlp, g_qkv, input_grad))
    g_in, g_mlp, g_out, grad_two = unit_rows(
        plane.astype(jnp.int32)[None], g_rest, g_mlp, spread, in_weight, norm2_gain.astype(f32)[:, None]
    )
    return (
        hidden_out[None],
        input_grad[None],
        g_qkv,
        g_out,
        g_in,
        g_mlp,
        grad_one[:, 0],
        grad_two[:, 0],
    )


def solution(mesh):
    fine = Mesh(mesh.devices.reshape(4, 4, 4, 2), ("z", "x", "y", "c"))
    blk = ("x", "y", "c")
    return jax.shard_map(
        shards,
        mesh=fine,
        in_specs=(
            P("z", blk, None),
            P("z", blk),
            P(blk),
            P(blk, None),
            P(blk, None),
            P(blk),
            P(blk, None),
            P(blk, None),
            P("z", blk, None),
        ),
        out_specs=(
            P("z", blk, None),
            P("z", blk, None),
            P(blk, None),
            P(blk, None),
            P(blk, None),
            P(blk, None),
            P(blk),
            P(blk),
        ),
        check_vma=False,
    )
```

```python
import functools

import jax
import jax.numpy as jnp
import numpy as np
from jax import lax
from jax.experimental import pallas as pl
from jax.experimental.pallas import tpu as pltpu
from jax.sharding import Mesh
from jax.sharding import PartitionSpec as P

HEADS = 16
HDIM = 64
EPS = 1e-05
THETA = 160000.0
NEG = -1e30
FLOOR = -1e29
ROWS = 128
BLOCK = 82
FIRST = (0, 21, 42, 62, 82)
SLOT = 24
WIDE = 32 * SLOT
SPAN = 8 * BLOCK
OUT_FIRST = 320
BUNDLE = 448
LOG2E = 1.4426950408889634
bf16 = jnp.bfloat16
f32 = jnp.float32
XY = ("x", "y")
YC = ("y", "c")
XYC = ("x", "y", "c")
SMEM = pl.BlockSpec(memory_space=pltpu.SMEM)
VMEM = pl.BlockSpec(memory_space=pltpu.VMEM)
HBM = pl.BlockSpec(memory_space=pltpu.HBM)
SHIFTS = (0, 1, 3, 2)


def dot_nn(a, b):
    return lax.dot_general(a, b, (((1,), (0,)), ((), ())), preferred_element_type=f32)


def dot_nt(a, b):
    return lax.dot_general(a, b, (((1,), (1,)), ((), ())), preferred_element_type=f32)


def dot_tn(a, b):
    return lax.dot_general(a, b, (((0,), (0,)), ((), ())), preferred_element_type=f32)


def shape(dims, dtype):
    return jax.ShapeDtypeStruct(dims, dtype)


def limits(mib):
    return pltpu.CompilerParams(vmem_limit_bytes=mib << 20)


def cost(us):
    return pl.CostEstimate(flops=int(us * 1.1e9), bytes_accessed=int(us * 3.4e6), transcendentals=0)


def weight_part(rows, first, blocks=32):
    return pl.BlockSpec((blocks, rows, 256), lambda i: (0, first // rows, 0))


def whole(*dims):
    return pl.BlockSpec(dims, lambda i: (0,) * len(dims))


def left_lanes(dims):
    return lax.broadcasted_iota(jnp.int32, dims, len(dims) - 1) < HDIM


def swapped(v):
    return pltpu.roll(v, HDIM, 1)


def norm_parts(values):
    mid = values - jnp.mean(values, axis=-1, keepdims=True)
    scale = lax.rsqrt(jnp.mean(mid * mid, axis=-1, keepdims=True) + EPS)
    return mid * scale, scale


def norm_back(e, z, scale):
    return (
        e - jnp.mean(e, axis=-1, keepdims=True) - z * jnp.mean(e * z, axis=-1, keepdims=True)
    ) * scale


def unpack_pair(even, odd):
    left = left_lanes(even.shape)
    top = jnp.where(left, even, swapped(odd))
    bottom = jnp.where(left, swapped(even), odd)
    return jnp.concatenate([top, bottom], axis=0)


def pack_pair(rows):
    top, bottom = rows[:64], rows[64:]
    left = left_lanes(top.shape)
    return jnp.where(left, top, swapped(bottom)), jnp.where(left, swapped(top), bottom)


def columns(rows_ref, cols_ref, k):
    for b in range(rows_ref.shape[1] // ROWS):
        s = pl.ds(b * ROWS, ROWS)
        cols_ref[s, :] = jnp.broadcast_to(rows_ref[k : k + 1, s], (ROWS, ROWS)).T


def tiles(visit, qlo, qhi, klo, khi, i, j, sq, sk):
    def check(q0, q1, k0, k1, rows, cols, wide, deep, parts):
        a, b, c, d = qlo[q0], qhi[q1], klo[k0], khi[k1]
        plain = (a == b) & (c == d) & (a == c)
        mixed = (a <= d) & (c <= b) & jnp.logical_not(plain)
        pl.when(plain)(lambda: visit(rows, cols, wide, deep, False))
        pl.when(mixed)(parts)

    def fine(t, _):
        fi, fj = i * sq + t // sk, j * sk + t % sk
        check(fi, fi, fj, fj, fi, fj, 1, 1, lambda: visit(fi, fj, 1, 1, True))
        return 0

    def all_fine():
        lax.fori_loop(0, sq * sk, fine, 0)

    check(i * sq, i * sq + sq - 1, j * sk, j * sk + sk - 1, i, j, sq, sk, all_fine)


def fwd_kernel(fq, fk, sk, qlo, qhi, klo, khi, q_ref, own_ref, oth_ref, seg_ref,
               pack_ref, o_ref, lse_ref, v_own, v_oth, m_ref, acc_ref, sq_ref):
    n = q_ref.shape[0]
    low = left_lanes((n, 128))
    v_own[...] = jnp.where(low, own_ref[...], jnp.ones((), bf16))
    v_oth[...] = jnp.where(low, oth_ref[...], jnp.ones((), bf16))
    pl.when(klo[0] != khi[n // fk - 1])(lambda: columns(seg_ref, sq_ref, 0))

    def q_step(i, _):
        qs = pl.ds(pl.multiple_of(i * fq, fq), fq)
        m_ref[...] = jnp.full_like(m_ref, FLOOR)
        acc_ref[...] = jnp.zeros_like(acc_ref)

        def visit(i, j, wide, deep, masked):
            ks = pl.ds(pl.multiple_of(j * deep * fk, deep * fk), deep * fk)
            q = q_ref[qs, :]
            sa = dot_nt(q, own_ref[ks, :])
            sb = dot_nt(q, oth_ref[ks, :])
            if masked:
                seg = sq_ref[qs, 0:1]
                sa = jnp.where(seg == seg_ref[0:1, ks], sa, NEG)
                sb = jnp.where(seg == seg_ref[1:2, ks], sb, NEG)
            old = m_ref[...]
            high = jnp.maximum(
                jnp.max(sa, axis=1, keepdims=True), jnp.max(sb, axis=1, keepdims=True)
            )
            new = jnp.maximum(old, high)
            pa = jnp.exp2(sa - new[:, :1]).astype(bf16)
            pb = jnp.exp2(sb - new[:, :1]).astype(bf16)
            m_ref[...] = new
            acc_ref[...] = (
                acc_ref[...] * jnp.exp2(old - new)
                + dot_nn(pa, v_own[ks, :])
                + dot_nn(pb, v_oth[ks, :])
            )

        def k_step(j, _):
            tiles(visit, qlo, qhi, klo, khi, i, j, 1, sk)
            return 0

        lax.fori_loop(0, n // (sk * fk), k_step, 0)
        acc = acc_ref[...]
        turned = swapped(acc)
        left = left_lanes((fq, 128))
        o = jnp.where(left, acc / turned, 0.0)
        o_ref[qs, :] = o.astype(bf16)
        lse = m_ref[...] + jnp.log2(jnp.where(left, turned, acc))
        half = left_lanes((64, 128))
        for b in range(fq // ROWS):
            block = slice(b * ROWS, (b + 1) * ROWS)
            lse_ref[0:1, pl.ds(pl.multiple_of(i * fq + b * ROWS, ROWS), ROWS)] = lse[block].T[0:1]
            upper, lower = o[block][:64], swapped(o[block][64:])
            pack_ref[i * (fq // ROWS) + b] = jnp.where(half, upper, lower).astype(bf16)
        return 0

    lax.fori_loop(0, n // fq, q_step, 0)


def attn_fwd(fq, fk, sk, ranges, q, own, oth, seg):
    n = q.shape[0]
    return pl.pallas_call(
        functools.partial(fwd_kernel, fq, fk, sk),
        out_shape=(shape((n // ROWS, 64, 128), bf16), shape((n, 128), bf16), shape((1, n), f32)),
        grid=(1,),
        in_specs=[SMEM] * 4 + [whole(*a.shape) for a in (q, own, oth, seg)],
        out_specs=(whole(n // ROWS, 64, 128), whole(n, 128), whole(1, n)),
        scratch_shapes=[
            pltpu.VMEM((n, 128), bf16),
            pltpu.VMEM((n, 128), bf16),
            pltpu.VMEM((fq, 128), f32),
            pltpu.VMEM((fq, 128), f32),
            pltpu.VMEM((n, 128), f32),
        ],
        compiler_params=limits(60),
        cost_estimate=cost(22),
        name="attn_fwd",
    )(*ranges, q, own, oth, seg)


def bwd_kernel(fine, sq, sk, qlo, qhi, klo, khi, q_ref, own_ref, oth_ref, pack_ref, o_ref, lrow,
               seg_ref, dq_out, dk_own, dk_oth, do_ref, drow, dk_sum, dq_ref, sk_own, sk_oth):
    n = q_ref.shape[0]
    low = left_lanes((ROWS, 128))

    @pl.when((klo[0, 0] != khi[0, n // fine - 1]) | (klo[0, 0] != khi[1, n // fine - 1]))
    def _():
        columns(seg_ref, sk_own, 0)
        columns(seg_ref, sk_oth, 1)

    for b in range(n // ROWS):
        s = pl.ds(b * ROWS, ROWS)
        packed = pack_ref[b].astype(f32)
        do = jnp.where(low, jnp.concatenate([packed, swapped(packed)], axis=0), 0.0)
        do_ref[s, :] = do.astype(bf16)
        delta = jnp.sum(do * o_ref[s, :].astype(f32), axis=1, keepdims=True)
        drow[0:1, s] = jnp.broadcast_to(delta, (ROWS, 128)).T[0:1, :]
    dq_ref[...] = jnp.zeros_like(dq_ref)
    sides = ((1, oth_ref, dk_oth, sk_oth), (0, own_ref, dk_own, sk_own))
    for half, k_ref, dk_ref, sk_ref in sides:
        dk_sum[...] = jnp.zeros_like(dk_sum)

        def visit(i, j, wide, deep, masked, k_ref=k_ref, sk_ref=sk_ref):
            qs = pl.ds(pl.multiple_of(i * wide * fine, wide * fine), wide * fine)
            ks = pl.ds(pl.multiple_of(j * deep * fine, deep * fine), deep * fine)
            keys = k_ref[ks, :]
            q = q_ref[qs, :]
            do = do_ref[qs, :]
            s = dot_nt(keys, q)
            dp = dot_nt(keys, do)
            p = jnp.exp2(s - lrow[0:1, qs])
            if masked:
                p = jnp.where(sk_ref[ks, 0:1] == seg_ref[0:1, qs], p, 0.0)
            ds = (p * (dp - drow[0:1, qs])).astype(bf16)
            dk_sum[ks, :] += dot_nn(p.astype(bf16), do) + dot_nn(ds, q)
            dq_ref[:, qs] += dot_nn(keys.T, ds)

        def k_step(j, _, half=half, visit=visit):
            def q_step(i, _):
                tiles(visit, qlo, qhi, klo.at[half], khi.at[half], i, j, sq, sk)
                return 0

            lax.fori_loop(0, n // (sq * fine), q_step, 0)
            return 0

        lax.fori_loop(0, n // (sk * fine), k_step, 0)
        low = left_lanes((n, 128))
        dk_ref[...] = (dk_sum[...] * jnp.where(low, 1.0, 1.0 / LOG2E)).astype(dk_ref.dtype)
    dq_out[...] = (dq_ref[...].T * HDIM**-0.5).astype(bf16)


def attn_bwd(fine, sq, sk, ranges, q, own, oth, pack, o, lse, seg):
    n = q.shape[0]
    return pl.pallas_call(
        functools.partial(bwd_kernel, fine, sq, sk),
        grid=(1,),
        out_shape=(shape((n, 128), bf16), shape((n, 128), f32), shape((n, 128), bf16)),
        in_specs=[SMEM] * 4
        + [whole(*a.shape) for a in (q, own, oth, pack, o, lse, seg)],
        out_specs=(whole(n, 128), whole(n, 128), whole(n, 128)),
        scratch_shapes=[
            pltpu.VMEM((n, 128), bf16),
            pltpu.VMEM((8, n), f32),
            pltpu.VMEM((n, 128), f32),
            pltpu.VMEM((128, n), f32),
            pltpu.VMEM((n, 128), f32),
            pltpu.VMEM((n, 128), f32),
        ],
        compiler_params=limits(60),
        cost_estimate=cost(120),
        name="attn_bwd",
    )(*ranges, q, own, oth, pack, o, lse, seg)


def heads_kernel(w_ref, gains_ref, seg_ref, sent_ref, wqkv_ref):
    left = left_lanes((32, 128))
    row = lax.broadcasted_iota(jnp.int32, (32, 128), 0)
    seg = jnp.broadcast_to(seg_ref[...], (32, 128))
    high, rest = (seg >> 6).astype(f32), (seg & 63).astype(f32)
    misc = jnp.broadcast_to(gains_ref[...], (32, 128))
    for k, part in enumerate((high, swapped(high), rest, swapped(rest))):
        misc = jnp.where(row == k + 1, part, misc)
    for p in range(HEADS // 2):
        q, k, v = (
            w_ref[:, 1024 * i + 128 * p : 1024 * i + 128 * (p + 1)].astype(f32) for i in range(3)
        )
        even = jnp.where(left, v, swapped(q)).astype(bf16)
        odd = jnp.where(left, swapped(v), q).astype(bf16)
        even_k = jnp.where(left, misc, swapped(k)).astype(bf16)
        odd_k = jnp.where(left, misc, k).astype(bf16)
        for c in range(2):
            sent_ref[4 * p + c, :, :128] = even
            sent_ref[4 * p + c, :, 128:] = even_k
            sent_ref[4 * p + 2 + c, :, :128] = odd
            sent_ref[4 * p + 2 + c, :, 128:] = odd_k
        wqkv_ref[:, 256 * p : 256 * p + 128] = even
        wqkv_ref[:, 256 * p + 128 : 256 * (p + 1)] = odd
        wqkv_ref[:, 2048 + 128 * p : 2048 + 128 * (p + 1)] = k.astype(bf16)


def heads_out(w, gains, seg):
    return pl.pallas_call(
        heads_kernel,
        out_shape=(shape((32, 32, 256), bf16), shape((32, 3072), bf16)),
        in_specs=[VMEM] * 3,
        out_specs=(VMEM, VMEM),
        compiler_params=limits(16),
        cost_estimate=cost(1),
        name="heads_out",
    )(w, gains, seg)


def unit_places():
    spread, pick = np.zeros((4, SPAN, 8 * SLOT)), np.zeros((4, 32, BLOCK))
    for z in range(4):
        for r in range(FIRST[z + 1] - FIRST[z]):
            pick[z, r, FIRST[z] + r] = 1
            for i in range(8):
                spread[z, BLOCK * i + FIRST[z] + r, SLOT * i + r] = 1
    return jnp.asarray(spread, bf16), jnp.asarray(pick, bf16)


def bundle_kernel(plane_ref, in_ref, spread_ref, pick_ref, mlp_ref, out_ref, bundle_ref, held):
    spread = spread_ref[plane_ref[0]]
    for k in range(8):
        part = dot_nn(in_ref[:, SPAN * k : SPAN * (k + 1)], spread)
        held[:, 8 * SLOT * k : 8 * SLOT * (k + 1)] = part
    for j in range(6):
        bundle_ref[32 * j : 32 * (j + 1), :] = held[:, 256 * j : 256 * (j + 1)].astype(bf16)
    mlp = dot_nn(pick_ref[plane_ref[0]], mlp_ref[...]).astype(bf16)
    for j in range(4):
        cols = slice(256 * j, 256 * (j + 1))
        bundle_ref[192 + 32 * j : 192 + 32 * (j + 1), :] = mlp[:, cols]
        bundle_ref[OUT_FIRST + 32 * j : OUT_FIRST + 32 * (j + 1), :] = out_ref[:, cols]


def bundle_out(plane, w_in, spread, pick, w_mlp, w_out):
    return pl.pallas_call(
        bundle_kernel,
        out_shape=shape((BUNDLE, 256), bf16),
        in_specs=[SMEM] + [VMEM] * 5,
        out_specs=VMEM,
        scratch_shapes=[pltpu.VMEM((32, 2 * WIDE), f32)],
        compiler_params=limits(16),
        cost_estimate=cost(1),
        name="bundle_out",
    )(plane, w_in, spread, pick, w_mlp, w_out)


def turns():
    inverse = THETA ** (-np.arange(0, HDIM, 2) / HDIM)
    sign = np.repeat([-1.0, 1.0, -1.0, 1.0], 32)
    both = []
    for scale in (64, 1):
        angle = np.tile(np.arange(64)[:, None] * scale * inverse[None], (1, 4))
        table = np.concatenate([np.cos(angle), np.sin(angle) * sign], axis=1).astype(np.float32)
        main = table.astype(jnp.bfloat16)
        both.append(np.concatenate([main, (table - main.astype(np.float32)).astype(jnp.bfloat16)]))
    return jnp.asarray(np.stack(both), bf16)


def tables_kernel(core_ref, seg_ref, turn_ref, cos_ref, sin_ref):
    code = lax.broadcasted_iota(jnp.int32, (ROWS, ROWS), 0) & 63
    lane = lax.broadcasted_iota(jnp.int32, (1, ROWS), 1)
    for b in range(seg_ref.shape[1] // ROWS):
        rows = slice(b * ROWS, (b + 1) * ROWS)
        place = (2 * b + core_ref[0]) * ROWS + lane - seg_ref[:, rows]
        high = dot_tn((code == (place >> 6)).astype(f32).astype(bf16), turn_ref[0])
        rest = dot_tn((code == (place & 63)).astype(f32).astype(bf16), turn_ref[1])
        cos_ref[rows, :] = high[:, :128] * rest[:, :128] - high[:, 128:] * rest[:, 128:]
        sin_ref[rows, :] = high[:, 128:] * rest[:, :128] + high[:, :128] * rest[:, 128:]


def tables(core, seg):
    n = seg.shape[1]
    return pl.pallas_call(
        tables_kernel,
        out_shape=(shape((n, 128), f32), shape((n, 128), f32)),
        in_specs=[SMEM, VMEM, VMEM],
        out_specs=(VMEM, VMEM),
        compiler_params=limits(16),
        cost_estimate=cost(0.1),
        name="tables",
    )(core, seg, turns())


def qkv_kernel(sizes, *refs):
    place = refs[0]
    pieces = refs[1 : 1 + len(sizes)]
    gain_ref, w_ref, cos_ref, sin_ref, n_ref, q_ref, k_ref = refs[1 + len(sizes) :]
    gain = gain_ref[...]
    w = w_ref[...]
    group = 0
    for piece, size in zip(pieces, sizes):
        z, _ = norm_parts(piece[...].astype(f32))
        normed = (z * gain).astype(bf16)
        both = dot_nn(normed, w)
        for g in range(size // 64):
            to = pl.ds(pl.multiple_of(place[group] * 64, 64), 64)
            group += 1
            mine = slice(g * 64, (g + 1) * 64)
            cos, sin = cos_ref[to, :], sin_ref[to, :]
            lane = lax.broadcasted_iota(jnp.int32, (64, 128), 1)

            def turn(t):
                other = jnp.where(lane < 96, pltpu.roll(t, 96, 1), pltpu.roll(t, 32, 1))
                return t * cos + other * sin

            first, second = both[mine, :128], both[mine, 128:]
            q_ref[to, :] = jnp.where(lane < HDIM, 0.0, turn(first) * (LOG2E * HDIM**-0.5)).astype(bf16)
            n_ref[to, :] = normed[mine]
            k_ref[to, :] = jnp.where(lane < HDIM, first, turn(second)).astype(bf16)


def qkv(place, pieces, gain, w, cos, sin):
    n, width = cos.shape[0], pieces[0].shape[1]
    sizes = tuple(p.shape[0] for p in pieces)
    return pl.pallas_call(
        functools.partial(qkv_kernel, sizes),
        out_shape=(shape((n, width), bf16), shape((n, 128), bf16), shape((n, 128), bf16)),
        in_specs=[SMEM] + [VMEM] * (len(pieces) + 4),
        out_specs=(VMEM, VMEM, VMEM),
        compiler_params=limits(56),
        cost_estimate=cost(6),
        name="qkv",
    )(place, *pieces, gain, w, cos, sin)


OUT_PARTS = [weight_part(32, OUT_FIRST + 32 * j) for j in range(4)]


def proj_kernel(pack_ref, x_ref, gain_ref, w0, w1, w2, w3, n_ref, h_ref, o_ref):
    for p in range(HEADS // 2):
        both = unpack_pair(pack_ref[2 * p].astype(f32), pack_ref[2 * p + 1].astype(f32))
        o_ref[:, p * 128 : (p + 1) * 128] = both.astype(bf16)
    o = o_ref[...]
    for j, w in enumerate((w0, w1, w2, w3)):
        cols = slice(256 * j, 256 * (j + 1))
        h_ref[:, cols] = x_ref[:, cols].astype(f32) + dot_nn(o, w[...].reshape(1024, 256))
    z, _ = norm_parts(h_ref[...])
    n_ref[...] = (z * gain_ref[...]).astype(bf16)


def proj(pack, x, gain, bundle):
    n, width = x.shape
    return pl.pallas_call(
        proj_kernel,
        grid=(1,),
        out_shape=(shape((n, width), bf16), shape((n, width), f32), shape((n, width), bf16)),
        in_specs=[whole(*pack.shape), whole(n, width), whole(1, width), *OUT_PARTS],
        out_specs=(whole(n, width), whole(n, width), whole(n, width)),
        compiler_params=limits(60),
        cost_estimate=cost(3),
        name="proj",
    )(pack, x, gain, bundle, bundle, bundle, bundle)


def normal_cdf(x, bell):
    t = 1.0 / (1.0 + (0.3275911 * 0.5**0.5) * jnp.abs(x))
    tail = 1.061405429
    for term in (-1.453152027, 1.421413741, -0.284496736, 0.254829592):
        tail = tail * t + term
    tail = 0.5 * tail * t * bell
    return jnp.where(x >= 0.0, 1.0 - tail, tail)


def units_kernel(*refs):
    n_refs, g_refs = refs[:4], refs[4:8]
    win_ref, m_refs = refs[8], refs[9:13]
    act_ref, dup_ref, n_all, g_all, w_ref = refs[13:18]
    d_refs, w_in = refs[18:22], refs[22]
    for i in range(4):
        n_all[i * ROWS : (i + 1) * ROWS, :] = n_refs[i][...]
        g_all[i * ROWS : (i + 1) * ROWS, :] = g_refs[i][...]
    normed = n_all[...]
    g = g_all[...]

    for a in range(4):
        part = m_refs[a][...].astype(f32)[:, :SLOT].reshape(WIDE, 256)
        w_ref[:, 256 * a : 256 * (a + 1)] = part.astype(bf16)
    for j in range(6):
        w_in[:, 256 * j : 256 * (j + 1)] = win_ref[:, 32 * j : 32 * (j + 1), :].reshape(1024, 256)

    for j in range(3):
        cols = slice(256 * j, 256 * (j + 1))
        more = slice(WIDE + 256 * j, WIDE + 256 * (j + 1))
        first = dot_nn(normed, w_in[:, cols])
        second = dot_nn(normed, w_in[:, more])
        d_act = dot_nt(g, w_ref[cols, :])
        bell = jnp.exp(-0.5 * first * first)
        cdf = normal_cdf(first, bell)
        slope = cdf + first * (bell * (1.0 / (2.0 * np.pi) ** 0.5))
        gated = first * cdf
        act_ref[:, cols] = (gated * second).astype(bf16)
        dup_ref[:, cols] = (d_act * second * slope).astype(bf16)
        dup_ref[:, more] = (d_act * gated).astype(bf16)
    total = dot_nt(dup_ref[...], w_in[...])
    for i in range(4):
        d_refs[i][...] = total[i * ROWS : (i + 1) * ROWS].astype(bf16)


def units(normed, cots, bundle):
    n, width = normed[0].shape
    tokens = 4 * n
    return pl.pallas_call(
        units_kernel,
        grid=(1,),
        out_shape=(
            shape((tokens, WIDE), bf16),
            shape((tokens, 2 * WIDE), bf16),
            shape((tokens, width), bf16),
            shape((tokens, width), bf16),
            shape((WIDE, width), bf16),
            *[shape((n, width), bf16)] * 4,
        ),
        in_specs=[whole(n, width)] * 8
        + [weight_part(192, 0)]
        + [weight_part(32, 192 + 32 * a) for a in range(4)],
        out_specs=(
            whole(tokens, WIDE),
            whole(tokens, 2 * WIDE),
            whole(tokens, width),
            whole(tokens, width),
            whole(WIDE, width),
            *[whole(n, width)] * 4,
        ),
        scratch_shapes=[pltpu.VMEM((width, 2 * WIDE), bf16)],
        compiler_params=limits(60),
        cost_estimate=cost(11),
        name="units",
    )(*normed, *cots, *[bundle] * 5)


def unit_grads_kernel(act_ref, dup_ref, n_all, g_all, out_hbm, out_ref, sem):
    act = act_ref[...].T
    for a in range(4):
        cols = slice(256 * a, 256 * (a + 1))
        grad = dot_nn(act, g_all[:, cols])
        for b in range(32):
            slot = jnp.concatenate([grad[SLOT * b : SLOT * (b + 1)], jnp.zeros((8, 256), f32)])
            out_ref[(b % 8) * 4 + b // 8, 192 + 32 * a : 192 + 32 * (a + 1), :] = slot.astype(bf16)
    normed = n_all[...].T
    for j in range(6):
        grad = dot_nn(normed, dup_ref[:, 256 * j : 256 * (j + 1)]).astype(bf16)
        for b in range(32):
            out_ref[(b % 8) * 4 + b // 8, 32 * j : 32 * (j + 1), :] = grad[32 * b : 32 * (b + 1)]
    copy = pltpu.make_async_copy(out_ref, out_hbm.at[:, pl.ds(0, OUT_FIRST)], sem)
    copy.start()
    copy.wait()


def unit_grads(act, dup, n_all, g_all):
    tokens, width = n_all.shape
    return pl.pallas_call(
        unit_grads_kernel,
        out_shape=shape((32, BUNDLE, 256), bf16),
        grid=(1,),
        in_specs=[whole(*a.shape) for a in (act, dup, n_all, g_all)],
        out_specs=HBM,
        scratch_shapes=[pltpu.VMEM((32, OUT_FIRST, 256), bf16), pltpu.SemaphoreType.DMA],
        compiler_params=limits(60),
        cost_estimate=cost(2),
        name="unit_grads",
    )(act, dup, n_all, g_all)


def out_grad_kernel(o_ref, da_ref, in_hbm, out_hbm, out_ref, sem):
    del in_hbm
    grad = dot_tn(o_ref[...], da_ref[...]).astype(bf16)
    for b in range(32):
        for j in range(4):
            out_ref[(b % 8) * 4 + b // 8, 32 * j : 32 * (j + 1), :] = grad[
                32 * b : 32 * (b + 1), 256 * j : 256 * (j + 1)
            ]
    copy = pltpu.make_async_copy(out_ref, out_hbm.at[:, pl.ds(OUT_FIRST, 128)], sem)
    copy.start()
    copy.wait()


def out_grad(o, da, grads):
    return pl.pallas_call(
        out_grad_kernel,
        out_shape=shape(grads.shape, bf16),
        grid=(1,),
        in_specs=[whole(*o.shape), whole(*da.shape), HBM],
        out_specs=HBM,
        scratch_shapes=[pltpu.VMEM((32, 128, 256), bf16), pltpu.SemaphoreType.DMA],
        input_output_aliases={2: 0},
        compiler_params=limits(60),
        cost_estimate=cost(1),
        name="out_grad",
    )(o, da, grads)


def unit_out_kernel(act_ref, w_ref, p0, p1, p2, p3):
    act = act_ref[...]
    for a in range(4):
        cols = slice(256 * a, 256 * (a + 1))
        part = dot_nn(act, w_ref[:, cols]).astype(bf16)
        for i, p in enumerate((p0, p1, p2, p3)):
            p[:, cols] = part[i * ROWS : (i + 1) * ROWS]


def unit_out(act, w):
    return pl.pallas_call(
        unit_out_kernel,
        grid=(1,),
        out_shape=[shape((ROWS, 1024), bf16)] * 4,
        in_specs=[whole(*act.shape), whole(*w.shape)],
        out_specs=[whole(ROWS, 1024)] * 4,
        compiler_params=limits(60),
        cost_estimate=cost(0.5),
        name="unit_out",
    )(act, w)


def proj_back_kernel(d0, d1, d2, d3, h_ref, gain_ref, cot_ref, w0, w1, w2, w3,
                     pack_ref, dh_ref, da_ref):
    total = d0[...].astype(f32) + d1[...].astype(f32) + d2[...].astype(f32) + d3[...].astype(f32)
    z, scale = norm_parts(h_ref[...])
    dh = cot_ref[...].astype(f32) + norm_back(total * gain_ref[...], z, scale)
    dh_ref[...] = dh
    da_ref[...] = dh.astype(bf16)
    do = sum(
        dot_nt(da_ref[:, 256 * j : 256 * (j + 1)], w[...].reshape(1024, 256))
        for j, w in enumerate((w0, w1, w2, w3))
    )
    for p in range(HEADS // 2):
        even, odd = pack_pair(do[:, p * 128 : (p + 1) * 128])
        pack_ref[2 * p] = even.astype(bf16)
        pack_ref[2 * p + 1] = odd.astype(bf16)


def proj_back(ds, h, gain, cot, bundle):
    n, width = h.shape
    return pl.pallas_call(
        proj_back_kernel,
        grid=(1,),
        out_shape=(shape((HEADS, 64, 128), bf16), shape((n, width), f32), shape((n, width), bf16)),
        in_specs=[whole(n, width)] * 5 + [whole(1, width), whole(n, width), *OUT_PARTS],
        out_specs=(whole(HEADS, 64, 128), whole(n, width), whole(n, width)),
        compiler_params=limits(60),
        cost_estimate=cost(3),
        name="proj_back",
    )(*ds, h, gain, cot, bundle, bundle, bundle, bundle)


def turn_back_kernel(core_ref, dq_ref, own_ref, oth_ref, cos_ref, sin_ref, n_ref,
                     sent_ref, keep_ref, give_ref, d_ref, grad_ref, held, sem):
    fetch = pltpu.make_async_copy(n_ref, held, sem)
    fetch.start()
    for b in range(dq_ref.shape[0] // ROWS):
        s = slice(b * ROWS, (b + 1) * ROWS)
        cos, sin = cos_ref[s, :], sin_ref[s, :]
        lane = lax.broadcasted_iota(jnp.int32, (ROWS, 128), 1)

        def turn(t):
            other = jnp.where(lane < 96, pltpu.roll(t, 96, 1), pltpu.roll(t, 32, 1))
            return t * cos - other * sin

        dk = own_ref[s, :] + oth_ref[s, :].astype(f32)
        first = jnp.where(lane < HDIM, dk, turn(dq_ref[s, :].astype(f32)))
        second = jnp.where(lane < HDIM, 0.0, turn(dk))
        d_ref[s, :128] = first.astype(bf16)
        d_ref[s, 128:] = second.astype(bf16)
        sent_ref[b, :ROWS, :] = first.astype(bf16)
        packed = jnp.where(left_lanes((64, 128)), swapped(second[:64]), second[64:])
        sent_ref[b, ROWS:, :] = packed.astype(bf16)
    fetch.wait()
    grad = dot_tn(d_ref[...], held[...]).T
    grad_ref[...] = grad.reshape(grad_ref.shape)
    core = core_ref[0]
    for h in range(HEADS):
        keep_ref[h] = grad_ref[2 * h + core]
        give_ref[h] = grad_ref[2 * h + 1 - core].astype(bf16)


def turn_back(core, dq, own, oth, cos, sin, normed):
    n = dq.shape[0]
    return pl.pallas_call(
        turn_back_kernel,
        out_shape=(
            shape((HEADS, 192, 128), bf16),
            shape((HEADS, 32, 256), f32),
            shape((HEADS, 32, 256), bf16),
        ),
        grid=(1,),
        in_specs=[SMEM] + [whole(*a.shape) for a in (dq, own, oth, cos, sin)] + [HBM],
        out_specs=(whole(HEADS, 192, 128), whole(HEADS, 32, 256), whole(HEADS, 32, 256)),
        scratch_shapes=[
            pltpu.VMEM((n, 256), bf16),
            pltpu.VMEM((32, 32, 256), f32),
            pltpu.VMEM(normed.shape, bf16),
            pltpu.SemaphoreType.DMA,
        ],
        compiler_params=limits(60),
        cost_estimate=cost(5),
        name="turn_back",
    )(core, dq, own, oth, cos, sin, normed)


def pack_kernel(sent_ref, keep_ref, took_ref, out_ref):
    out_ref[:, :192, :] = sent_ref[...]
    left = left_lanes((16, 128))
    for h in range(HEADS):
        both = keep_ref[h] + took_ref[h].astype(f32)
        k = both[:, 128:]
        out_ref[h, 192:224, :] = both[:, :128].astype(bf16)
        out_ref[h, 224:, :] = jnp.where(left, swapped(k[:16]), k[16:]).astype(bf16)


def pack_head(sent, keep, took):
    return pl.pallas_call(
        pack_kernel,
        out_shape=shape((HEADS, 240, 128), bf16),
        grid=(1,),
        in_specs=[whole(*a.shape) for a in (sent, keep, took)],
        out_specs=whole(HEADS, 240, 128),
        compiler_params=limits(60),
        cost_estimate=cost(1),
        name="pack_head",
    )(sent, keep, took)


def input_kernel(got_ref, w_ref, x_ref, gain_ref, dh_ref, out_ref, d_ref, acc_ref):
    step = pl.program_id(0)

    @pl.when(step == 0)
    def _():
        for h in range(HEADS):
            d_ref[h // 4, :, 128 * (h % 4) : 128 * (h % 4 + 1)] = got_ref[h, :ROWS, :]
        for p in range(HEADS // 2):
            both = unpack_pair(
                got_ref[2 * p, ROWS:192, :].astype(f32), got_ref[2 * p + 1, ROWS:192, :].astype(f32)
            )
            d_ref[4 + p // 4, :, 128 * (p % 4) : 128 * (p % 4 + 1)] = both.astype(bf16)
        acc_ref[...] = jnp.zeros_like(acc_ref)

    acc_ref[...] += dot_nt(d_ref[step], w_ref[...])

    @pl.when(step == pl.num_programs(0) - 1)
    def _():
        z, scale = norm_parts(x_ref[...].astype(f32))
        back = norm_back(acc_ref[...] * gain_ref[...], z, scale)
        out_ref[...] = (dh_ref[...] + back).astype(bf16)


def input_back(got, w, x, gain, dh):
    n, width = x.shape
    return pl.pallas_call(
        input_kernel,
        grid=(6,),
        out_shape=shape((n, width), bf16),
        in_specs=[
            whole(*got.shape),
            pl.BlockSpec((width, 512), lambda i: (0, i)),
            whole(n, width),
            whole(1, width),
            whole(n, width),
        ],
        out_specs=whole(n, width),
        scratch_shapes=[pltpu.VMEM((6, n, 512), bf16), pltpu.VMEM((n, width), f32)],
        compiler_params=limits(32),
        cost_estimate=cost(4),
        name="input_back",
    )(got, w, x, gain, dh)


def rows_kernel(got_ref, sum_ref, out_ref):
    left = left_lanes((32, 128))
    half = left_lanes((16, 128))
    for p in range(HEADS // 2):
        even, odd = (got_ref[2 * p + i, 192:224, :].astype(f32) for i in range(2))
        even_k, odd_k = (got_ref[2 * p + i, 224:240, :].astype(f32) for i in range(2))
        q = jnp.where(left, swapped(even), odd)
        v = jnp.where(left, even, swapped(odd))
        k = jnp.concatenate(
            [jnp.where(half, even_k, swapped(odd_k)), jnp.where(half, swapped(even_k), odd_k)]
        )
        for i, part in enumerate((q, k, v)):
            j = 8 * i + p
            out_ref[32 * (j // 2) : 32 * (j // 2 + 1), 128 * (j % 2) : 128 * (j % 2 + 1)] = part.astype(bf16)
    out_ref[384:, :] = sum_ref[...]


def gather_rows(got, sums):
    return pl.pallas_call(
        rows_kernel,
        out_shape=shape((384 + BUNDLE, 256), bf16),
        in_specs=[VMEM] * 2,
        out_specs=VMEM,
        compiler_params=limits(16),
        cost_estimate=cost(1),
        name="gather_rows",
    )(got, sums)


def planes_kernel(plane_ref, r0, r1, r2, r3, spread_ref, pick_ref, wqkv_ref, win_ref, g1_ref, g2_ref,
                  qkv_ref, out_ref, in_ref, mlp_ref, norm1_ref, norm2_ref, held):
    pieces = (r0, r1, r2, r3)
    planes = [lax.rem(plane_ref[0] + 4 - k, 4) for k in SHIFTS]

    def total(first):
        return sum(r[first : first + 32, :].astype(f32) for r in pieces)

    norm = jnp.zeros((32, 1), f32)
    for j in range(12):
        cols = slice(256 * j, 256 * (j + 1))
        part = total(32 * j)
        qkv_ref[:, cols] = part
        norm += jnp.sum(part * wqkv_ref[:, cols].astype(f32), axis=1, keepdims=True)
    norm1_ref[...] = norm / g1_ref[...]
    for j in range(4):
        cols = slice(256 * j, 256 * (j + 1))
        out_ref[:, cols] = total(384 + OUT_FIRST + 32 * j)
        first = 384 + 192 + 32 * j
        mlp_ref[:, cols] = sum(
            dot_tn(pick_ref[z], r[first : first + 32, :]) for z, r in zip(planes, pieces)
        )
    grads = jnp.zeros((256, SPAN), f32)
    for z, r in zip(planes, pieces):
        wide = jnp.concatenate([r[384 + 32 * j : 384 + 32 * (j + 1), :] for j in range(6)], axis=1)
        for k in range(8):
            held[32 * k : 32 * (k + 1), :] = wide[:, 8 * SLOT * k : 8 * SLOT * (k + 1)]
        grads += dot_nt(held[...], spread_ref[z])
    norm = jnp.zeros((32, 1), f32)
    for k in range(8):
        cols = slice(SPAN * k, SPAN * (k + 1))
        part = grads[32 * k : 32 * (k + 1)]
        in_ref[:, cols] = part
        norm += jnp.sum(part * win_ref[:, cols].astype(f32), axis=1, keepdims=True)
    norm2_ref[...] = norm / g2_ref[...]


def add_planes(plane, parts, spread, pick, wqkv, win, gain_one, gain_two):
    return pl.pallas_call(
        planes_kernel,
        out_shape=(
            shape(wqkv.shape, f32),
            shape((32, 1024), f32),
            shape(win.shape, f32),
            shape((BLOCK, 1024), f32),
            shape((32, 1), f32),
            shape((32, 1), f32),
        ),
        in_specs=[SMEM] + [VMEM] * 10,
        out_specs=(VMEM,) * 6,
        scratch_shapes=[pltpu.VMEM((256, 8 * SLOT), bf16)],
        compiler_params=limits(24),
        cost_estimate=cost(5),
        name="add_planes",
    )(plane, *parts, spread, pick, wqkv, win, gain_one, gain_two)


def shift(value, axis, steps):
    count = lax.axis_size(axis)
    return lax.ppermute(value, axis, [(i, (i + steps) % count) for i in range(count)])


def from_planes(value):
    return [value] + [shift(value, "z", k) for k in SHIFTS[1:]]


def back_to_planes(pieces):
    return [pieces[0]] + [shift(p, "z", -k) for p, k in zip(pieces[1:], SHIFTS[1:])]


def far(value, near, axis):
    half = value.shape[0] // 2
    behind, ahead = near
    return [value, behind, ahead, shift(behind[:half], axis, 1), shift(ahead[half:], axis, 3)]


def exchange(value, axes):
    return lax.all_to_all(value, axes, split_axis=0, concat_axis=0, tiled=True)


def shards(hidden_in, seg_start, norm1_gain, qkv_weight, out_weight, norm2_gain, in_weight,
           mlp_weight, out_cotangent):
    plane, core = lax.axis_index("z"), lax.axis_index("c")
    mine = (lax.axis_index("x"), lax.axis_index("y"))
    plane_id, core_id = plane.astype(jnp.int32)[None], core.astype(jnp.int32)[None]
    x_own = hidden_in[0]
    cot = out_cotangent[0]
    width = x_own.shape[1]
    rows = qkv_weight.shape[0]

    upper, lower = x_own[:64], x_own[64:]
    upper = [upper] + [shift(upper, "x", k) for k in SHIFTS[1:]]
    lower = [lower] + [shift(lower, "y", k) for k in SHIFTS[1:]]
    upper, lower = jnp.concatenate(upper), jnp.concatenate(lower)

    gains = jnp.pad(jnp.concatenate([norm1_gain, norm2_gain]), (0, HDIM)).astype(f32)[None]
    sent, wqkv = heads_out(qkv_weight, gains, seg_start)
    spread, pick = unit_places()
    bundle = bundle_out(plane_id, in_weight, spread, pick, mlp_weight, out_weight)
    upper, lower, sent, bundle = lax.optimization_barrier((upper, lower, sent, bundle))
    got = exchange(sent, XYC)
    pieces = [upper, shift(upper, "y", 1), shift(upper, "y", 3)]
    pieces += [shift(pieces[1], "y", 1)]
    pieces += [lower, shift(lower, "x", 1), shift(lower, "x", 3)]
    pieces += [shift(pieces[6], "x", 3)]
    place = []
    for half in (0, 1):
        for outer in SHIFTS:
            for inner in SHIFTS:
                sx, sy = (inner, outer) if half == 0 else (outer, inner)
                place.append((((mine[0] - sx) % 4) * 4 + (mine[1] - sy) % 4) * 2 + half)
    place = jnp.stack(place).astype(jnp.int32)
    w_head = got.reshape(width, 256)
    gain_one = got[:, 0, 128:160].reshape(1, width).astype(f32)
    gain_two = got[:, 0, 160:192].reshape(1, width).astype(f32)
    high, rest = got[:, 1:3, 128:192].astype(jnp.int32), got[:, 3:5, 128:192].astype(jnp.int32)
    seg_all = (high * 64 + rest).reshape(HEADS, 2, ROWS)
    seg_own = jnp.where(core == 0, seg_all[:, 0], seg_all[:, 1]).reshape(-1)
    seg_oth = jnp.where(core == 0, seg_all[:, 1], seg_all[:, 0]).reshape(-1)
    cosine, sine = tables(core_id, seg_own[None])
    pieces, cosine, sine, bundle = lax.optimization_barrier((pieces, cosine, sine, bundle))
    bundle = lax.all_gather(bundle, XYC, axis=0, tiled=False)

    cots = from_planes(cot)

    normed_one, queries, keys = qkv(place, pieces, gain_one, w_head, cosine, sine)
    keys_oth = shift(keys, "c", 1)

    def bounds(seg, size):
        tiles = seg.reshape(-1, size)
        return tiles[:, 0], tiles[:, -1]

    (qlo, qhi), (olo, ohi), (tlo, thi) = bounds(seg_own, 256), bounds(seg_own, 1024), bounds(seg_oth, 1024)
    both_segs = jnp.stack([seg_own, seg_oth]).astype(f32)
    o_pack, o, lse = attn_fwd(
        256, 1024, 2, (qlo, qhi, jnp.minimum(olo, tlo), jnp.maximum(ohi, thi)),
        queries, keys, keys_oth, both_segs,
    )
    o_pack, cots = lax.optimization_barrier((o_pack, cots))
    o_got = exchange(o_pack, XY)
    wqkv, o_got = lax.optimization_barrier((wqkv, o_got))
    wqkv = lax.all_gather(wqkv, XYC, axis=0, tiled=True)

    normed_two, middle, o_tok = proj(o_got, x_own, gain_two, bundle)
    act, dup, n_all, g_all, w_units, *d_parts = units(from_planes(normed_two), cots, bundle)
    d_parts = back_to_planes(d_parts)
    g_sum = unit_grads(act, dup, n_all, g_all)
    d_parts, g_sum = lax.optimization_barrier((d_parts, g_sum))
    do_pack, d_mid, d_attn = proj_back(d_parts, middle, gain_two, cot, bundle)
    do_got = exchange(do_pack, XY)
    g_sum = out_grad(o_tok, d_attn, g_sum)
    g_sum, wqkv = lax.optimization_barrier((g_sum, wqkv))
    g_sum = lax.psum_scatter(g_sum.reshape(8, 4 * BUNDLE, 256), YC, scatter_dimension=0, tiled=False)

    (qlo, qhi), (tlo, thi) = bounds(seg_own, 512), bounds(seg_oth, 512)
    ranges = (qlo, qhi, jnp.stack([qlo, tlo]), jnp.stack([qhi, thi]))
    dq, dk_own, dk_oth = attn_bwd(512, 4, 2, ranges, queries, keys, keys_oth, do_got, o, lse, both_segs)
    d_sent, keep, give = turn_back(core_id, dq, dk_own, shift(dk_oth, "c", 1), cosine, sine, normed_one)

    d_sent = pack_head(d_sent, keep, shift(give, "c", 1))
    g_sum, d_sent, act = lax.optimization_barrier((g_sum, d_sent, act))
    g_sum = lax.psum_scatter(g_sum.reshape(4, BUNDLE, 256), "x", scatter_dimension=0, tiled=False)
    d_got = exchange(d_sent, XY)
    out_parts = back_to_planes(unit_out(act, w_units))
    d_got, out_parts = lax.optimization_barrier((d_got, out_parts))

    g_rows = from_planes(gather_rows(d_got, g_sum))
    input_grad = input_back(d_got, wqkv, x_own, gain_one, d_mid)
    hidden_out = (middle + sum(p.astype(f32) for p in out_parts)).astype(bf16)
    g_rows, input_grad, hidden_out = lax.optimization_barrier((g_rows, input_grad, hidden_out))
    g_qkv, g_out, g_in, g_mlp, grad_one, grad_two = add_planes(
        plane_id, g_rows, spread, pick, qkv_weight, in_weight,
        norm1_gain.astype(f32)[:, None], norm2_gain.astype(f32)[:, None],
    )
    return (
        hidden_out[None],
        input_grad[None],
        g_qkv,
        g_out,
        g_in,
        g_mlp,
        grad_one[:, 0],
        grad_two[:, 0],
    )


def solution(mesh):
    fine = Mesh(mesh.devices.reshape(4, 4, 4, 2), ("z", "x", "y", "c"))
    blk = ("x", "y", "c")
    return jax.shard_map(
        shards,
        mesh=fine,
        in_specs=(
            P("z", blk, None),
            P("z", blk),
            P(blk),
            P(blk, None),
            P(blk, None),
            P(blk),
            P(blk, None),
            P(blk, None),
            P("z", blk, None),
        ),
        out_specs=(
            P("z", blk, None),
            P("z", blk, None),
            P(blk, None),
            P(blk, None),
            P(blk, None),
            P(blk, None),
            P(blk),
            P(blk),
        ),
        check_vma=False,
    )
```

```python
import functools

import jax
import jax.numpy as jnp
import numpy as np
from jax import lax
from jax.experimental import pallas as pl
from jax.experimental.pallas import tpu as pltpu
from jax.sharding import Mesh
from jax.sharding import PartitionSpec as P

HEADS = 16
HDIM = 64
EPS = 1e-05
THETA = 160000.0
NEG = -1e30
FLOOR = -1e29
ROWS = 128
BLOCK = 82
FIRST = (0, 21, 42, 62, 82)
SLOT = 24
WIDE = 32 * SLOT
SPAN = 8 * BLOCK
OUT_FIRST = 288
BUNDLE = 416
LOG2E = 1.4426950408889634
bf16 = jnp.bfloat16
f32 = jnp.float32
XY = ("x", "y")
YC = ("y", "c")
XYC = ("x", "y", "c")
SMEM = pl.BlockSpec(memory_space=pltpu.SMEM)
VMEM = pl.BlockSpec(memory_space=pltpu.VMEM)
HBM = pl.BlockSpec(memory_space=pltpu.HBM)
SHIFTS = (0, 1, 3, 2)


def dot_nn(a, b):
    return lax.dot_general(a, b, (((1,), (0,)), ((), ())), preferred_element_type=f32)


def dot_nt(a, b):
    return lax.dot_general(a, b, (((1,), (1,)), ((), ())), preferred_element_type=f32)


def dot_tn(a, b):
    return lax.dot_general(a, b, (((0,), (0,)), ((), ())), preferred_element_type=f32)


def shape(dims, dtype):
    return jax.ShapeDtypeStruct(dims, dtype)


def limits(mib):
    return pltpu.CompilerParams(vmem_limit_bytes=mib << 20)


def cost(us):
    return pl.CostEstimate(flops=int(us * 1.1e9), bytes_accessed=int(us * 3.4e6), transcendentals=0)


def weight_part(rows, first, blocks=32):
    return pl.BlockSpec((blocks, rows, 256), lambda i: (0, first // rows, 0))


def whole(*dims):
    return pl.BlockSpec(dims, lambda i: (0,) * len(dims))


def left_lanes(dims):
    return lax.broadcasted_iota(jnp.int32, dims, len(dims) - 1) < HDIM


def swapped(v):
    return pltpu.roll(v, HDIM, 1)


def norm_parts(values):
    mid = values - jnp.mean(values, axis=-1, keepdims=True)
    scale = lax.rsqrt(jnp.mean(mid * mid, axis=-1, keepdims=True) + EPS)
    return mid * scale, scale


def norm_back(e, z, scale):
    return (
        e - jnp.mean(e, axis=-1, keepdims=True) - z * jnp.mean(e * z, axis=-1, keepdims=True)
    ) * scale


def unpack_pair(even, odd):
    left = left_lanes(even.shape)
    top = jnp.where(left, even, swapped(odd))
    bottom = jnp.where(left, swapped(even), odd)
    return jnp.concatenate([top, bottom], axis=0)


def pack_pair(rows):
    top, bottom = rows[:64], rows[64:]
    left = left_lanes(top.shape)
    return jnp.where(left, top, swapped(bottom)), jnp.where(left, swapped(top), bottom)


def columns(rows_ref, cols_ref, k):
    for b in range(rows_ref.shape[1] // ROWS):
        s = pl.ds(b * ROWS, ROWS)
        cols_ref[s, :] = jnp.broadcast_to(rows_ref[k : k + 1, s], (ROWS, ROWS)).T


def tiles(visit, qlo, qhi, klo, khi, i, j, sq, sk):
    def check(q0, q1, k0, k1, rows, cols, wide, deep, parts):
        a, b, c, d = qlo[q0], qhi[q1], klo[k0], khi[k1]
        plain = (a == b) & (c == d) & (a == c)
        mixed = (a <= d) & (c <= b) & jnp.logical_not(plain)
        pl.when(plain)(lambda: visit(rows, cols, wide, deep, False))
        pl.when(mixed)(parts)

    def fine(t, _):
        fi, fj = i * sq + t // sk, j * sk + t % sk
        check(fi, fi, fj, fj, fi, fj, 1, 1, lambda: visit(fi, fj, 1, 1, True))
        return 0

    def all_fine():
        lax.fori_loop(0, sq * sk, fine, 0)

    check(i * sq, i * sq + sq - 1, j * sk, j * sk + sk - 1, i, j, sq, sk, all_fine)


def fwd_kernel(fq, fk, sk, qlo, qhi, klo, khi, q_ref, own_ref, oth_ref, seg_ref,
               pack_ref, o_ref, lse_ref, v_own, v_oth, m_ref, acc_ref, sq_ref):
    n = q_ref.shape[0]
    low = left_lanes((n, 128))
    v_own[...] = jnp.where(low, own_ref[...], jnp.ones((), bf16))
    v_oth[...] = jnp.where(low, oth_ref[...], jnp.ones((), bf16))
    pl.when(klo[0] != khi[n // fk - 1])(lambda: columns(seg_ref, sq_ref, 0))

    def q_step(i, _):
        qs = pl.ds(pl.multiple_of(i * fq, fq), fq)
        m_ref[...] = jnp.full_like(m_ref, FLOOR)
        acc_ref[...] = jnp.zeros_like(acc_ref)

        def visit(i, j, wide, deep, masked):
            ks = pl.ds(pl.multiple_of(j * deep * fk, deep * fk), deep * fk)
            q = q_ref[qs, :]
            sa = dot_nt(q, own_ref[ks, :])
            sb = dot_nt(q, oth_ref[ks, :])
            if masked:
                seg = sq_ref[qs, 0:1]
                sa = jnp.where(seg == seg_ref[0:1, ks], sa, NEG)
                sb = jnp.where(seg == seg_ref[1:2, ks], sb, NEG)
            old = m_ref[...]
            high = jnp.maximum(
                jnp.max(sa, axis=1, keepdims=True), jnp.max(sb, axis=1, keepdims=True)
            )
            new = jnp.maximum(old, high)
            pa = jnp.exp2(sa - new[:, :1]).astype(bf16)
            pb = jnp.exp2(sb - new[:, :1]).astype(bf16)
            m_ref[...] = new
            acc_ref[...] = (
                acc_ref[...] * jnp.exp2(old - new)
                + dot_nn(pa, v_own[ks, :])
                + dot_nn(pb, v_oth[ks, :])
            )

        def k_step(j, _):
            tiles(visit, qlo, qhi, klo, khi, i, j, 1, sk)
            return 0

        lax.fori_loop(0, n // (sk * fk), k_step, 0)
        acc = acc_ref[...]
        turned = swapped(acc)
        left = left_lanes((fq, 128))
        o = jnp.where(left, acc / turned, 0.0)
        o_ref[qs, :] = o.astype(bf16)
        lse = m_ref[...] + jnp.log2(jnp.where(left, turned, acc))
        half = left_lanes((64, 128))
        for b in range(fq // ROWS):
            block = slice(b * ROWS, (b + 1) * ROWS)
            lse_ref[0:1, pl.ds(pl.multiple_of(i * fq + b * ROWS, ROWS), ROWS)] = lse[block].T[0:1]
            upper, lower = o[block][:64], swapped(o[block][64:])
            pack_ref[i * (fq // ROWS) + b] = jnp.where(half, upper, lower).astype(bf16)
        return 0

    lax.fori_loop(0, n // fq, q_step, 0)


def attn_fwd(fq, fk, sk, ranges, q, own, oth, seg):
    n = q.shape[0]
    return pl.pallas_call(
        functools.partial(fwd_kernel, fq, fk, sk),
        out_shape=(shape((n // ROWS, 64, 128), bf16), shape((n, 128), bf16), shape((1, n), f32)),
        grid=(1,),
        in_specs=[SMEM] * 4 + [whole(*a.shape) for a in (q, own, oth, seg)],
        out_specs=(whole(n // ROWS, 64, 128), whole(n, 128), whole(1, n)),
        scratch_shapes=[
            pltpu.VMEM((n, 128), bf16),
            pltpu.VMEM((n, 128), bf16),
            pltpu.VMEM((fq, 128), f32),
            pltpu.VMEM((fq, 128), f32),
            pltpu.VMEM((n, 128), f32),
        ],
        compiler_params=limits(24),
        cost_estimate=cost(22),
        name="attn_fwd",
    )(*ranges, q, own, oth, seg)


def bwd_kernel(fine, sq, sk, qlo, qhi, klo, khi, q_ref, own_ref, oth_ref, pack_ref, o_ref, lrow,
               seg_ref, dq_out, dk_own, dk_oth, do_ref, drow, dk_sum, dq_ref, sk_own, sk_oth):
    n = q_ref.shape[0]
    low = left_lanes((ROWS, 128))

    @pl.when((klo[0, 0] != khi[0, n // fine - 1]) | (klo[0, 0] != khi[1, n // fine - 1]))
    def _():
        columns(seg_ref, sk_own, 0)
        columns(seg_ref, sk_oth, 1)

    for b in range(n // ROWS):
        s = pl.ds(b * ROWS, ROWS)
        packed = pack_ref[b].astype(f32)
        do = jnp.where(low, jnp.concatenate([packed, swapped(packed)], axis=0), 0.0)
        do_ref[s, :] = do.astype(bf16)
        delta = jnp.sum(do * o_ref[s, :].astype(f32), axis=1, keepdims=True)
        drow[0:1, s] = jnp.broadcast_to(delta, (ROWS, 128)).T[0:1, :]
    dq_ref[...] = jnp.zeros_like(dq_ref)
    sides = ((1, oth_ref, dk_oth, sk_oth), (0, own_ref, dk_own, sk_own))
    for half, k_ref, dk_ref, sk_ref in sides:
        dk_sum[...] = jnp.zeros_like(dk_sum)

        def visit(i, j, wide, deep, masked, k_ref=k_ref, sk_ref=sk_ref):
            qs = pl.ds(pl.multiple_of(i * wide * fine, wide * fine), wide * fine)
            ks = pl.ds(pl.multiple_of(j * deep * fine, deep * fine), deep * fine)
            keys = k_ref[ks, :]
            q = q_ref[qs, :]
            do = do_ref[qs, :]
            s = dot_nt(keys, q)
            dp = dot_nt(keys, do)
            p = jnp.exp2(s - lrow[0:1, qs])
            if masked:
                p = jnp.where(sk_ref[ks, 0:1] == seg_ref[0:1, qs], p, 0.0)
            ds = (p * (dp - drow[0:1, qs])).astype(bf16)
            dk_sum[ks, :] += dot_nn(p.astype(bf16), do) + dot_nn(ds, q)
            dq_ref[:, qs] += dot_nn(keys.T, ds)

        def k_step(j, _, half=half, visit=visit):
            def q_step(i, _):
                tiles(visit, qlo, qhi, klo.at[half], khi.at[half], i, j, sq, sk)
                return 0

            lax.fori_loop(0, n // (sq * fine), q_step, 0)
            return 0

        lax.fori_loop(0, n // (sk * fine), k_step, 0)
        low = left_lanes((n, 128))
        dk_ref[...] = (dk_sum[...] * jnp.where(low, 1.0, 1.0 / LOG2E)).astype(dk_ref.dtype)
    dq_out[...] = (dq_ref[...].T * HDIM**-0.5).astype(bf16)


def attn_bwd(fine, sq, sk, ranges, q, own, oth, pack, o, lse, seg):
    n = q.shape[0]
    return pl.pallas_call(
        functools.partial(bwd_kernel, fine, sq, sk),
        grid=(1,),
        out_shape=(shape((n, 128), bf16), shape((n, 128), f32), shape((n, 128), bf16)),
        in_specs=[SMEM] * 4
        + [whole(*a.shape) for a in (q, own, oth, pack, o, lse, seg)],
        out_specs=(whole(n, 128), whole(n, 128), whole(n, 128)),
        scratch_shapes=[
            pltpu.VMEM((n, 128), bf16),
            pltpu.VMEM((8, n), f32),
            pltpu.VMEM((n, 128), f32),
            pltpu.VMEM((128, n), f32),
            pltpu.VMEM((n, 128), f32),
            pltpu.VMEM((n, 128), f32),
        ],
        compiler_params=limits(60),
        cost_estimate=cost(120),
        name="attn_bwd",
    )(*ranges, q, own, oth, pack, o, lse, seg)


def heads_kernel(w_ref, gains_ref, seg_ref, sent_ref, wqkv_ref):
    left = left_lanes((32, 128))
    row = lax.broadcasted_iota(jnp.int32, (32, 128), 0)
    seg = jnp.broadcast_to(seg_ref[...], (32, 128))
    high, rest = (seg >> 6).astype(f32), (seg & 63).astype(f32)
    misc = jnp.broadcast_to(gains_ref[...], (32, 128))
    for k, part in enumerate((high, swapped(high), rest, swapped(rest))):
        misc = jnp.where(row == k + 1, part, misc)
    for p in range(HEADS // 2):
        q, k, v = (
            w_ref[:, 1024 * i + 128 * p : 1024 * i + 128 * (p + 1)].astype(f32) for i in range(3)
        )
        even = jnp.where(left, v, swapped(q)).astype(bf16)
        odd = jnp.where(left, swapped(v), q).astype(bf16)
        even_k = jnp.where(left, misc, swapped(k)).astype(bf16)
        odd_k = jnp.where(left, misc, k).astype(bf16)
        for c in range(2):
            sent_ref[4 * p + c, :, :128] = even
            sent_ref[4 * p + c, :, 128:] = even_k
            sent_ref[4 * p + 2 + c, :, :128] = odd
            sent_ref[4 * p + 2 + c, :, 128:] = odd_k
        wqkv_ref[:, 256 * p : 256 * p + 128] = even
        wqkv_ref[:, 256 * p + 128 : 256 * (p + 1)] = odd
        wqkv_ref[:, 2048 + 128 * p : 2048 + 128 * (p + 1)] = k.astype(bf16)


def heads_out(w, gains, seg):
    return pl.pallas_call(
        heads_kernel,
        out_shape=(shape((32, 32, 256), bf16), shape((32, 3072), bf16)),
        in_specs=[VMEM] * 3,
        out_specs=(VMEM, VMEM),
        compiler_params=limits(16),
        cost_estimate=cost(1),
        name="heads_out",
    )(w, gains, seg)


def unit_places():
    spread, pick = np.zeros((4, SPAN, 8 * SLOT)), np.zeros((4, SLOT, BLOCK))
    for z in range(4):
        for r in range(FIRST[z + 1] - FIRST[z]):
            pick[z, r, FIRST[z] + r] = 1
            for i in range(8):
                spread[z, BLOCK * i + FIRST[z] + r, SLOT * i + r] = 1
    return jnp.asarray(spread, bf16), jnp.asarray(pick, bf16)


def bundle_kernel(plane_ref, in_ref, spread_ref, pick_ref, mlp_ref, out_ref, bundle_ref, held):
    spread = spread_ref[plane_ref[0]]
    for k in range(8):
        part = dot_nn(in_ref[:, SPAN * k : SPAN * (k + 1)], spread)
        held[:, 8 * SLOT * k : 8 * SLOT * (k + 1)] = part
    for j in range(6):
        bundle_ref[32 * j : 32 * (j + 1), :] = held[:, 256 * j : 256 * (j + 1)].astype(bf16)
    mlp = dot_nn(pick_ref[plane_ref[0]], mlp_ref[...])
    parts = [mlp[:, 256 * j : 256 * (j + 1)] for j in range(4)]
    bundle_ref[192:OUT_FIRST, :] = jnp.concatenate(parts).astype(bf16)
    for j in range(4):
        cols = slice(256 * j, 256 * (j + 1))
        bundle_ref[OUT_FIRST + 32 * j : OUT_FIRST + 32 * (j + 1), :] = out_ref[:, cols]


def bundle_out(plane, w_in, spread, pick, w_mlp, w_out):
    return pl.pallas_call(
        bundle_kernel,
        out_shape=shape((BUNDLE, 256), bf16),
        in_specs=[SMEM] + [VMEM] * 5,
        out_specs=VMEM,
        scratch_shapes=[pltpu.VMEM((32, 2 * WIDE), f32)],
        compiler_params=limits(16),
        cost_estimate=cost(1),
        name="bundle_out",
    )(plane, w_in, spread, pick, w_mlp, w_out)


def turns():
    inverse = THETA ** (-np.arange(0, HDIM, 2) / HDIM)
    sign = np.repeat([-1.0, 1.0, -1.0, 1.0], 32)
    both = []
    for scale in (64, 1):
        angle = np.tile(np.arange(64)[:, None] * scale * inverse[None], (1, 4))
        table = np.concatenate([np.cos(angle), np.sin(angle) * sign], axis=1).astype(np.float32)
        main = table.astype(jnp.bfloat16)
        both.append(np.concatenate([main, (table - main.astype(np.float32)).astype(jnp.bfloat16)]))
    return jnp.asarray(np.stack(both), bf16)


def fill_tables(core, seg_ref, turn_ref, cos_ref, sin_ref):
    code = lax.broadcasted_iota(jnp.int32, (ROWS, ROWS), 0) & 63
    lane = lax.broadcasted_iota(jnp.int32, (1, ROWS), 1)
    for b in range(seg_ref.shape[1] // ROWS):
        rows = slice(b * ROWS, (b + 1) * ROWS)
        place = (2 * b + core) * ROWS + lane - seg_ref[:, rows]
        high = dot_tn((code == (place >> 6)).astype(f32).astype(bf16), turn_ref[0])
        rest = dot_tn((code == (place & 63)).astype(f32).astype(bf16), turn_ref[1])
        cos_ref[rows, :] = high[:, :128] * rest[:, :128] - high[:, 128:] * rest[:, 128:]
        sin_ref[rows, :] = high[:, 128:] * rest[:, :128] + high[:, :128] * rest[:, 128:]


def qkv_kernel(sizes, *refs):
    place = refs[0]
    pieces = refs[1 : 1 + len(sizes)]
    gain_ref, w_ref, seg_ref, turn_ref, n_ref, q_ref, k_ref, cos_ref, sin_ref = refs[1 + len(sizes) :]
    fill_tables(place[32], seg_ref, turn_ref, cos_ref, sin_ref)
    gain = gain_ref[...]
    w = w_ref[...]
    group = 0
    for piece, size in zip(pieces, sizes):
        z, _ = norm_parts(piece[...].astype(f32))
        normed = (z * gain).astype(bf16)
        both = dot_nn(normed, w)
        for g in range(size // 64):
            to = pl.ds(pl.multiple_of(place[group] * 64, 64), 64)
            group += 1
            mine = slice(g * 64, (g + 1) * 64)
            cos, sin = cos_ref[to, :], sin_ref[to, :]
            lane = lax.broadcasted_iota(jnp.int32, (64, 128), 1)

            def turn(t):
                other = jnp.where(lane < 96, pltpu.roll(t, 96, 1), pltpu.roll(t, 32, 1))
                return t * cos + other * sin

            first, second = both[mine, :128], both[mine, 128:]
            q_ref[to, :] = jnp.where(lane < HDIM, 0.0, turn(first) * (LOG2E * HDIM**-0.5)).astype(bf16)
            n_ref[to, :] = normed[mine]
            k_ref[to, :] = jnp.where(lane < HDIM, first, turn(second)).astype(bf16)


def qkv(place, pieces, gain, w, seg):
    n, width = seg.shape[1], pieces[0].shape[1]
    sizes = tuple(p.shape[0] for p in pieces)
    return pl.pallas_call(
        functools.partial(qkv_kernel, sizes),
        out_shape=(shape((n, width), bf16), shape((n, 128), bf16), shape((n, 128), bf16)),
        in_specs=[SMEM] + [VMEM] * (len(pieces) + 4),
        out_specs=(VMEM, VMEM, VMEM),
        scratch_shapes=[pltpu.VMEM((n, 128), f32)] * 2,
        compiler_params=limits(24),
        cost_estimate=cost(6),
        name="qkv",
    )(place, *pieces, gain, w, seg, turns())


OUT_PARTS = [weight_part(32, OUT_FIRST + 32 * j) for j in range(4)]


def proj_kernel(pack_ref, x_ref, gain_ref, w0, w1, w2, w3, n_ref, h_ref, o_ref):
    for p in range(HEADS // 2):
        both = unpack_pair(pack_ref[2 * p].astype(f32), pack_ref[2 * p + 1].astype(f32))
        o_ref[:, p * 128 : (p + 1) * 128] = both.astype(bf16)
    o = o_ref[...]
    for j, w in enumerate((w0, w1, w2, w3)):
        cols = slice(256 * j, 256 * (j + 1))
        h_ref[:, cols] = x_ref[:, cols].astype(f32) + dot_nn(o, w[...].reshape(1024, 256))
    z, _ = norm_parts(h_ref[...])
    n_ref[...] = (z * gain_ref[...]).astype(bf16)


def proj(pack, x, gain, bundle):
    n, width = x.shape
    return pl.pallas_call(
        proj_kernel,
        grid=(1,),
        out_shape=(shape((n, width), bf16), shape((n, width), f32), shape((n, width), bf16)),
        in_specs=[whole(*pack.shape), whole(n, width), whole(1, width), *OUT_PARTS],
        out_specs=(whole(n, width), whole(n, width), whole(n, width)),
        compiler_params=limits(58),
        cost_estimate=cost(3),
        name="proj",
    )(pack, x, gain, bundle, bundle, bundle, bundle)


def normal_cdf(x, bell):
    t = 1.0 / (1.0 + (0.3275911 * 0.5**0.5) * jnp.abs(x))
    tail = 1.061405429
    for term in (-1.453152027, 1.421413741, -0.284496736, 0.254829592):
        tail = tail * t + term
    tail = 0.5 * tail * t * bell
    return jnp.where(x >= 0.0, 1.0 - tail, tail)


def units_kernel(*refs):
    n_refs, g_refs = refs[:4], refs[4:8]
    win_ref, m_ref = refs[8], refs[9]
    act_ref, dup_ref, n_all, g_all, w_ref = refs[10:15]
    d_refs, w_in = refs[15:19], refs[19]
    for i in range(4):
        n_all[i * ROWS : (i + 1) * ROWS, :] = n_refs[i][...]
        g_all[i * ROWS : (i + 1) * ROWS, :] = g_refs[i][...]
    normed = n_all[...]
    g = g_all[...]

    slots = m_ref[...].astype(f32)
    for a in range(4):
        part = slots[:, SLOT * a : SLOT * (a + 1)].reshape(WIDE, 256)
        w_ref[:, 256 * a : 256 * (a + 1)] = part.astype(bf16)
    for j in range(6):
        w_in[:, 256 * j : 256 * (j + 1)] = win_ref[:, 32 * j : 32 * (j + 1), :].reshape(1024, 256)

    for j in range(3):
        cols = slice(256 * j, 256 * (j + 1))
        more = slice(WIDE + 256 * j, WIDE + 256 * (j + 1))
        first = dot_nn(normed, w_in[:, cols])
        second = dot_nn(normed, w_in[:, more])
        d_act = dot_nt(g, w_ref[cols, :])
        bell = jnp.exp(-0.5 * first * first)
        cdf = normal_cdf(first, bell)
        slope = cdf + first * (bell * (1.0 / (2.0 * np.pi) ** 0.5))
        gated = first * cdf
        act_ref[:, cols] = (gated * second).astype(bf16)
        dup_ref[:, cols] = (d_act * second * slope).astype(bf16)
        dup_ref[:, more] = (d_act * gated).astype(bf16)
    total = dot_nt(dup_ref[...], w_in[...])
    for i in range(4):
        d_refs[i][...] = total[i * ROWS : (i + 1) * ROWS].astype(bf16)


def units(normed, cots, bundle):
    n, width = normed[0].shape
    tokens = 4 * n
    return pl.pallas_call(
        units_kernel,
        grid=(1,),
        out_shape=(
            shape((tokens, WIDE), bf16),
            shape((tokens, 2 * WIDE), bf16),
            shape((tokens, width), bf16),
            shape((tokens, width), bf16),
            shape((WIDE, width), bf16),
            *[shape((n, width), bf16)] * 4,
        ),
        in_specs=[whole(n, width)] * 8
        + [weight_part(192, 0), weight_part(4 * SLOT, 192)],
        out_specs=(
            whole(tokens, WIDE),
            whole(tokens, 2 * WIDE),
            whole(tokens, width),
            whole(tokens, width),
            whole(WIDE, width),
            *[whole(n, width)] * 4,
        ),
        scratch_shapes=[pltpu.VMEM((width, 2 * WIDE), bf16)],
        compiler_params=limits(58),
        cost_estimate=cost(11),
        name="units",
    )(*normed, *cots, bundle, bundle)


def unit_grads_kernel(act_ref, dup_ref, n_all, g_all, out_hbm, out_ref, sem):
    act = act_ref[...].T
    grads = [dot_nn(act, g_all[:, 256 * a : 256 * (a + 1)]) for a in range(4)]
    for b in range(32):
        slot = jnp.concatenate([grad[SLOT * b : SLOT * (b + 1)] for grad in grads])
        out_ref[(b % 8) * 4 + b // 8, 192:OUT_FIRST, :] = slot.astype(bf16)
    normed = n_all[...].T
    for j in range(6):
        grad = dot_nn(normed, dup_ref[:, 256 * j : 256 * (j + 1)]).astype(bf16)
        for b in range(32):
            out_ref[(b % 8) * 4 + b // 8, 32 * j : 32 * (j + 1), :] = grad[32 * b : 32 * (b + 1)]
    copy = pltpu.make_async_copy(out_ref, out_hbm.at[:, pl.ds(0, OUT_FIRST)], sem)
    copy.start()
    copy.wait()


def unit_grads(act, dup, n_all, g_all):
    tokens, width = n_all.shape
    return pl.pallas_call(
        unit_grads_kernel,
        out_shape=shape((32, BUNDLE, 256), bf16),
        grid=(1,),
        in_specs=[whole(*a.shape) for a in (act, dup, n_all, g_all)],
        out_specs=HBM,
        scratch_shapes=[pltpu.VMEM((32, OUT_FIRST, 256), bf16), pltpu.SemaphoreType.DMA],
        compiler_params=limits(60),
        cost_estimate=cost(2),
        name="unit_grads",
    )(act, dup, n_all, g_all)


def out_grad_kernel(o_ref, da_ref, in_hbm, out_hbm, out_ref, sem):
    del in_hbm
    grad = dot_tn(o_ref[...], da_ref[...]).astype(bf16)
    for b in range(32):
        for j in range(4):
            out_ref[(b % 8) * 4 + b // 8, 32 * j : 32 * (j + 1), :] = grad[
                32 * b : 32 * (b + 1), 256 * j : 256 * (j + 1)
            ]
    copy = pltpu.make_async_copy(out_ref, out_hbm.at[:, pl.ds(OUT_FIRST, 128)], sem)
    copy.start()
    copy.wait()


def out_grad(o, da, grads):
    return pl.pallas_call(
        out_grad_kernel,
        out_shape=shape(grads.shape, bf16),
        grid=(1,),
        in_specs=[whole(*o.shape), whole(*da.shape), HBM],
        out_specs=HBM,
        scratch_shapes=[pltpu.VMEM((32, 128, 256), bf16), pltpu.SemaphoreType.DMA],
        input_output_aliases={2: 0},
        compiler_params=limits(60),
        cost_estimate=cost(1),
        name="out_grad",
    )(o, da, grads)


def unit_out_kernel(act_ref, w_ref, p0, p1, p2, p3):
    act = act_ref[...]
    for a in range(4):
        cols = slice(256 * a, 256 * (a + 1))
        part = dot_nn(act, w_ref[:, cols]).astype(bf16)
        for i, p in enumerate((p0, p1, p2, p3)):
            p[:, cols] = part[i * ROWS : (i + 1) * ROWS]


def unit_out(act, w):
    return pl.pallas_call(
        unit_out_kernel,
        grid=(1,),
        out_shape=[shape((ROWS, 1024), bf16)] * 4,
        in_specs=[whole(*act.shape), whole(*w.shape)],
        out_specs=[whole(ROWS, 1024)] * 4,
        compiler_params=limits(60),
        cost_estimate=cost(0.5),
        name="unit_out",
    )(act, w)


def proj_back_kernel(d0, d1, d2, d3, h_ref, gain_ref, cot_ref, w0, w1, w2, w3,
                     pack_ref, dh_ref, da_ref):
    total = d0[...].astype(f32) + d1[...].astype(f32) + d2[...].astype(f32) + d3[...].astype(f32)
    z, scale = norm_parts(h_ref[...])
    dh = cot_ref[...].astype(f32) + norm_back(total * gain_ref[...], z, scale)
    dh_ref[...] = dh
    da_ref[...] = dh.astype(bf16)
    do = sum(
        dot_nt(da_ref[:, 256 * j : 256 * (j + 1)], w[...].reshape(1024, 256))
        for j, w in enumerate((w0, w1, w2, w3))
    )
    for p in range(HEADS // 2):
        even, odd = pack_pair(do[:, p * 128 : (p + 1) * 128])
        pack_ref[2 * p] = even.astype(bf16)
        pack_ref[2 * p + 1] = odd.astype(bf16)


def proj_back(ds, h, gain, cot, bundle):
    n, width = h.shape
    return pl.pallas_call(
        proj_back_kernel,
        grid=(1,),
        out_shape=(shape((HEADS, 64, 128), bf16), shape((n, width), f32), shape((n, width), bf16)),
        in_specs=[whole(n, width)] * 5 + [whole(1, width), whole(n, width), *OUT_PARTS],
        out_specs=(whole(HEADS, 64, 128), whole(n, width), whole(n, width)),
        compiler_params=limits(58),
        cost_estimate=cost(3),
        name="proj_back",
    )(*ds, h, gain, cot, bundle, bundle, bundle, bundle)


def turn_back_kernel(core_ref, dq_ref, own_ref, oth_ref, seg_ref, turn_ref, n_ref,
                     sent_ref, keep_ref, give_ref, d_ref, grad_ref, held, cos_ref, sin_ref, sem):
    fetch = pltpu.make_async_copy(n_ref, held, sem)
    fetch.start()
    fill_tables(core_ref[0], seg_ref, turn_ref, cos_ref, sin_ref)
    for b in range(dq_ref.shape[0] // ROWS):
        s = slice(b * ROWS, (b + 1) * ROWS)
        cos, sin = cos_ref[s, :], sin_ref[s, :]
        lane = lax.broadcasted_iota(jnp.int32, (ROWS, 128), 1)

        def turn(t):
            other = jnp.where(lane < 96, pltpu.roll(t, 96, 1), pltpu.roll(t, 32, 1))
            return t * cos - other * sin

        dk = own_ref[s, :] + oth_ref[s, :].astype(f32)
        first = jnp.where(lane < HDIM, dk, turn(dq_ref[s, :].astype(f32)))
        second = jnp.where(lane < HDIM, 0.0, turn(dk))
        d_ref[s, :128] = first.astype(bf16)
        d_ref[s, 128:] = second.astype(bf16)
        sent_ref[b, :ROWS, :] = first.astype(bf16)
        packed = jnp.where(left_lanes((64, 128)), swapped(second[:64]), second[64:])
        sent_ref[b, ROWS:192, :] = packed.astype(bf16)
    fetch.wait()
    grad = dot_tn(d_ref[...], held[...]).T
    grad_ref[...] = grad.reshape(grad_ref.shape)
    core = core_ref[0]
    for h in range(HEADS):
        keep_ref[h] = grad_ref[2 * h + core]
        give_ref[h] = grad_ref[2 * h + 1 - core].astype(bf16)


def turn_back(core, dq, own, oth, seg, normed):
    n = dq.shape[0]
    return pl.pallas_call(
        turn_back_kernel,
        out_shape=(
            shape((HEADS, 192, 128), bf16),
            shape((HEADS, 32, 256), f32),
            shape((HEADS, 32, 256), bf16),
        ),
        grid=(1,),
        in_specs=[SMEM]
        + [whole(*a.shape) for a in (dq, own, oth, seg)]
        + [whole(2, ROWS, 256), HBM],
        out_specs=(whole(HEADS, 192, 128), whole(HEADS, 32, 256), whole(HEADS, 32, 256)),
        scratch_shapes=[
            pltpu.VMEM((n, 256), bf16),
            pltpu.VMEM((32, 32, 256), f32),
            pltpu.VMEM(normed.shape, bf16),
            pltpu.VMEM((n, 128), f32),
            pltpu.VMEM((n, 128), f32),
            pltpu.SemaphoreType.DMA,
        ],
        compiler_params=limits(60),
        cost_estimate=cost(5),
        name="turn_back",
    )(core, dq, own, oth, seg, turns(), normed)


def pack_kernel(keep_ref, took_ref, out_ref):
    left = left_lanes((16, 128))
    for h in range(HEADS):
        both = keep_ref[h] + took_ref[h].astype(f32)
        k = both[:, 128:]
        out_ref[h, :32, :] = both[:, :128].astype(bf16)
        out_ref[h, 32:, :] = jnp.where(left, swapped(k[:16]), k[16:]).astype(bf16)


def pack_head(keep, took):
    return pl.pallas_call(
        pack_kernel,
        grid=(1,),
        out_shape=shape((HEADS, 48, 128), bf16),
        in_specs=[whole(*keep.shape), whole(*took.shape)],
        out_specs=whole(HEADS, 48, 128),
        compiler_params=limits(60),
        cost_estimate=cost(1),
        name="pack_head",
    )(keep, took)


def input_kernel(got_ref, w_ref, x_ref, gain_ref, dh_ref, out_ref, d_ref, acc_ref):
    step = pl.program_id(0)

    @pl.when(step == 0)
    def _():
        for h in range(HEADS):
            d_ref[h // 4, :, 128 * (h % 4) : 128 * (h % 4 + 1)] = got_ref[h, :ROWS, :]
        for p in range(HEADS // 2):
            both = unpack_pair(
                got_ref[2 * p, ROWS:192, :].astype(f32), got_ref[2 * p + 1, ROWS:192, :].astype(f32)
            )
            d_ref[4 + p // 4, :, 128 * (p % 4) : 128 * (p % 4 + 1)] = both.astype(bf16)
        acc_ref[...] = jnp.zeros_like(acc_ref)

    acc_ref[...] += dot_nt(d_ref[step], w_ref[...])

    @pl.when(step == pl.num_programs(0) - 1)
    def _():
        z, scale = norm_parts(x_ref[...].astype(f32))
        back = norm_back(acc_ref[...] * gain_ref[...], z, scale)
        out_ref[...] = (dh_ref[...] + back).astype(bf16)


def input_back(got, w, x, gain, dh):
    n, width = x.shape
    return pl.pallas_call(
        input_kernel,
        grid=(6,),
        out_shape=shape((n, width), bf16),
        in_specs=[
            whole(*got.shape),
            pl.BlockSpec((width, 512), lambda i: (0, i)),
            whole(n, width),
            whole(1, width),
            whole(n, width),
        ],
        out_specs=whole(n, width),
        scratch_shapes=[pltpu.VMEM((6, n, 512), bf16), pltpu.VMEM((n, width), f32)],
        compiler_params=limits(32),
        cost_estimate=cost(4),
        name="input_back",
    )(got, w, x, gain, dh)


def rows_kernel(got_ref, out_ref):
    left = left_lanes((32, 128))
    half = left_lanes((16, 128))
    for p in range(HEADS // 2):
        even, odd = (got_ref[2 * p + i, :32, :].astype(f32) for i in range(2))
        even_k, odd_k = (got_ref[2 * p + i, 32:, :].astype(f32) for i in range(2))
        q = jnp.where(left, swapped(even), odd)
        v = jnp.where(left, even, swapped(odd))
        k = jnp.concatenate(
            [jnp.where(half, even_k, swapped(odd_k)), jnp.where(half, swapped(even_k), odd_k)]
        )
        for i, part in enumerate((q, k, v)):
            j = 8 * i + p
            out_ref[32 * (j // 2) : 32 * (j // 2 + 1), 128 * (j % 2) : 128 * (j % 2 + 1)] = part.astype(bf16)


def gather_rows(got):
    return pl.pallas_call(
        rows_kernel,
        out_shape=shape((384, 256), bf16),
        in_specs=[VMEM],
        out_specs=VMEM,
        compiler_params=limits(16),
        cost_estimate=cost(1),
        name="gather_rows",
    )(got)


def as_row(column):
    full = jnp.concatenate([column, jnp.zeros((ROWS - 32, 1), f32)])
    return jnp.broadcast_to(full, (ROWS, ROWS)).T[0:1]


def planes_kernel(plane_ref, h0, h1, h2, h3, r0, r1, r2, r3, spread_ref, pick_ref, wqkv_ref, win_ref, g1_ref, g2_ref,
                  qkv_ref, out_ref, in_ref, mlp_ref, norm1_ref, norm2_ref, held):
    pieces = (r0, r1, r2, r3)
    planes = [plane_ref[k] for k in range(4)]

    def total(refs, first):
        return sum(r[first : first + 32, :].astype(f32) for r in refs)

    norm = jnp.zeros((32, 1), f32)
    for j in range(12):
        cols = slice(256 * j, 256 * (j + 1))
        part = total((h0, h1, h2, h3), 32 * j)
        qkv_ref[:, cols] = part
        norm += jnp.sum(part * wqkv_ref[:, cols].astype(f32), axis=1, keepdims=True)
    norm1_ref[...] = as_row(norm / g1_ref[...])
    all_slots = [r[192:OUT_FIRST, :].astype(f32) for r in pieces]
    for j in range(4):
        cols = slice(256 * j, 256 * (j + 1))
        out_ref[:, cols] = total(pieces, OUT_FIRST + 32 * j)
        slot = slice(SLOT * j, SLOT * (j + 1))
        mlp_ref[:, cols] = sum(
            dot_tn(pick_ref[z], slots[slot].astype(bf16)) for z, slots in zip(planes, all_slots)
        )
    grads = jnp.zeros((256, SPAN), f32)
    for z, r in zip(planes, pieces):
        wide = jnp.concatenate([r[32 * j : 32 * (j + 1), :] for j in range(6)], axis=1)
        for k in range(8):
            held[32 * k : 32 * (k + 1), :] = wide[:, 8 * SLOT * k : 8 * SLOT * (k + 1)]
        grads += dot_nt(held[...], spread_ref[z])
    norm = jnp.zeros((32, 1), f32)
    for k in range(8):
        cols = slice(SPAN * k, SPAN * (k + 1))
        part = grads[32 * k : 32 * (k + 1)]
        in_ref[:, cols] = part
        norm += jnp.sum(part * win_ref[:, cols].astype(f32), axis=1, keepdims=True)
    norm2_ref[...] = as_row(norm / g2_ref[...])


def add_planes(plane, heads, parts, spread, pick, wqkv, win, gain_one, gain_two):
    return pl.pallas_call(
        planes_kernel,
        out_shape=(
            shape(wqkv.shape, f32),
            shape((32, 1024), f32),
            shape(win.shape, f32),
            shape((BLOCK, 1024), f32),
            shape((1, ROWS), f32),
            shape((1, ROWS), f32),
        ),
        in_specs=[SMEM] + [VMEM] * 14,
        out_specs=(VMEM,) * 6,
        scratch_shapes=[pltpu.VMEM((256, 8 * SLOT), bf16)],
        compiler_params=limits(24),
        cost_estimate=cost(5),
        name="add_planes",
    )(plane, *heads, *parts, spread, pick, wqkv, win, gain_one, gain_two)


def shift(value, axis, steps):
    count = lax.axis_size(axis)
    return lax.ppermute(value, axis, [(i, (i + steps) % count) for i in range(count)])


def both_ways(value, axis):
    first = [(2 * i + c, (2 * i + 2 - 4 * c) % 8 + c) for i in range(4) for c in range(2)]
    other = [(b, a) for a, b in first]
    near = lax.ppermute(value, (axis, "c"), first)
    return [value, near, lax.ppermute(value, (axis, "c"), other), lax.ppermute(near, (axis, "c"), first)]


def from_planes(value):
    return [value] + [shift(value, "z", k) for k in SHIFTS[1:]]


def back_to_planes(pieces):
    return [pieces[0]] + [shift(p, "z", -k) for p, k in zip(pieces[1:], SHIFTS[1:])]


def far(value, near, axis):
    half = value.shape[0] // 2
    behind, ahead = near
    return [value, behind, ahead, shift(behind[:half], axis, 1), shift(ahead[half:], axis, 3)]


def exchange(value, axes):
    return lax.all_to_all(value, axes, split_axis=0, concat_axis=0, tiled=True)


def shards(hidden_in, seg_start, norm1_gain, qkv_weight, out_weight, norm2_gain, in_weight,
           mlp_weight, out_cotangent):
    plane, core = lax.axis_index("z"), lax.axis_index("c")
    mine = (lax.axis_index("x"), lax.axis_index("y"))
    plane_id, core_id = plane.astype(jnp.int32)[None], core.astype(jnp.int32)[None]
    x_own = hidden_in[0]
    cot = out_cotangent[0]
    width = x_own.shape[1]
    rows = qkv_weight.shape[0]

    upper, lower = x_own[:64], x_own[64:]
    upper = [upper] + [shift(upper, "x", k) for k in SHIFTS[1:]]
    lower = [lower] + [shift(lower, "y", k) for k in SHIFTS[1:]]
    upper, lower = jnp.concatenate(upper), jnp.concatenate(lower)

    gains = jnp.pad(jnp.concatenate([norm1_gain, norm2_gain]), (0, HDIM)).astype(f32)[None]
    sent, wqkv = heads_out(qkv_weight, gains, seg_start)
    spread, pick = unit_places()
    bundle = bundle_out(plane_id, in_weight, spread, pick, mlp_weight, out_weight)
    upper, lower, sent, bundle = lax.optimization_barrier((upper, lower, sent, bundle))
    got = exchange(sent, XYC)
    pieces = both_ways(upper, "y") + both_ways(lower, "x")
    steps = (0, 1 - 2 * core, 2 * core - 1, 2)
    place = []
    for half in (0, 1):
        for outer in steps:
            for inner in SHIFTS:
                sx, sy = (inner, outer) if half == 0 else (outer, inner)
                place.append((((mine[0] - sx) % 4) * 4 + (mine[1] - sy) % 4) * 2 + half)
    place = jnp.stack([*place, core]).astype(jnp.int32)
    w_head = got.reshape(width, 256)
    gain_one = got[:, 0, 128:160].reshape(1, width).astype(f32)
    gain_two = got[:, 0, 160:192].reshape(1, width).astype(f32)
    high, rest = got[:, 1:3, 128:192].astype(jnp.int32), got[:, 3:5, 128:192].astype(jnp.int32)
    seg_all = (high * 64 + rest).reshape(HEADS, 2, ROWS)
    seg_own = jnp.where(core == 0, seg_all[:, 0], seg_all[:, 1]).reshape(-1)
    seg_oth = jnp.where(core == 0, seg_all[:, 1], seg_all[:, 0]).reshape(-1)
    pieces, seg_own, seg_oth, gain_one, gain_two, bundle = lax.optimization_barrier(
        (pieces, seg_own, seg_oth, gain_one, gain_two, bundle)
    )
    bundle = lax.all_gather(bundle, XYC, axis=0, tiled=False)


    normed_one, queries, keys = qkv(place, pieces, gain_one, w_head, seg_own[None])
    keys_oth = shift(keys, "c", 1)

    def bounds(seg, size):
        tiles = seg.reshape(-1, size)
        return tiles[:, 0], tiles[:, -1]

    (qlo, qhi), (olo, ohi), (tlo, thi) = bounds(seg_own, 256), bounds(seg_own, 1024), bounds(seg_oth, 1024)
    both_segs = jnp.stack([seg_own, seg_oth]).astype(f32)
    o_pack, o, lse = attn_fwd(
        256, 1024, 2, (qlo, qhi, jnp.minimum(olo, tlo), jnp.maximum(ohi, thi)),
        queries, keys, keys_oth, both_segs,
    )
    o_pack, cot = lax.optimization_barrier((o_pack, cot))
    cots = from_planes(cot)
    o_got = exchange(o_pack, XY)
    wqkv, o_got, cots = lax.optimization_barrier((wqkv, o_got, cots))
    wqkv = lax.all_gather(wqkv, XYC, axis=0, tiled=True)

    normed_two, middle, o_tok = proj(o_got, x_own, gain_two, bundle)
    act, dup, n_all, g_all, w_units, *d_parts = units(from_planes(normed_two), cots, bundle)
    d_parts = back_to_planes(d_parts)
    g_sum = unit_grads(act, dup, n_all, g_all)
    d_parts, g_sum = lax.optimization_barrier((d_parts, g_sum))
    do_pack, d_mid, d_attn = proj_back(d_parts, middle, gain_two, cot, bundle)
    do_got = exchange(do_pack, XY)
    act, d_attn = lax.optimization_barrier((act, d_attn))
    g_sum = out_grad(o_tok, d_attn, g_sum)
    out_parts = unit_out(act, w_units)
    do_got, out_parts = lax.optimization_barrier((do_got, out_parts))
    g_sum, wqkv = lax.optimization_barrier((g_sum, wqkv))
    g_sum = lax.psum_scatter(g_sum.reshape(8, 4 * BUNDLE, 256), YC, scatter_dimension=0, tiled=False)

    (qlo, qhi), (tlo, thi) = bounds(seg_own, 512), bounds(seg_oth, 512)
    ranges = (qlo, qhi, jnp.stack([qlo, tlo]), jnp.stack([qhi, thi]))
    dq, dk_own, dk_oth = attn_bwd(512, 4, 2, ranges, queries, keys, keys_oth, do_got, o, lse, both_segs)
    d_sent, keep, give = turn_back(core_id, dq, dk_own, shift(dk_oth, "c", 1), seg_own[None], normed_one)

    g_head = pack_head(keep, shift(give, "c", 1))
    g_head, g_sum, out_parts = lax.optimization_barrier((g_head, g_sum, out_parts))
    g_head = exchange(g_head, XY)
    g_sum = lax.psum_scatter(g_sum.reshape(4, BUNDLE, 256), "x", scatter_dimension=0, tiled=False)
    out_parts = back_to_planes(out_parts)
    g_head, d_sent, out_parts = lax.optimization_barrier((g_head, d_sent, out_parts))
    d_got = exchange(d_sent, XY)
    heads = gather_rows(g_head)
    heads, g_sum = lax.optimization_barrier((heads, g_sum))

    heads, g_rows = from_planes(heads), from_planes(g_sum)
    input_grad = input_back(d_got, wqkv, x_own, gain_one, d_mid)
    hidden_out = (middle + sum(p.astype(f32) for p in out_parts)).astype(bf16)
    heads, g_rows, input_grad, hidden_out = lax.optimization_barrier(
        (heads, g_rows, input_grad, hidden_out)
    )
    g_qkv, g_out, g_in, g_mlp, grad_one, grad_two = add_planes(
        jnp.stack([(plane - k) % 4 for k in SHIFTS]).astype(jnp.int32), heads, g_rows, spread, pick,
        qkv_weight, in_weight,
        norm1_gain.astype(f32)[:, None], norm2_gain.astype(f32)[:, None],
    )
    return (
        hidden_out[None],
        input_grad[None],
        g_qkv,
        g_out,
        g_in,
        g_mlp,
        grad_one[0, :32],
        grad_two[0, :32],
    )


def solution(mesh):
    fine = Mesh(mesh.devices.reshape(4, 4, 4, 2), ("z", "x", "y", "c"))
    blk = ("x", "y", "c")
    return jax.shard_map(
        shards,
        mesh=fine,
        in_specs=(
            P("z", blk, None),
            P("z", blk),
            P(blk),
            P(blk, None),
            P(blk, None),
            P(blk),
            P(blk, None),
            P(blk, None),
            P("z", blk, None),
        ),
        out_specs=(
            P("z", blk, None),
            P("z", blk, None),
            P(blk, None),
            P(blk, None),
            P(blk, None),
            P(blk, None),
            P(blk),
            P(blk),
        ),
        check_vma=False,
    )
```

```python
import functools

import jax
import jax.numpy as jnp
import numpy as np
from jax import lax
from jax.experimental import pallas as pl
from jax.experimental.pallas import tpu as pltpu
from jax.sharding import Mesh
from jax.sharding import PartitionSpec as P

HEADS = 16
HDIM = 64
EPS = 1e-05
THETA = 160000.0
NEG = -1e30
FLOOR = -1e29
ROWS = 128
BLOCK = 82
FIRST = (0, 21, 42, 62, 82)
SLOT = 24
WIDE = 32 * SLOT
SPAN = 8 * BLOCK
OUT_FIRST = 288
BUNDLE = 416
LOG2E = 1.4426950408889634
bf16 = jnp.bfloat16
f32 = jnp.float32
XY = ("x", "y")
YC = ("y", "c")
XYC = ("x", "y", "c")
SMEM = pl.BlockSpec(memory_space=pltpu.SMEM)
VMEM = pl.BlockSpec(memory_space=pltpu.VMEM)
HBM = pl.BlockSpec(memory_space=pltpu.HBM)
SHIFTS = (0, 1, 3, 2)


def dot_nn(a, b):
    return lax.dot_general(a, b, (((1,), (0,)), ((), ())), preferred_element_type=f32)


def dot_nt(a, b):
    return lax.dot_general(a, b, (((1,), (1,)), ((), ())), preferred_element_type=f32)


def dot_tn(a, b):
    return lax.dot_general(a, b, (((0,), (0,)), ((), ())), preferred_element_type=f32)


def shape(dims, dtype):
    return jax.ShapeDtypeStruct(dims, dtype)


def limits(mib):
    return pltpu.CompilerParams(vmem_limit_bytes=mib << 20)


def cost(us):
    return pl.CostEstimate(flops=int(us * 1.1e9), bytes_accessed=int(us * 3.4e6), transcendentals=0)


def weight_part(rows, first, blocks=32):
    return pl.BlockSpec((blocks, rows, 256), lambda i: (0, first // rows, 0))


def whole(*dims):
    return pl.BlockSpec(dims, lambda i: (0,) * len(dims))


def left_lanes(dims):
    return lax.broadcasted_iota(jnp.int32, dims, len(dims) - 1) < HDIM


def swapped(v):
    return pltpu.roll(v, HDIM, 1)


def norm_parts(values):
    mid = values - jnp.mean(values, axis=-1, keepdims=True)
    scale = lax.rsqrt(jnp.mean(mid * mid, axis=-1, keepdims=True) + EPS)
    return mid * scale, scale


def norm_back(e, z, scale):
    return (
        e - jnp.mean(e, axis=-1, keepdims=True) - z * jnp.mean(e * z, axis=-1, keepdims=True)
    ) * scale


def unpack_pair(even, odd):
    left = left_lanes(even.shape)
    top = jnp.where(left, even, swapped(odd))
    bottom = jnp.where(left, swapped(even), odd)
    return jnp.concatenate([top, bottom], axis=0)


def pack_pair(rows):
    top, bottom = rows[:64], rows[64:]
    left = left_lanes(top.shape)
    return jnp.where(left, top, swapped(bottom)), jnp.where(left, swapped(top), bottom)


def columns(rows_ref, cols_ref, k):
    for b in range(rows_ref.shape[1] // ROWS):
        s = pl.ds(b * ROWS, ROWS)
        cols_ref[s, :] = jnp.broadcast_to(rows_ref[k : k + 1, s], (ROWS, ROWS)).T


def tiles(visit, qlo, qhi, klo, khi, i, j, sq, sk):
    def check(q0, q1, k0, k1, rows, cols, wide, deep, parts):
        a, b, c, d = qlo[q0], qhi[q1], klo[k0], khi[k1]
        plain = (a == b) & (c == d) & (a == c)
        mixed = (a <= d) & (c <= b) & jnp.logical_not(plain)
        pl.when(plain)(lambda: visit(rows, cols, wide, deep, False))
        pl.when(mixed)(parts)

    def fine(t, _):
        fi, fj = i * sq + t // sk, j * sk + t % sk
        check(fi, fi, fj, fj, fi, fj, 1, 1, lambda: visit(fi, fj, 1, 1, True))
        return 0

    def all_fine():
        lax.fori_loop(0, sq * sk, fine, 0)

    check(i * sq, i * sq + sq - 1, j * sk, j * sk + sk - 1, i, j, sq, sk, all_fine)


def fwd_kernel(fq, fk, sk, qlo, qhi, klo, khi, q_ref, own_ref, oth_ref, seg_ref,
               pack_ref, o_ref, lse_ref, v_own, v_oth, m_ref, acc_ref, sq_ref):
    n = q_ref.shape[0]
    low = left_lanes((n, 128))
    v_own[...] = jnp.where(low, own_ref[...], jnp.ones((), bf16))
    v_oth[...] = jnp.where(low, oth_ref[...], jnp.ones((), bf16))
    pl.when(klo[0] != khi[n // fk - 1])(lambda: columns(seg_ref, sq_ref, 0))

    def q_step(i, _):
        qs = pl.ds(pl.multiple_of(i * fq, fq), fq)
        m_ref[...] = jnp.full_like(m_ref, FLOOR)
        acc_ref[...] = jnp.zeros_like(acc_ref)

        def visit(i, j, wide, deep, masked):
            ks = pl.ds(pl.multiple_of(j * deep * fk, deep * fk), deep * fk)
            q = q_ref[qs, :]
            sa = dot_nt(q, own_ref[ks, :])
            sb = dot_nt(q, oth_ref[ks, :])
            if masked:
                seg = sq_ref[qs, 0:1]
                sa = jnp.where(seg == seg_ref[0:1, ks], sa, NEG)
                sb = jnp.where(seg == seg_ref[1:2, ks], sb, NEG)
            old = m_ref[...]
            high = jnp.maximum(
                jnp.max(sa, axis=1, keepdims=True), jnp.max(sb, axis=1, keepdims=True)
            )
            new = jnp.maximum(old, high)
            pa = jnp.exp2(sa - new[:, :1]).astype(bf16)
            pb = jnp.exp2(sb - new[:, :1]).astype(bf16)
            m_ref[...] = new
            acc_ref[...] = (
                acc_ref[...] * jnp.exp2(old - new)
                + dot_nn(pa, v_own[ks, :])
                + dot_nn(pb, v_oth[ks, :])
            )

        def k_step(j, _):
            tiles(visit, qlo, qhi, klo, khi, i, j, 1, sk)
            return 0

        lax.fori_loop(0, n // (sk * fk), k_step, 0)
        acc = acc_ref[...]
        turned = swapped(acc)
        left = left_lanes((fq, 128))
        o = jnp.where(left, acc / turned, 0.0)
        o_ref[qs, :] = o.astype(bf16)
        lse = m_ref[...] + jnp.log2(jnp.where(left, turned, acc))
        half = left_lanes((64, 128))
        for b in range(fq // ROWS):
            block = slice(b * ROWS, (b + 1) * ROWS)
            lse_ref[0:1, pl.ds(pl.multiple_of(i * fq + b * ROWS, ROWS), ROWS)] = lse[block].T[0:1]
            upper, lower = o[block][:64], swapped(o[block][64:])
            pack_ref[i * (fq // ROWS) + b] = jnp.where(half, upper, lower).astype(bf16)
        return 0

    lax.fori_loop(0, n // fq, q_step, 0)


def attn_fwd(fq, fk, sk, ranges, q, own, oth, seg):
    n = q.shape[0]
    return pl.pallas_call(
        functools.partial(fwd_kernel, fq, fk, sk),
        out_shape=(shape((n // ROWS, 64, 128), bf16), shape((n, 128), bf16), shape((1, n), f32)),
        grid=(1,),
        in_specs=[SMEM] * 4 + [whole(*a.shape) for a in (q, own, oth, seg)],
        out_specs=(whole(n // ROWS, 64, 128), whole(n, 128), whole(1, n)),
        scratch_shapes=[
            pltpu.VMEM((n, 128), bf16),
            pltpu.VMEM((n, 128), bf16),
            pltpu.VMEM((fq, 128), f32),
            pltpu.VMEM((fq, 128), f32),
            pltpu.VMEM((n, 128), f32),
        ],
        compiler_params=limits(24),
        cost_estimate=cost(22),
        name="attn_fwd",
    )(*ranges, q, own, oth, seg)


def bwd_kernel(fine, sq, sk, qlo, qhi, klo, khi, q_ref, own_ref, oth_ref, pack_ref, o_ref, lrow,
               seg_ref, dq_out, dk_own, dk_oth, do_ref, drow, dk_sum, dq_ref, sk_own, sk_oth):
    n = q_ref.shape[0]
    low = left_lanes((ROWS, 128))

    @pl.when((klo[0, 0] != khi[0, n // fine - 1]) | (klo[0, 0] != khi[1, n // fine - 1]))
    def _():
        columns(seg_ref, sk_own, 0)
        columns(seg_ref, sk_oth, 1)

    for b in range(n // ROWS):
        s = pl.ds(b * ROWS, ROWS)
        packed = pack_ref[b].astype(f32)
        do = jnp.where(low, jnp.concatenate([packed, swapped(packed)], axis=0), 0.0)
        do_ref[s, :] = do.astype(bf16)
        delta = jnp.sum(do * o_ref[s, :].astype(f32), axis=1, keepdims=True)
        drow[0:1, s] = jnp.broadcast_to(delta, (ROWS, 128)).T[0:1, :]
    dq_ref[...] = jnp.zeros_like(dq_ref)
    sides = ((1, oth_ref, dk_oth, sk_oth), (0, own_ref, dk_own, sk_own))
    for half, k_ref, dk_ref, sk_ref in sides:
        dk_sum[...] = jnp.zeros_like(dk_sum)

        def visit(i, j, wide, deep, masked, k_ref=k_ref, sk_ref=sk_ref):
            qs = pl.ds(pl.multiple_of(i * wide * fine, wide * fine), wide * fine)
            ks = pl.ds(pl.multiple_of(j * deep * fine, deep * fine), deep * fine)
            keys = k_ref[ks, :]
            q = q_ref[qs, :]
            do = do_ref[qs, :]
            s = dot_nt(keys, q)
            dp = dot_nt(keys, do)
            p = jnp.exp2(s - lrow[0:1, qs])
            if masked:
                p = jnp.where(sk_ref[ks, 0:1] == seg_ref[0:1, qs], p, 0.0)
            ds = (p * (dp - drow[0:1, qs])).astype(bf16)
            dk_sum[ks, :] += dot_nn(p.astype(bf16), do) + dot_nn(ds, q)
            dq_ref[:, qs] += dot_nn(keys.T, ds)

        def k_step(j, _, half=half, visit=visit):
            def q_step(i, _):
                tiles(visit, qlo, qhi, klo.at[half], khi.at[half], i, j, sq, sk)
                return 0

            lax.fori_loop(0, n // (sq * fine), q_step, 0)
            return 0

        lax.fori_loop(0, n // (sk * fine), k_step, 0)
        low = left_lanes((n, 128))
        dk_ref[...] = (dk_sum[...] * jnp.where(low, 1.0, 1.0 / LOG2E)).astype(dk_ref.dtype)
    dq_out[...] = (dq_ref[...].T * HDIM**-0.5).astype(bf16)


def attn_bwd(fine, sq, sk, ranges, q, own, oth, pack, o, lse, seg):
    n = q.shape[0]
    return pl.pallas_call(
        functools.partial(bwd_kernel, fine, sq, sk),
        grid=(1,),
        out_shape=(shape((n, 128), bf16), shape((n, 128), f32), shape((n, 128), bf16)),
        in_specs=[SMEM] * 4
        + [whole(*a.shape) for a in (q, own, oth, pack, o, lse, seg)],
        out_specs=(whole(n, 128), whole(n, 128), whole(n, 128)),
        scratch_shapes=[
            pltpu.VMEM((n, 128), bf16),
            pltpu.VMEM((8, n), f32),
            pltpu.VMEM((n, 128), f32),
            pltpu.VMEM((128, n), f32),
            pltpu.VMEM((n, 128), f32),
            pltpu.VMEM((n, 128), f32),
        ],
        compiler_params=limits(60),
        cost_estimate=cost(120),
        name="attn_bwd",
    )(*ranges, q, own, oth, pack, o, lse, seg)


def heads_kernel(w_ref, gains_ref, seg_ref, sent_ref, wqkv_ref):
    left = left_lanes((32, 128))
    row = lax.broadcasted_iota(jnp.int32, (32, 128), 0)
    seg = jnp.broadcast_to(seg_ref[...], (32, 128))
    high, rest = (seg >> 6).astype(f32), (seg & 63).astype(f32)
    misc = jnp.broadcast_to(gains_ref[...], (32, 128))
    for k, part in enumerate((high, swapped(high), rest, swapped(rest))):
        misc = jnp.where(row == k + 1, part, misc)
    for p in range(HEADS // 2):
        q, k, v = (
            w_ref[:, 1024 * i + 128 * p : 1024 * i + 128 * (p + 1)].astype(f32) for i in range(3)
        )
        even = jnp.where(left, v, swapped(q)).astype(bf16)
        odd = jnp.where(left, swapped(v), q).astype(bf16)
        even_k = jnp.where(left, misc, swapped(k)).astype(bf16)
        odd_k = jnp.where(left, misc, k).astype(bf16)
        for c in range(2):
            sent_ref[4 * p + c, :, :128] = even
            sent_ref[4 * p + c, :, 128:] = even_k
            sent_ref[4 * p + 2 + c, :, :128] = odd
            sent_ref[4 * p + 2 + c, :, 128:] = odd_k
        wqkv_ref[:, 256 * p : 256 * p + 128] = even
        wqkv_ref[:, 256 * p + 128 : 256 * (p + 1)] = odd
        wqkv_ref[:, 2048 + 128 * p : 2048 + 128 * (p + 1)] = k.astype(bf16)


def heads_out(w, gains, seg):
    return pl.pallas_call(
        heads_kernel,
        out_shape=(shape((32, 32, 256), bf16), shape((32, 3072), bf16)),
        in_specs=[VMEM] * 3,
        out_specs=(VMEM, VMEM),
        compiler_params=limits(16),
        cost_estimate=cost(1),
        name="heads_out",
    )(w, gains, seg)


def unit_places():
    spread, pick = np.zeros((4, SPAN, 8 * SLOT)), np.zeros((4, SLOT, BLOCK))
    for z in range(4):
        for r in range(FIRST[z + 1] - FIRST[z]):
            pick[z, r, FIRST[z] + r] = 1
            for i in range(8):
                spread[z, BLOCK * i + FIRST[z] + r, SLOT * i + r] = 1
    return jnp.asarray(spread, bf16), jnp.asarray(pick, bf16)


def bundle_kernel(plane_ref, in_ref, spread_ref, pick_ref, mlp_ref, out_ref, bundle_ref, held):
    spread = spread_ref[plane_ref[0]]
    for k in range(8):
        part = dot_nn(in_ref[:, SPAN * k : SPAN * (k + 1)], spread)
        held[:, 8 * SLOT * k : 8 * SLOT * (k + 1)] = part
    for j in range(6):
        bundle_ref[32 * j : 32 * (j + 1), :] = held[:, 256 * j : 256 * (j + 1)].astype(bf16)
    mlp = dot_nn(pick_ref[plane_ref[0]], mlp_ref[...])
    parts = [mlp[:, 256 * j : 256 * (j + 1)] for j in range(4)]
    bundle_ref[192:OUT_FIRST, :] = jnp.concatenate(parts).astype(bf16)
    for j in range(4):
        cols = slice(256 * j, 256 * (j + 1))
        bundle_ref[OUT_FIRST + 32 * j : OUT_FIRST + 32 * (j + 1), :] = out_ref[:, cols]


def bundle_out(plane, w_in, spread, pick, w_mlp, w_out):
    return pl.pallas_call(
        bundle_kernel,
        out_shape=shape((BUNDLE, 256), bf16),
        in_specs=[SMEM] + [VMEM] * 5,
        out_specs=VMEM,
        scratch_shapes=[pltpu.VMEM((32, 2 * WIDE), f32)],
        compiler_params=limits(16),
        cost_estimate=cost(1),
        name="bundle_out",
    )(plane, w_in, spread, pick, w_mlp, w_out)


def turns():
    inverse = THETA ** (-np.arange(0, HDIM, 2) / HDIM)
    sign = np.repeat([-1.0, 1.0, -1.0, 1.0], 32)
    both = []
    for scale in (64, 1):
        angle = np.tile(np.arange(64)[:, None] * scale * inverse[None], (1, 4))
        table = np.concatenate([np.cos(angle), np.sin(angle) * sign], axis=1).astype(np.float32)
        main = table.astype(jnp.bfloat16)
        both.append(np.concatenate([main, (table - main.astype(np.float32)).astype(jnp.bfloat16)]))
    return jnp.asarray(np.stack(both), bf16)


def fill_tables(core, seg_ref, turn_ref, cos_ref, sin_ref):
    code = lax.broadcasted_iota(jnp.int32, (ROWS, ROWS), 0) & 63
    lane = lax.broadcasted_iota(jnp.int32, (1, ROWS), 1)
    for b in range(seg_ref.shape[1] // ROWS):
        rows = slice(b * ROWS, (b + 1) * ROWS)
        place = (2 * b + core) * ROWS + lane - seg_ref[:, rows]
        high = dot_tn((code == (place >> 6)).astype(f32).astype(bf16), turn_ref[0])
        rest = dot_tn((code == (place & 63)).astype(f32).astype(bf16), turn_ref[1])
        cos_ref[rows, :] = high[:, :128] * rest[:, :128] - high[:, 128:] * rest[:, 128:]
        sin_ref[rows, :] = high[:, 128:] * rest[:, :128] + high[:, :128] * rest[:, 128:]


def qkv_kernel(sizes, *refs):
    place = refs[0]
    pieces = refs[1 : 1 + len(sizes)]
    gain_ref, w_ref, seg_ref, turn_ref, n_ref, q_ref, k_ref, cos_ref, sin_ref = refs[1 + len(sizes) :]
    fill_tables(place[32], seg_ref, turn_ref, cos_ref, sin_ref)
    gain = gain_ref[...]
    w = w_ref[...]
    group = 0
    for piece, size in zip(pieces, sizes):
        z, _ = norm_parts(piece[...].astype(f32))
        normed = (z * gain).astype(bf16)
        both = dot_nn(normed, w)
        for g in range(size // 64):
            to = pl.ds(pl.multiple_of(place[group] * 64, 64), 64)
            group += 1
            mine = slice(g * 64, (g + 1) * 64)
            cos, sin = cos_ref[to, :], sin_ref[to, :]
            lane = lax.broadcasted_iota(jnp.int32, (64, 128), 1)

            def turn(t):
                other = jnp.where(lane < 96, pltpu.roll(t, 96, 1), pltpu.roll(t, 32, 1))
                return t * cos + other * sin

            first, second = both[mine, :128], both[mine, 128:]
            q_ref[to, :] = jnp.where(lane < HDIM, 0.0, turn(first) * (LOG2E * HDIM**-0.5)).astype(bf16)
            n_ref[to, :] = normed[mine]
            k_ref[to, :] = jnp.where(lane < HDIM, first, turn(second)).astype(bf16)


def qkv(place, pieces, gain, w, seg):
    n, width = seg.shape[1], pieces[0].shape[1]
    sizes = tuple(p.shape[0] for p in pieces)
    return pl.pallas_call(
        functools.partial(qkv_kernel, sizes),
        out_shape=(shape((n, width), bf16), shape((n, 128), bf16), shape((n, 128), bf16)),
        in_specs=[SMEM] + [VMEM] * (len(pieces) + 4),
        out_specs=(VMEM, VMEM, VMEM),
        scratch_shapes=[pltpu.VMEM((n, 128), f32)] * 2,
        compiler_params=limits(24),
        cost_estimate=cost(6),
        name="qkv",
    )(place, *pieces, gain, w, seg, turns())


OUT_PARTS = [weight_part(32, OUT_FIRST + 32 * j) for j in range(4)]


def proj_kernel(pack_ref, x_ref, gain_ref, w0, w1, w2, w3, n_ref, h_ref, o_ref):
    for p in range(HEADS // 2):
        both = unpack_pair(pack_ref[2 * p].astype(f32), pack_ref[2 * p + 1].astype(f32))
        o_ref[:, p * 128 : (p + 1) * 128] = both.astype(bf16)
    o = o_ref[...]
    for j, w in enumerate((w0, w1, w2, w3)):
        cols = slice(256 * j, 256 * (j + 1))
        h_ref[:, cols] = x_ref[:, cols].astype(f32) + dot_nn(o, w[...].reshape(1024, 256))
    z, _ = norm_parts(h_ref[...])
    n_ref[...] = (z * gain_ref[...]).astype(bf16)


def proj(pack, x, gain, bundle):
    n, width = x.shape
    return pl.pallas_call(
        proj_kernel,
        grid=(1,),
        out_shape=(shape((n, width), bf16), shape((n, width), f32), shape((n, width), bf16)),
        in_specs=[whole(*pack.shape), whole(n, width), whole(1, width), *OUT_PARTS],
        out_specs=(whole(n, width), whole(n, width), whole(n, width)),
        compiler_params=limits(58),
        cost_estimate=cost(3),
        name="proj",
    )(pack, x, gain, bundle, bundle, bundle, bundle)


def normal_cdf(x, bell):
    t = 1.0 / (1.0 + (0.3275911 * 0.5**0.5) * jnp.abs(x))
    tail = 1.061405429
    for term in (-1.453152027, 1.421413741, -0.284496736, 0.254829592):
        tail = tail * t + term
    tail = 0.5 * tail * t * bell
    return jnp.where(x >= 0.0, 1.0 - tail, tail)


def units_kernel(*refs):
    n_refs, g_refs = refs[:4], refs[4:8]
    win_ref, m_ref = refs[8], refs[9]
    act_ref, dup_ref, n_all, g_all, w_ref = refs[10:15]
    d_refs, w_in = refs[15:19], refs[19]
    for i in range(4):
        n_all[i * ROWS : (i + 1) * ROWS, :] = n_refs[i][...]
        g_all[i * ROWS : (i + 1) * ROWS, :] = g_refs[i][...]
    normed = n_all[...]
    g = g_all[...]

    slots = m_ref[...].astype(f32)
    for a in range(4):
        part = slots[:, SLOT * a : SLOT * (a + 1)].reshape(WIDE, 256)
        w_ref[:, 256 * a : 256 * (a + 1)] = part.astype(bf16)
    for j in range(6):
        w_in[:, 256 * j : 256 * (j + 1)] = win_ref[:, 32 * j : 32 * (j + 1), :].reshape(1024, 256)

    for j in range(3):
        cols = slice(256 * j, 256 * (j + 1))
        more = slice(WIDE + 256 * j, WIDE + 256 * (j + 1))
        first = dot_nn(normed, w_in[:, cols])
        second = dot_nn(normed, w_in[:, more])
        d_act = dot_nt(g, w_ref[cols, :])
        bell = jnp.exp(-0.5 * first * first)
        cdf = normal_cdf(first, bell)
        slope = cdf + first * (bell * (1.0 / (2.0 * np.pi) ** 0.5))
        gated = first * cdf
        act_ref[:, cols] = (gated * second).astype(bf16)
        dup_ref[:, cols] = (d_act * second * slope).astype(bf16)
        dup_ref[:, more] = (d_act * gated).astype(bf16)
    total = dot_nt(dup_ref[...], w_in[...])
    for i in range(4):
        d_refs[i][...] = total[i * ROWS : (i + 1) * ROWS].astype(bf16)


def units(normed, cots, bundle):
    n, width = normed[0].shape
    tokens = 4 * n
    return pl.pallas_call(
        units_kernel,
        grid=(1,),
        out_shape=(
            shape((tokens, WIDE), bf16),
            shape((tokens, 2 * WIDE), bf16),
            shape((tokens, width), bf16),
            shape((tokens, width), bf16),
            shape((WIDE, width), bf16),
            *[shape((n, width), bf16)] * 4,
        ),
        in_specs=[whole(n, width)] * 8
        + [weight_part(192, 0), weight_part(4 * SLOT, 192)],
        out_specs=(
            whole(tokens, WIDE),
            whole(tokens, 2 * WIDE),
            whole(tokens, width),
            whole(tokens, width),
            whole(WIDE, width),
            *[whole(n, width)] * 4,
        ),
        scratch_shapes=[pltpu.VMEM((width, 2 * WIDE), bf16)],
        compiler_params=limits(58),
        cost_estimate=cost(11),
        name="units",
    )(*normed, *cots, bundle, bundle)


def unit_grads_kernel(act_ref, dup_ref, n_all, g_all, out_hbm, out_ref, sem):
    act = act_ref[...].T
    grads = [dot_nn(act, g_all[:, 256 * a : 256 * (a + 1)]) for a in range(4)]
    for b in range(32):
        slot = jnp.concatenate([grad[SLOT * b : SLOT * (b + 1)] for grad in grads])
        out_ref[(b % 8) * 4 + b // 8, 192:OUT_FIRST, :] = slot.astype(bf16)
    normed = n_all[...].T
    for j in range(6):
        grad = dot_nn(normed, dup_ref[:, 256 * j : 256 * (j + 1)]).astype(bf16)
        for b in range(32):
            out_ref[(b % 8) * 4 + b // 8, 32 * j : 32 * (j + 1), :] = grad[32 * b : 32 * (b + 1)]
    copy = pltpu.make_async_copy(out_ref, out_hbm.at[:, pl.ds(0, OUT_FIRST)], sem)
    copy.start()
    copy.wait()


def unit_grads(act, dup, n_all, g_all):
    tokens, width = n_all.shape
    return pl.pallas_call(
        unit_grads_kernel,
        out_shape=shape((32, BUNDLE, 256), bf16),
        grid=(1,),
        in_specs=[whole(*a.shape) for a in (act, dup, n_all, g_all)],
        out_specs=HBM,
        scratch_shapes=[pltpu.VMEM((32, OUT_FIRST, 256), bf16), pltpu.SemaphoreType.DMA],
        compiler_params=limits(60),
        cost_estimate=cost(2),
        name="unit_grads",
    )(act, dup, n_all, g_all)


def out_grad_kernel(o_ref, da_ref, in_hbm, out_hbm, out_ref, sem):
    del in_hbm
    grad = dot_tn(o_ref[...], da_ref[...]).astype(bf16)
    for b in range(32):
        for j in range(4):
            out_ref[(b % 8) * 4 + b // 8, 32 * j : 32 * (j + 1), :] = grad[
                32 * b : 32 * (b + 1), 256 * j : 256 * (j + 1)
            ]
    copy = pltpu.make_async_copy(out_ref, out_hbm.at[:, pl.ds(OUT_FIRST, 128)], sem)
    copy.start()
    copy.wait()


def out_grad(o, da, grads):
    return pl.pallas_call(
        out_grad_kernel,
        out_shape=shape(grads.shape, bf16),
        grid=(1,),
        in_specs=[whole(*o.shape), whole(*da.shape), HBM],
        out_specs=HBM,
        scratch_shapes=[pltpu.VMEM((32, 128, 256), bf16), pltpu.SemaphoreType.DMA],
        input_output_aliases={2: 0},
        compiler_params=limits(60),
        cost_estimate=cost(1),
        name="out_grad",
    )(o, da, grads)


def unit_out_kernel(act_ref, w_ref, p0, p1, p2, p3):
    act = act_ref[...]
    for a in range(4):
        cols = slice(256 * a, 256 * (a + 1))
        part = dot_nn(act, w_ref[:, cols]).astype(bf16)
        for i, p in enumerate((p0, p1, p2, p3)):
            p[:, cols] = part[i * ROWS : (i + 1) * ROWS]


def unit_out(act, w):
    return pl.pallas_call(
        unit_out_kernel,
        grid=(1,),
        out_shape=[shape((ROWS, 1024), bf16)] * 4,
        in_specs=[whole(*act.shape), whole(*w.shape)],
        out_specs=[whole(ROWS, 1024)] * 4,
        compiler_params=limits(60),
        cost_estimate=cost(0.5),
        name="unit_out",
    )(act, w)


def proj_back_kernel(d0, d1, d2, d3, h_ref, gain_ref, cot_ref, w0, w1, w2, w3,
                     pack_ref, dh_ref, da_ref):
    total = d0[...].astype(f32) + d1[...].astype(f32) + d2[...].astype(f32) + d3[...].astype(f32)
    z, scale = norm_parts(h_ref[...])
    dh = cot_ref[...].astype(f32) + norm_back(total * gain_ref[...], z, scale)
    dh_ref[...] = dh
    da_ref[...] = dh.astype(bf16)
    do = sum(
        dot_nt(da_ref[:, 256 * j : 256 * (j + 1)], w[...].reshape(1024, 256))
        for j, w in enumerate((w0, w1, w2, w3))
    )
    for p in range(HEADS // 2):
        even, odd = pack_pair(do[:, p * 128 : (p + 1) * 128])
        pack_ref[2 * p] = even.astype(bf16)
        pack_ref[2 * p + 1] = odd.astype(bf16)


def proj_back(ds, h, gain, cot, bundle):
    n, width = h.shape
    return pl.pallas_call(
        proj_back_kernel,
        grid=(1,),
        out_shape=(shape((HEADS, 64, 128), bf16), shape((n, width), f32), shape((n, width), bf16)),
        in_specs=[whole(n, width)] * 5 + [whole(1, width), whole(n, width), *OUT_PARTS],
        out_specs=(whole(HEADS, 64, 128), whole(n, width), whole(n, width)),
        compiler_params=limits(58),
        cost_estimate=cost(3),
        name="proj_back",
    )(*ds, h, gain, cot, bundle, bundle, bundle, bundle)


def turn_back_kernel(core_ref, dq_ref, own_ref, oth_ref, seg_ref, turn_ref, n_ref,
                     sent_ref, keep_ref, give_ref, d_ref, grad_ref, held, cos_ref, sin_ref, sem):
    fetch = pltpu.make_async_copy(n_ref, held, sem)
    fetch.start()
    fill_tables(core_ref[0], seg_ref, turn_ref, cos_ref, sin_ref)
    for b in range(dq_ref.shape[0] // ROWS):
        s = slice(b * ROWS, (b + 1) * ROWS)
        cos, sin = cos_ref[s, :], sin_ref[s, :]
        lane = lax.broadcasted_iota(jnp.int32, (ROWS, 128), 1)

        def turn(t):
            other = jnp.where(lane < 96, pltpu.roll(t, 96, 1), pltpu.roll(t, 32, 1))
            return t * cos - other * sin

        dk = own_ref[s, :] + oth_ref[s, :].astype(f32)
        first = jnp.where(lane < HDIM, dk, turn(dq_ref[s, :].astype(f32)))
        second = jnp.where(lane < HDIM, 0.0, turn(dk))
        d_ref[s, :128] = first.astype(bf16)
        d_ref[s, 128:] = second.astype(bf16)
        sent_ref[b, :ROWS, :] = first.astype(bf16)
        packed = jnp.where(left_lanes((64, 128)), swapped(second[:64]), second[64:])
        sent_ref[b, ROWS:192, :] = packed.astype(bf16)
    fetch.wait()
    grad = dot_tn(d_ref[...], held[...]).T
    grad_ref[...] = grad.reshape(grad_ref.shape)
    core = core_ref[0]
    for h in range(HEADS):
        keep_ref[h] = grad_ref[2 * h + core]
        give_ref[h] = grad_ref[2 * h + 1 - core].astype(bf16)


def turn_back(core, dq, own, oth, seg, normed):
    n = dq.shape[0]
    return pl.pallas_call(
        turn_back_kernel,
        out_shape=(
            shape((HEADS, 192, 128), bf16),
            shape((HEADS, 32, 256), f32),
            shape((HEADS, 32, 256), bf16),
        ),
        grid=(1,),
        in_specs=[SMEM]
        + [whole(*a.shape) for a in (dq, own, oth, seg)]
        + [whole(2, ROWS, 256), HBM],
        out_specs=(whole(HEADS, 192, 128), whole(HEADS, 32, 256), whole(HEADS, 32, 256)),
        scratch_shapes=[
            pltpu.VMEM((n, 256), bf16),
            pltpu.VMEM((32, 32, 256), f32),
            pltpu.VMEM(normed.shape, bf16),
            pltpu.VMEM((n, 128), f32),
            pltpu.VMEM((n, 128), f32),
            pltpu.SemaphoreType.DMA,
        ],
        compiler_params=limits(60),
        cost_estimate=cost(5),
        name="turn_back",
    )(core, dq, own, oth, seg, turns(), normed)


def pack_kernel(keep_ref, took_ref, out_ref):
    left = left_lanes((16, 128))
    for h in range(HEADS):
        both = keep_ref[h] + took_ref[h].astype(f32)
        k = both[:, 128:]
        out_ref[h, :32, :] = both[:, :128].astype(bf16)
        out_ref[h, 32:, :] = jnp.where(left, swapped(k[:16]), k[16:]).astype(bf16)


def pack_head(keep, took):
    return pl.pallas_call(
        pack_kernel,
        grid=(1,),
        out_shape=shape((HEADS, 48, 128), bf16),
        in_specs=[whole(*keep.shape), whole(*took.shape)],
        out_specs=whole(HEADS, 48, 128),
        compiler_params=limits(58),
        cost_estimate=cost(1),
        name="pack_head",
    )(keep, took)


def input_kernel(got_ref, w_ref, x_ref, gain_ref, dh_ref, out_ref, d_ref, acc_ref):
    step = pl.program_id(0)

    @pl.when(step == 0)
    def _():
        for h in range(HEADS):
            d_ref[h // 4, :, 128 * (h % 4) : 128 * (h % 4 + 1)] = got_ref[h, :ROWS, :]
        for p in range(HEADS // 2):
            both = unpack_pair(
                got_ref[2 * p, ROWS:192, :].astype(f32), got_ref[2 * p + 1, ROWS:192, :].astype(f32)
            )
            d_ref[4 + p // 4, :, 128 * (p % 4) : 128 * (p % 4 + 1)] = both.astype(bf16)
        acc_ref[...] = jnp.zeros_like(acc_ref)

    acc_ref[...] += dot_nt(d_ref[step], w_ref[...])

    @pl.when(step == pl.num_programs(0) - 1)
    def _():
        z, scale = norm_parts(x_ref[...].astype(f32))
        back = norm_back(acc_ref[...] * gain_ref[...], z, scale)
        out_ref[...] = (dh_ref[...] + back).astype(bf16)


def input_back(got, w, x, gain, dh):
    n, width = x.shape
    return pl.pallas_call(
        input_kernel,
        grid=(6,),
        out_shape=shape((n, width), bf16),
        in_specs=[
            whole(*got.shape),
            pl.BlockSpec((width, 512), lambda i: (0, i)),
            whole(n, width),
            whole(1, width),
            whole(n, width),
        ],
        out_specs=whole(n, width),
        scratch_shapes=[pltpu.VMEM((6, n, 512), bf16), pltpu.VMEM((n, width), f32)],
        compiler_params=limits(32),
        cost_estimate=cost(4),
        name="input_back",
    )(got, w, x, gain, dh)


def rows_kernel(got_ref, out_ref):
    left = left_lanes((32, 128))
    half = left_lanes((16, 128))
    for p in range(HEADS // 2):
        even, odd = (got_ref[2 * p + i, :32, :].astype(f32) for i in range(2))
        even_k, odd_k = (got_ref[2 * p + i, 32:, :].astype(f32) for i in range(2))
        q = jnp.where(left, swapped(even), odd)
        v = jnp.where(left, even, swapped(odd))
        k = jnp.concatenate(
            [jnp.where(half, even_k, swapped(odd_k)), jnp.where(half, swapped(even_k), odd_k)]
        )
        for i, part in enumerate((q, k, v)):
            j = 8 * i + p
            out_ref[32 * (j // 2) : 32 * (j // 2 + 1), 128 * (j % 2) : 128 * (j % 2 + 1)] = part.astype(bf16)


def gather_rows(got):
    return pl.pallas_call(
        rows_kernel,
        out_shape=shape((384, 256), bf16),
        in_specs=[VMEM],
        out_specs=VMEM,
        compiler_params=limits(16),
        cost_estimate=cost(1),
        name="gather_rows",
    )(got)


def as_row(column):
    full = jnp.concatenate([column, jnp.zeros((ROWS - 32, 1), f32)])
    return jnp.broadcast_to(full, (ROWS, ROWS)).T[0:1]


def planes_kernel(plane_ref, h0, h1, h2, h3, r0, r1, r2, r3, spread_ref, pick_ref, wqkv_ref, win_ref, g1_ref, g2_ref,
                  qkv_ref, out_ref, in_ref, mlp_ref, norm1_ref, norm2_ref, held):
    pieces = (r0, r1, r2, r3)
    planes = [plane_ref[k] for k in range(4)]

    def total(refs, first):
        return sum(r[first : first + 32, :].astype(f32) for r in refs)

    norm = jnp.zeros((32, 1), f32)
    for j in range(12):
        cols = slice(256 * j, 256 * (j + 1))
        part = total((h0, h1, h2, h3), 32 * j)
        qkv_ref[:, cols] = part
        norm += jnp.sum(part * wqkv_ref[:, cols].astype(f32), axis=1, keepdims=True)
    norm1_ref[...] = as_row(norm / g1_ref[...])
    all_slots = [r[192:OUT_FIRST, :].astype(f32) for r in pieces]
    for j in range(4):
        cols = slice(256 * j, 256 * (j + 1))
        out_ref[:, cols] = total(pieces, OUT_FIRST + 32 * j)
        slot = slice(SLOT * j, SLOT * (j + 1))
        mlp_ref[:, cols] = sum(
            dot_tn(pick_ref[z], slots[slot].astype(bf16)) for z, slots in zip(planes, all_slots)
        )
    grads = jnp.zeros((256, SPAN), f32)
    for z, r in zip(planes, pieces):
        wide = jnp.concatenate([r[32 * j : 32 * (j + 1), :] for j in range(6)], axis=1)
        for k in range(8):
            held[32 * k : 32 * (k + 1), :] = wide[:, 8 * SLOT * k : 8 * SLOT * (k + 1)]
        grads += dot_nt(held[...], spread_ref[z])
    norm = jnp.zeros((32, 1), f32)
    for k in range(8):
        cols = slice(SPAN * k, SPAN * (k + 1))
        part = grads[32 * k : 32 * (k + 1)]
        in_ref[:, cols] = part
        norm += jnp.sum(part * win_ref[:, cols].astype(f32), axis=1, keepdims=True)
    norm2_ref[...] = as_row(norm / g2_ref[...])


def add_planes(plane, heads, parts, spread, pick, wqkv, win, gain_one, gain_two):
    return pl.pallas_call(
        planes_kernel,
        out_shape=(
            shape(wqkv.shape, f32),
            shape((32, 1024), f32),
            shape(win.shape, f32),
            shape((BLOCK, 1024), f32),
            shape((1, ROWS), f32),
            shape((1, ROWS), f32),
        ),
        in_specs=[SMEM] + [VMEM] * 14,
        out_specs=(VMEM,) * 6,
        scratch_shapes=[pltpu.VMEM((256, 8 * SLOT), bf16)],
        compiler_params=limits(24),
        cost_estimate=cost(5),
        name="add_planes",
    )(plane, *heads, *parts, spread, pick, wqkv, win, gain_one, gain_two)


def shift(value, axis, steps):
    count = lax.axis_size(axis)
    return lax.ppermute(value, axis, [(i, (i + steps) % count) for i in range(count)])


def both_ways(value, axis):
    first = [(2 * i + c, (2 * i + 2 - 4 * c) % 8 + c) for i in range(4) for c in range(2)]
    other = [(b, a) for a, b in first]
    near = lax.ppermute(value, (axis, "c"), first)
    return [value, near, lax.ppermute(value, (axis, "c"), other), lax.ppermute(near, (axis, "c"), first)]


def from_planes(value):
    return [value] + [shift(value, "z", k) for k in SHIFTS[1:]]


def back_to_planes(pieces):
    return [pieces[0]] + [shift(p, "z", -k) for p, k in zip(pieces[1:], SHIFTS[1:])]


def far(value, near, axis):
    half = value.shape[0] // 2
    behind, ahead = near
    return [value, behind, ahead, shift(behind[:half], axis, 1), shift(ahead[half:], axis, 3)]


def exchange(value, axes):
    return lax.all_to_all(value, axes, split_axis=0, concat_axis=0, tiled=True)


def shards(hidden_in, seg_start, norm1_gain, qkv_weight, out_weight, norm2_gain, in_weight,
           mlp_weight, out_cotangent):
    plane, core = lax.axis_index("z"), lax.axis_index("c")
    mine = (lax.axis_index("x"), lax.axis_index("y"))
    plane_id, core_id = plane.astype(jnp.int32)[None], core.astype(jnp.int32)[None]
    x_own = hidden_in[0]
    cot = out_cotangent[0]
    width = x_own.shape[1]
    rows = qkv_weight.shape[0]

    upper, lower = x_own[:64], x_own[64:]
    upper = [upper] + [shift(upper, "x", k) for k in SHIFTS[1:]]
    lower = [lower] + [shift(lower, "y", k) for k in SHIFTS[1:]]
    upper, lower = jnp.concatenate(upper), jnp.concatenate(lower)

    gains = jnp.pad(jnp.concatenate([norm1_gain, norm2_gain]), (0, HDIM)).astype(f32)[None]
    sent, wqkv = heads_out(qkv_weight, gains, seg_start)
    spread, pick = unit_places()
    bundle = bundle_out(plane_id, in_weight, spread, pick, mlp_weight, out_weight)
    upper, lower, sent = lax.optimization_barrier((upper, lower, sent))
    got = exchange(sent, XYC)
    pieces = both_ways(upper, "y") + both_ways(lower, "x")
    steps = (0, 1 - 2 * core, 2 * core - 1, 2)
    place = []
    for half in (0, 1):
        for outer in steps:
            for inner in SHIFTS:
                sx, sy = (inner, outer) if half == 0 else (outer, inner)
                place.append((((mine[0] - sx) % 4) * 4 + (mine[1] - sy) % 4) * 2 + half)
    place = jnp.stack([*place, core]).astype(jnp.int32)
    w_head = got.reshape(width, 256)
    gain_one = got[:, 0, 128:160].reshape(1, width).astype(f32)
    gain_two = got[:, 0, 160:192].reshape(1, width).astype(f32)
    high, rest = got[:, 1:3, 128:192].astype(jnp.int32), got[:, 3:5, 128:192].astype(jnp.int32)
    seg_all = (high * 64 + rest).reshape(HEADS, 2, ROWS)
    seg_own = jnp.where(core == 0, seg_all[:, 0], seg_all[:, 1]).reshape(-1)
    seg_oth = jnp.where(core == 0, seg_all[:, 1], seg_all[:, 0]).reshape(-1)
    pieces, seg_own, seg_oth, gain_one, gain_two, bundle = lax.optimization_barrier(
        (pieces, seg_own, seg_oth, gain_one, gain_two, bundle)
    )
    bundle = lax.all_gather(bundle, XYC, axis=0, tiled=False)


    normed_one, queries, keys = qkv(place, pieces, gain_one, w_head, seg_own[None])
    keys_oth = shift(keys, "c", 1)

    def bounds(seg, size):
        tiles = seg.reshape(-1, size)
        return tiles[:, 0], tiles[:, -1]

    (qlo, qhi), (olo, ohi), (tlo, thi) = bounds(seg_own, 256), bounds(seg_own, 1024), bounds(seg_oth, 1024)
    both_segs = jnp.stack([seg_own, seg_oth]).astype(f32)
    o_pack, o, lse = attn_fwd(
        256, 1024, 2, (qlo, qhi, jnp.minimum(olo, tlo), jnp.maximum(ohi, thi)),
        queries, keys, keys_oth, both_segs,
    )
    o_pack, cot = lax.optimization_barrier((o_pack, cot))
    cots = from_planes(cot)
    o_got = exchange(o_pack, XY)
    wqkv, o_got, cots = lax.optimization_barrier((wqkv, o_got, cots))
    wqkv = lax.all_gather(wqkv, XYC, axis=0, tiled=True)

    normed_two, middle, o_tok = proj(o_got, x_own, gain_two, bundle)
    act, dup, n_all, g_all, w_units, *d_parts = units(from_planes(normed_two), cots, bundle)
    d_parts = back_to_planes(d_parts)
    g_sum = unit_grads(act, dup, n_all, g_all)
    d_parts, g_sum = lax.optimization_barrier((d_parts, g_sum))
    do_pack, d_mid, d_attn = proj_back(d_parts, middle, gain_two, cot, bundle)
    do_got = exchange(do_pack, XY)
    act, d_attn = lax.optimization_barrier((act, d_attn))
    g_sum = out_grad(o_tok, d_attn, g_sum)
    out_parts = unit_out(act, w_units)
    do_got, out_parts = lax.optimization_barrier((do_got, out_parts))
    g_sum, wqkv = lax.optimization_barrier((g_sum, wqkv))
    g_sum = lax.psum_scatter(g_sum.reshape(8, 4 * BUNDLE, 256), YC, scatter_dimension=0, tiled=False)

    (qlo, qhi), (tlo, thi) = bounds(seg_own, 512), bounds(seg_oth, 512)
    ranges = (qlo, qhi, jnp.stack([qlo, tlo]), jnp.stack([qhi, thi]))
    dq, dk_own, dk_oth = attn_bwd(512, 4, 2, ranges, queries, keys, keys_oth, do_got, o, lse, both_segs)
    dk_oth, out_parts = lax.optimization_barrier((dk_oth, out_parts))
    out_parts = back_to_planes(out_parts)
    d_sent, keep, give = turn_back(core_id, dq, dk_own, shift(dk_oth, "c", 1), seg_own[None], normed_one)

    give, out_parts = lax.optimization_barrier((give, out_parts))
    g_head = pack_head(keep, shift(give, "c", 1))
    g_head, g_sum = lax.optimization_barrier((g_head, g_sum))
    g_head = exchange(g_head, XY)
    g_sum = lax.psum_scatter(g_sum.reshape(4, BUNDLE, 256), "x", scatter_dimension=0, tiled=False)
    g_head, d_sent = lax.optimization_barrier((g_head, d_sent))
    d_got = exchange(d_sent, XY)
    heads = gather_rows(g_head)

    heads, g_rows = from_planes(heads), from_planes(g_sum)
    input_grad = input_back(d_got, wqkv, x_own, gain_one, d_mid)
    hidden_out = (middle + sum(p.astype(f32) for p in out_parts)).astype(bf16)
    heads, g_rows, input_grad, hidden_out = lax.optimization_barrier(
        (heads, g_rows, input_grad, hidden_out)
    )
    g_qkv, g_out, g_in, g_mlp, grad_one, grad_two = add_planes(
        jnp.stack([(plane - k) % 4 for k in SHIFTS]).astype(jnp.int32), heads, g_rows, spread, pick,
        qkv_weight, in_weight,
        norm1_gain.astype(f32)[:, None], norm2_gain.astype(f32)[:, None],
    )
    return (
        hidden_out[None],
        input_grad[None],
        g_qkv,
        g_out,
        g_in,
        g_mlp,
        grad_one[0, :32],
        grad_two[0, :32],
    )


def solution(mesh):
    fine = Mesh(mesh.devices.reshape(4, 4, 4, 2), ("z", "x", "y", "c"))
    blk = ("x", "y", "c")
    return jax.shard_map(
        shards,
        mesh=fine,
        in_specs=(
            P("z", blk, None),
            P("z", blk),
            P(blk),
            P(blk, None),
            P(blk, None),
            P(blk),
            P(blk, None),
            P(blk, None),
            P("z", blk, None),
        ),
        out_specs=(
            P("z", blk, None),
            P("z", blk, None),
            P(blk, None),
            P(blk, None),
            P(blk, None),
            P(blk, None),
            P(blk),
            P(blk),
        ),
        check_vma=False,
    )
```

```python
import functools

import jax
import jax.numpy as jnp
import numpy as np
from jax import lax
from jax.experimental import pallas as pl
from jax.experimental.pallas import tpu as pltpu
from jax.sharding import Mesh
from jax.sharding import PartitionSpec as P

HEADS = 16
HDIM = 64
EPS = 1e-05
THETA = 160000.0
NEG = -1e30
FLOOR = -1e29
ROWS = 128
BLOCK = 82
FIRST = (0, 21, 42, 62, 82)
SLOT = 24
WIDE = 32 * SLOT
SPAN = 8 * BLOCK
OUT_FIRST = 288
BUNDLE = 416
LOG2E = 1.4426950408889634
bf16 = jnp.bfloat16
f32 = jnp.float32
XY = ("x", "y")
YC = ("y", "c")
XYC = ("x", "y", "c")
SMEM = pl.BlockSpec(memory_space=pltpu.SMEM)
VMEM = pl.BlockSpec(memory_space=pltpu.VMEM)
HBM = pl.BlockSpec(memory_space=pltpu.HBM)
SHIFTS = (0, 1, 3, 2)


def dot_nn(a, b):
    return lax.dot_general(a, b, (((1,), (0,)), ((), ())), preferred_element_type=f32)


def dot_nt(a, b):
    return lax.dot_general(a, b, (((1,), (1,)), ((), ())), preferred_element_type=f32)


def dot_tn(a, b):
    return lax.dot_general(a, b, (((0,), (0,)), ((), ())), preferred_element_type=f32)


def shape(dims, dtype):
    return jax.ShapeDtypeStruct(dims, dtype)


def limits(mib):
    return pltpu.CompilerParams(vmem_limit_bytes=mib << 20)


def cost(us):
    return pl.CostEstimate(flops=int(us * 1.1e9), bytes_accessed=int(us * 3.4e6), transcendentals=0)


def weight_part(rows, first, blocks=32):
    return pl.BlockSpec((blocks, rows, 256), lambda i: (0, first // rows, 0))


def whole(*dims):
    return pl.BlockSpec(dims, lambda i: (0,) * len(dims))


def left_lanes(dims):
    return lax.broadcasted_iota(jnp.int32, dims, len(dims) - 1) < HDIM


def swapped(v):
    return pltpu.roll(v, HDIM, 1)


def norm_parts(values):
    mid = values - jnp.mean(values, axis=-1, keepdims=True)
    scale = lax.rsqrt(jnp.mean(mid * mid, axis=-1, keepdims=True) + EPS)
    return mid * scale, scale


def norm_back(e, z, scale):
    return (
        e - jnp.mean(e, axis=-1, keepdims=True) - z * jnp.mean(e * z, axis=-1, keepdims=True)
    ) * scale


def unpack_pair(even, odd):
    left = left_lanes(even.shape)
    top = jnp.where(left, even, swapped(odd))
    bottom = jnp.where(left, swapped(even), odd)
    return jnp.concatenate([top, bottom], axis=0)


def pack_pair(rows):
    top, bottom = rows[:64], rows[64:]
    left = left_lanes(top.shape)
    return jnp.where(left, top, swapped(bottom)), jnp.where(left, swapped(top), bottom)


def columns(rows_ref, cols_ref, k):
    for b in range(rows_ref.shape[1] // ROWS):
        s = pl.ds(b * ROWS, ROWS)
        cols_ref[s, :] = jnp.broadcast_to(rows_ref[k : k + 1, s], (ROWS, ROWS)).T


def tiles(visit, qlo, qhi, klo, khi, i, j, sq, sk):
    def check(q0, q1, k0, k1, rows, cols, wide, deep, parts):
        a, b, c, d = qlo[q0], qhi[q1], klo[k0], khi[k1]
        plain = (a == b) & (c == d) & (a == c)
        mixed = (a <= d) & (c <= b) & jnp.logical_not(plain)
        pl.when(plain)(lambda: visit(rows, cols, wide, deep, False))
        pl.when(mixed)(parts)

    def fine(t, _):
        fi, fj = i * sq + t // sk, j * sk + t % sk
        check(fi, fi, fj, fj, fi, fj, 1, 1, lambda: visit(fi, fj, 1, 1, True))
        return 0

    def all_fine():
        lax.fori_loop(0, sq * sk, fine, 0)

    check(i * sq, i * sq + sq - 1, j * sk, j * sk + sk - 1, i, j, sq, sk, all_fine)


def fwd_kernel(fq, fk, sk, qlo, qhi, klo, khi, q_ref, own_ref, oth_ref, seg_ref,
               pack_ref, o_ref, lse_ref, v_own, v_oth, m_ref, acc_ref, sq_ref):
    n = q_ref.shape[0]
    low = left_lanes((n, 128))
    v_own[...] = jnp.where(low, own_ref[...], jnp.ones((), bf16))
    v_oth[...] = jnp.where(low, oth_ref[...], jnp.ones((), bf16))
    pl.when(klo[0] != khi[n // fk - 1])(lambda: columns(seg_ref, sq_ref, 0))

    def q_step(i, _):
        qs = pl.ds(pl.multiple_of(i * fq, fq), fq)
        m_ref[...] = jnp.full_like(m_ref, FLOOR)
        acc_ref[...] = jnp.zeros_like(acc_ref)

        def visit(i, j, wide, deep, masked):
            ks = pl.ds(pl.multiple_of(j * deep * fk, deep * fk), deep * fk)
            q = q_ref[qs, :]
            sa = dot_nt(q, own_ref[ks, :])
            sb = dot_nt(q, oth_ref[ks, :])
            if masked:
                seg = sq_ref[qs, 0:1]
                sa = jnp.where(seg == seg_ref[0:1, ks], sa, NEG)
                sb = jnp.where(seg == seg_ref[1:2, ks], sb, NEG)
            old = m_ref[...]
            high = jnp.maximum(
                jnp.max(sa, axis=1, keepdims=True), jnp.max(sb, axis=1, keepdims=True)
            )
            new = jnp.maximum(old, high)
            pa = jnp.exp2(sa - new[:, :1]).astype(bf16)
            pb = jnp.exp2(sb - new[:, :1]).astype(bf16)
            m_ref[...] = new
            acc_ref[...] = (
                acc_ref[...] * jnp.exp2(old - new)
                + dot_nn(pa, v_own[ks, :])
                + dot_nn(pb, v_oth[ks, :])
            )

        def k_step(j, _):
            tiles(visit, qlo, qhi, klo, khi, i, j, 1, sk)
            return 0

        lax.fori_loop(0, n // (sk * fk), k_step, 0)
        acc = acc_ref[...]
        turned = swapped(acc)
        left = left_lanes((fq, 128))
        o = jnp.where(left, acc / turned, 0.0)
        o_ref[qs, :] = o.astype(bf16)
        lse = m_ref[...] + jnp.log2(jnp.where(left, turned, acc))
        half = left_lanes((64, 128))
        for b in range(fq // ROWS):
            block = slice(b * ROWS, (b + 1) * ROWS)
            lse_ref[0:1, pl.ds(pl.multiple_of(i * fq + b * ROWS, ROWS), ROWS)] = lse[block].T[0:1]
            upper, lower = o[block][:64], swapped(o[block][64:])
            pack_ref[i * (fq // ROWS) + b] = jnp.where(half, upper, lower).astype(bf16)
        return 0

    lax.fori_loop(0, n // fq, q_step, 0)


def attn_fwd(fq, fk, sk, ranges, q, own, oth, seg):
    n = q.shape[0]
    return pl.pallas_call(
        functools.partial(fwd_kernel, fq, fk, sk),
        out_shape=(shape((n // ROWS, 64, 128), bf16), shape((n, 128), bf16), shape((1, n), f32)),
        grid=(1,),
        in_specs=[SMEM] * 4 + [whole(*a.shape) for a in (q, own, oth, seg)],
        out_specs=(whole(n // ROWS, 64, 128), whole(n, 128), whole(1, n)),
        scratch_shapes=[
            pltpu.VMEM((n, 128), bf16),
            pltpu.VMEM((n, 128), bf16),
            pltpu.VMEM((fq, 128), f32),
            pltpu.VMEM((fq, 128), f32),
            pltpu.VMEM((n, 128), f32),
        ],
        compiler_params=limits(24),
        cost_estimate=cost(22),
        name="attn_fwd",
    )(*ranges, q, own, oth, seg)


def bwd_kernel(fine, sq, sk, qlo, qhi, klo, khi, q_ref, own_ref, oth_ref, pack_ref, o_ref, lrow,
               seg_ref, dq_out, dk_own, dk_oth, do_ref, drow, dk_sum, dq_ref, sk_own, sk_oth):
    n = q_ref.shape[0]
    low = left_lanes((ROWS, 128))

    @pl.when((klo[0, 0] != khi[0, n // fine - 1]) | (klo[0, 0] != khi[1, n // fine - 1]))
    def _():
        columns(seg_ref, sk_own, 0)
        columns(seg_ref, sk_oth, 1)

    for b in range(n // ROWS):
        s = pl.ds(b * ROWS, ROWS)
        packed = pack_ref[b].astype(f32)
        do = jnp.where(low, jnp.concatenate([packed, swapped(packed)], axis=0), 0.0)
        do_ref[s, :] = do.astype(bf16)
        delta = jnp.sum(do * o_ref[s, :].astype(f32), axis=1, keepdims=True)
        drow[0:1, s] = jnp.broadcast_to(delta, (ROWS, 128)).T[0:1, :]
    dq_ref[...] = jnp.zeros_like(dq_ref)
    sides = ((1, oth_ref, dk_oth, sk_oth), (0, own_ref, dk_own, sk_own))
    for half, k_ref, dk_ref, sk_ref in sides:
        dk_sum[...] = jnp.zeros_like(dk_sum)

        def visit(i, j, wide, deep, masked, k_ref=k_ref, sk_ref=sk_ref):
            qs = pl.ds(pl.multiple_of(i * wide * fine, wide * fine), wide * fine)
            ks = pl.ds(pl.multiple_of(j * deep * fine, deep * fine), deep * fine)
            keys = k_ref[ks, :]
            q = q_ref[qs, :]
            do = do_ref[qs, :]
            s = dot_nt(keys, q)
            dp = dot_nt(keys, do)
            p = jnp.exp2(s - lrow[0:1, qs])
            if masked:
                p = jnp.where(sk_ref[ks, 0:1] == seg_ref[0:1, qs], p, 0.0)
            ds = (p * (dp - drow[0:1, qs])).astype(bf16)
            dk_sum[ks, :] += dot_nn(p.astype(bf16), do) + dot_nn(ds, q)
            dq_ref[:, qs] += dot_nn(keys.T, ds)

        def k_step(j, _, half=half, visit=visit):
            def q_step(i, _):
                tiles(visit, qlo, qhi, klo.at[half], khi.at[half], i, j, sq, sk)
                return 0

            lax.fori_loop(0, n // (sq * fine), q_step, 0)
            return 0

        lax.fori_loop(0, n // (sk * fine), k_step, 0)
        low = left_lanes((n, 128))
        dk_ref[...] = (dk_sum[...] * jnp.where(low, 1.0, 1.0 / LOG2E)).astype(dk_ref.dtype)
    dq_out[...] = (dq_ref[...].T * HDIM**-0.5).astype(bf16)


def attn_bwd(fine, sq, sk, ranges, q, own, oth, pack, o, lse, seg):
    n = q.shape[0]
    return pl.pallas_call(
        functools.partial(bwd_kernel, fine, sq, sk),
        grid=(1,),
        out_shape=(shape((n, 128), bf16), shape((n, 128), f32), shape((n, 128), bf16)),
        in_specs=[SMEM] * 4
        + [whole(*a.shape) for a in (q, own, oth, pack, o, lse, seg)],
        out_specs=(whole(n, 128), whole(n, 128), whole(n, 128)),
        scratch_shapes=[
            pltpu.VMEM((n, 128), bf16),
            pltpu.VMEM((8, n), f32),
            pltpu.VMEM((n, 128), f32),
            pltpu.VMEM((128, n), f32),
            pltpu.VMEM((n, 128), f32),
            pltpu.VMEM((n, 128), f32),
        ],
        compiler_params=limits(60),
        cost_estimate=cost(120),
        name="attn_bwd",
    )(*ranges, q, own, oth, pack, o, lse, seg)


def heads_kernel(w_ref, gains_ref, seg_ref, sent_ref, wqkv_ref):
    left = left_lanes((32, 128))
    row = lax.broadcasted_iota(jnp.int32, (32, 128), 0)
    seg = jnp.broadcast_to(seg_ref[...], (32, 128))
    high, rest = (seg >> 6).astype(f32), (seg & 63).astype(f32)
    misc = jnp.broadcast_to(gains_ref[...], (32, 128))
    for k, part in enumerate((high, swapped(high), rest, swapped(rest))):
        misc = jnp.where(row == k + 1, part, misc)
    for p in range(HEADS // 2):
        q, k, v = (
            w_ref[:, 1024 * i + 128 * p : 1024 * i + 128 * (p + 1)].astype(f32) for i in range(3)
        )
        even = jnp.where(left, v, swapped(q)).astype(bf16)
        odd = jnp.where(left, swapped(v), q).astype(bf16)
        even_k = jnp.where(left, misc, swapped(k)).astype(bf16)
        odd_k = jnp.where(left, misc, k).astype(bf16)
        for c in range(2):
            sent_ref[4 * p + c, :, :128] = even
            sent_ref[4 * p + c, :, 128:] = even_k
            sent_ref[4 * p + 2 + c, :, :128] = odd
            sent_ref[4 * p + 2 + c, :, 128:] = odd_k
        wqkv_ref[:, 256 * p : 256 * p + 128] = even
        wqkv_ref[:, 256 * p + 128 : 256 * (p + 1)] = odd
        wqkv_ref[:, 2048 + 128 * p : 2048 + 128 * (p + 1)] = k.astype(bf16)


def heads_out(w, gains, seg):
    return pl.pallas_call(
        heads_kernel,
        out_shape=(shape((32, 32, 256), bf16), shape((32, 3072), bf16)),
        in_specs=[VMEM] * 3,
        out_specs=(VMEM, VMEM),
        compiler_params=limits(16),
        cost_estimate=cost(1),
        name="heads_out",
    )(w, gains, seg)


def unit_places():
    spread, pick = np.zeros((4, SPAN, 8 * SLOT)), np.zeros((4, SLOT, BLOCK))
    for z in range(4):
        for r in range(FIRST[z + 1] - FIRST[z]):
            pick[z, r, FIRST[z] + r] = 1
            for i in range(8):
                spread[z, BLOCK * i + FIRST[z] + r, SLOT * i + r] = 1
    return jnp.asarray(spread, bf16), jnp.asarray(pick, bf16)


def bundle_kernel(plane_ref, in_ref, spread_ref, pick_ref, mlp_ref, out_ref, bundle_ref, held):
    spread = spread_ref[plane_ref[0]]
    for k in range(8):
        part = dot_nn(in_ref[:, SPAN * k : SPAN * (k + 1)], spread)
        held[:, 8 * SLOT * k : 8 * SLOT * (k + 1)] = part
    for j in range(6):
        bundle_ref[32 * j : 32 * (j + 1), :] = held[:, 256 * j : 256 * (j + 1)].astype(bf16)
    mlp = dot_nn(pick_ref[plane_ref[0]], mlp_ref[...])
    parts = [mlp[:, 256 * j : 256 * (j + 1)] for j in range(4)]
    bundle_ref[192:OUT_FIRST, :] = jnp.concatenate(parts).astype(bf16)
    for j in range(4):
        cols = slice(256 * j, 256 * (j + 1))
        bundle_ref[OUT_FIRST + 32 * j : OUT_FIRST + 32 * (j + 1), :] = out_ref[:, cols]


def bundle_out(plane, w_in, spread, pick, w_mlp, w_out):
    return pl.pallas_call(
        bundle_kernel,
        out_shape=shape((BUNDLE, 256), bf16),
        in_specs=[SMEM] + [VMEM] * 5,
        out_specs=VMEM,
        scratch_shapes=[pltpu.VMEM((32, 2 * WIDE), f32)],
        compiler_params=limits(16),
        cost_estimate=cost(1),
        name="bundle_out",
    )(plane, w_in, spread, pick, w_mlp, w_out)


def turns():
    inverse = THETA ** (-np.arange(0, HDIM, 2) / HDIM)
    sign = np.repeat([-1.0, 1.0, -1.0, 1.0], 32)
    both = []
    for scale in (64, 1):
        angle = np.tile(np.arange(64)[:, None] * scale * inverse[None], (1, 4))
        table = np.concatenate([np.cos(angle), np.sin(angle) * sign], axis=1).astype(np.float32)
        main = table.astype(jnp.bfloat16)
        both.append(np.concatenate([main, (table - main.astype(np.float32)).astype(jnp.bfloat16)]))
    return jnp.asarray(np.stack(both), bf16)


def fill_tables(core, seg_ref, turn_ref, cos_ref, sin_ref):
    code = lax.broadcasted_iota(jnp.int32, (ROWS, ROWS), 0) & 63
    lane = lax.broadcasted_iota(jnp.int32, (1, ROWS), 1)
    for b in range(seg_ref.shape[1] // ROWS):
        rows = slice(b * ROWS, (b + 1) * ROWS)
        place = (2 * b + core) * ROWS + lane - seg_ref[:, rows]
        high = dot_tn((code == (place >> 6)).astype(f32).astype(bf16), turn_ref[0])
        rest = dot_tn((code == (place & 63)).astype(f32).astype(bf16), turn_ref[1])
        cos_ref[rows, :] = high[:, :128] * rest[:, :128] - high[:, 128:] * rest[:, 128:]
        sin_ref[rows, :] = high[:, 128:] * rest[:, :128] + high[:, :128] * rest[:, 128:]


def qkv_kernel(sizes, *refs):
    place = refs[0]
    pieces = refs[1 : 1 + len(sizes)]
    gain_ref, w_ref, seg_ref, turn_ref, n_ref, q_ref, k_ref, cos_ref, sin_ref = refs[1 + len(sizes) :]
    fill_tables(place[32], seg_ref, turn_ref, cos_ref, sin_ref)
    gain = gain_ref[...]
    w = w_ref[...]
    group = 0
    for piece, size in zip(pieces, sizes):
        z, _ = norm_parts(piece[...].astype(f32))
        normed = (z * gain).astype(bf16)
        both = dot_nn(normed, w)
        for g in range(size // 64):
            to = pl.ds(pl.multiple_of(place[group] * 64, 64), 64)
            group += 1
            mine = slice(g * 64, (g + 1) * 64)
            cos, sin = cos_ref[to, :], sin_ref[to, :]
            lane = lax.broadcasted_iota(jnp.int32, (64, 128), 1)

            def turn(t):
                other = jnp.where(lane < 96, pltpu.roll(t, 96, 1), pltpu.roll(t, 32, 1))
                return t * cos + other * sin

            first, second = both[mine, :128], both[mine, 128:]
            q_ref[to, :] = jnp.where(lane < HDIM, 0.0, turn(first) * (LOG2E * HDIM**-0.5)).astype(bf16)
            n_ref[to, :] = normed[mine]
            k_ref[to, :] = jnp.where(lane < HDIM, first, turn(second)).astype(bf16)


def qkv(place, pieces, gain, w, seg):
    n, width = seg.shape[1], pieces[0].shape[1]
    sizes = tuple(p.shape[0] for p in pieces)
    return pl.pallas_call(
        functools.partial(qkv_kernel, sizes),
        out_shape=(shape((n, width), bf16), shape((n, 128), bf16), shape((n, 128), bf16)),
        in_specs=[SMEM] + [VMEM] * (len(pieces) + 4),
        out_specs=(VMEM, VMEM, VMEM),
        scratch_shapes=[pltpu.VMEM((n, 128), f32)] * 2,
        compiler_params=limits(24),
        cost_estimate=cost(6),
        name="qkv",
    )(place, *pieces, gain, w, seg, turns())


OUT_PARTS = [weight_part(32, OUT_FIRST + 32 * j) for j in range(4)]


def proj_kernel(pack_ref, x_ref, gain_ref, w0, w1, w2, w3, n_ref, h_ref, o_ref):
    for p in range(HEADS // 2):
        both = unpack_pair(pack_ref[2 * p].astype(f32), pack_ref[2 * p + 1].astype(f32))
        o_ref[:, p * 128 : (p + 1) * 128] = both.astype(bf16)
    o = o_ref[...]
    for j, w in enumerate((w0, w1, w2, w3)):
        cols = slice(256 * j, 256 * (j + 1))
        h_ref[:, cols] = x_ref[:, cols].astype(f32) + dot_nn(o, w[...].reshape(1024, 256))
    z, _ = norm_parts(h_ref[...])
    n_ref[...] = (z * gain_ref[...]).astype(bf16)


def proj(pack, x, gain, bundle):
    n, width = x.shape
    return pl.pallas_call(
        proj_kernel,
        grid=(1,),
        out_shape=(shape((n, width), bf16), shape((n, width), f32), shape((n, width), bf16)),
        in_specs=[whole(*pack.shape), whole(n, width), whole(1, width), *OUT_PARTS],
        out_specs=(whole(n, width), whole(n, width), whole(n, width)),
        compiler_params=limits(58),
        cost_estimate=cost(3),
        name="proj",
    )(pack, x, gain, bundle, bundle, bundle, bundle)


def normal_cdf(x, bell):
    t = 1.0 / (1.0 + (0.3275911 * 0.5**0.5) * jnp.abs(x))
    tail = 1.061405429
    for term in (-1.453152027, 1.421413741, -0.284496736, 0.254829592):
        tail = tail * t + term
    tail = 0.5 * tail * t * bell
    return jnp.where(x >= 0.0, 1.0 - tail, tail)


def units_kernel(*refs):
    n_refs, g_refs = refs[:4], refs[4:8]
    win_ref, m_ref = refs[8], refs[9]
    act_ref, dup_ref, n_all, g_all, w_ref = refs[10:15]
    d_refs, w_in = refs[15:19], refs[19]
    for i in range(4):
        n_all[i * ROWS : (i + 1) * ROWS, :] = n_refs[i][...]
        g_all[i * ROWS : (i + 1) * ROWS, :] = g_refs[i][...]
    normed = n_all[...]
    g = g_all[...]

    slots = m_ref[...].astype(f32)
    for a in range(4):
        part = slots[:, SLOT * a : SLOT * (a + 1)].reshape(WIDE, 256)
        w_ref[:, 256 * a : 256 * (a + 1)] = part.astype(bf16)
    for j in range(6):
        w_in[:, 256 * j : 256 * (j + 1)] = win_ref[:, 32 * j : 32 * (j + 1), :].reshape(1024, 256)

    for j in range(3):
        cols = slice(256 * j, 256 * (j + 1))
        more = slice(WIDE + 256 * j, WIDE + 256 * (j + 1))
        first = dot_nn(normed, w_in[:, cols])
        second = dot_nn(normed, w_in[:, more])
        d_act = dot_nt(g, w_ref[cols, :])
        bell = jnp.exp(-0.5 * first * first)
        cdf = normal_cdf(first, bell)
        slope = cdf + first * (bell * (1.0 / (2.0 * np.pi) ** 0.5))
        gated = first * cdf
        act_ref[:, cols] = (gated * second).astype(bf16)
        dup_ref[:, cols] = (d_act * second * slope).astype(bf16)
        dup_ref[:, more] = (d_act * gated).astype(bf16)
    total = dot_nt(dup_ref[...], w_in[...])
    for i in range(4):
        d_refs[i][...] = total[i * ROWS : (i + 1) * ROWS].astype(bf16)


def units(normed, cots, bundle):
    n, width = normed[0].shape
    tokens = 4 * n
    return pl.pallas_call(
        units_kernel,
        grid=(1,),
        out_shape=(
            shape((tokens, WIDE), bf16),
            shape((tokens, 2 * WIDE), bf16),
            shape((tokens, width), bf16),
            shape((tokens, width), bf16),
            shape((WIDE, width), bf16),
            *[shape((n, width), bf16)] * 4,
        ),
        in_specs=[whole(n, width)] * 8
        + [weight_part(192, 0), weight_part(4 * SLOT, 192)],
        out_specs=(
            whole(tokens, WIDE),
            whole(tokens, 2 * WIDE),
            whole(tokens, width),
            whole(tokens, width),
            whole(WIDE, width),
            *[whole(n, width)] * 4,
        ),
        scratch_shapes=[pltpu.VMEM((width, 2 * WIDE), bf16)],
        compiler_params=limits(58),
        cost_estimate=cost(11),
        name="units",
    )(*normed, *cots, bundle, bundle)


def unit_grads_kernel(act_ref, dup_ref, n_all, g_all, out_hbm, out_ref, sem):
    act = act_ref[...].T
    grads = [dot_nn(act, g_all[:, 256 * a : 256 * (a + 1)]) for a in range(4)]
    for b in range(32):
        slot = jnp.concatenate([grad[SLOT * b : SLOT * (b + 1)] for grad in grads])
        out_ref[(b % 8) * 4 + b // 8, 192:OUT_FIRST, :] = slot.astype(bf16)
    normed = n_all[...].T
    for j in range(6):
        grad = dot_nn(normed, dup_ref[:, 256 * j : 256 * (j + 1)]).astype(bf16)
        for b in range(32):
            out_ref[(b % 8) * 4 + b // 8, 32 * j : 32 * (j + 1), :] = grad[32 * b : 32 * (b + 1)]
    copy = pltpu.make_async_copy(out_ref, out_hbm.at[:, pl.ds(0, OUT_FIRST)], sem)
    copy.start()
    copy.wait()


def unit_grads(act, dup, n_all, g_all):
    tokens, width = n_all.shape
    return pl.pallas_call(
        unit_grads_kernel,
        out_shape=shape((32, BUNDLE, 256), bf16),
        grid=(1,),
        in_specs=[whole(*a.shape) for a in (act, dup, n_all, g_all)],
        out_specs=HBM,
        scratch_shapes=[pltpu.VMEM((32, OUT_FIRST, 256), bf16), pltpu.SemaphoreType.DMA],
        compiler_params=limits(60),
        cost_estimate=cost(2),
        name="unit_grads",
    )(act, dup, n_all, g_all)


def out_grad_kernel(o_ref, da_ref, in_hbm, out_hbm, out_ref, sem):
    del in_hbm
    grad = dot_tn(o_ref[...], da_ref[...]).astype(bf16)
    for b in range(32):
        for j in range(4):
            out_ref[(b % 8) * 4 + b // 8, 32 * j : 32 * (j + 1), :] = grad[
                32 * b : 32 * (b + 1), 256 * j : 256 * (j + 1)
            ]
    copy = pltpu.make_async_copy(out_ref, out_hbm.at[:, pl.ds(OUT_FIRST, 128)], sem)
    copy.start()
    copy.wait()


def out_grad(o, da, grads):
    return pl.pallas_call(
        out_grad_kernel,
        out_shape=shape(grads.shape, bf16),
        grid=(1,),
        in_specs=[whole(*o.shape), whole(*da.shape), HBM],
        out_specs=HBM,
        scratch_shapes=[pltpu.VMEM((32, 128, 256), bf16), pltpu.SemaphoreType.DMA],
        input_output_aliases={2: 0},
        compiler_params=limits(60),
        cost_estimate=cost(1),
        name="out_grad",
    )(o, da, grads)


def unit_out_kernel(act_ref, w_ref, p0, p1, p2, p3):
    act = act_ref[...]
    for a in range(4):
        cols = slice(256 * a, 256 * (a + 1))
        part = dot_nn(act, w_ref[:, cols]).astype(bf16)
        for i, p in enumerate((p0, p1, p2, p3)):
            p[:, cols] = part[i * ROWS : (i + 1) * ROWS]


def unit_out(act, w):
    return pl.pallas_call(
        unit_out_kernel,
        grid=(1,),
        out_shape=[shape((ROWS, 1024), bf16)] * 4,
        in_specs=[whole(*act.shape), whole(*w.shape)],
        out_specs=[whole(ROWS, 1024)] * 4,
        compiler_params=limits(60),
        cost_estimate=cost(0.5),
        name="unit_out",
    )(act, w)


def proj_back_kernel(d0, d1, d2, d3, h_ref, gain_ref, cot_ref, w0, w1, w2, w3,
                     pack_ref, dh_ref, da_ref):
    total = d0[...].astype(f32) + d1[...].astype(f32) + d2[...].astype(f32) + d3[...].astype(f32)
    z, scale = norm_parts(h_ref[...])
    dh = cot_ref[...].astype(f32) + norm_back(total * gain_ref[...], z, scale)
    dh_ref[...] = dh
    da_ref[...] = dh.astype(bf16)
    do = sum(
        dot_nt(w[...].reshape(1024, 256), da_ref[:, 256 * j : 256 * (j + 1)])
        for j, w in enumerate((w0, w1, w2, w3))
    ).T
    for p in range(HEADS // 2):
        even, odd = pack_pair(do[:, p * 128 : (p + 1) * 128])
        pack_ref[2 * p] = even.astype(bf16)
        pack_ref[2 * p + 1] = odd.astype(bf16)


def proj_back(ds, h, gain, cot, bundle):
    n, width = h.shape
    return pl.pallas_call(
        proj_back_kernel,
        grid=(1,),
        out_shape=(shape((HEADS, 64, 128), bf16), shape((n, width), f32), shape((n, width), bf16)),
        in_specs=[whole(n, width)] * 5 + [whole(1, width), whole(n, width), *OUT_PARTS],
        out_specs=(whole(HEADS, 64, 128), whole(n, width), whole(n, width)),
        compiler_params=limits(58),
        cost_estimate=cost(3),
        name="proj_back",
    )(*ds, h, gain, cot, bundle, bundle, bundle, bundle)


def turn_back_kernel(core_ref, dq_ref, own_ref, oth_ref, seg_ref, turn_ref, n_ref,
                     sent_ref, keep_ref, give_ref, d_ref, grad_ref, held, cos_ref, sin_ref, sem):
    fetch = pltpu.make_async_copy(n_ref, held, sem)
    fetch.start()
    fill_tables(core_ref[0], seg_ref, turn_ref, cos_ref, sin_ref)
    for b in range(dq_ref.shape[0] // ROWS):
        s = slice(b * ROWS, (b + 1) * ROWS)
        cos, sin = cos_ref[s, :], sin_ref[s, :]
        lane = lax.broadcasted_iota(jnp.int32, (ROWS, 128), 1)

        def turn(t):
            other = jnp.where(lane < 96, pltpu.roll(t, 96, 1), pltpu.roll(t, 32, 1))
            return t * cos - other * sin

        dk = own_ref[s, :] + oth_ref[s, :].astype(f32)
        first = jnp.where(lane < HDIM, dk, turn(dq_ref[s, :].astype(f32)))
        second = jnp.where(lane < HDIM, 0.0, turn(dk))
        d_ref[s, :128] = first.astype(bf16)
        d_ref[s, 128:] = second.astype(bf16)
        sent_ref[b, :ROWS, :] = first.astype(bf16)
        packed = jnp.where(left_lanes((64, 128)), swapped(second[:64]), second[64:])
        sent_ref[b, ROWS:192, :] = packed.astype(bf16)
    fetch.wait()
    grad = dot_tn(d_ref[...], held[...]).T
    grad_ref[...] = grad.reshape(grad_ref.shape)
    core = core_ref[0]
    for h in range(HEADS):
        keep_ref[h] = grad_ref[2 * h + core]
        give_ref[h] = grad_ref[2 * h + 1 - core].astype(bf16)


def turn_back(core, dq, own, oth, seg, normed):
    n = dq.shape[0]
    return pl.pallas_call(
        turn_back_kernel,
        out_shape=(
            shape((HEADS, 192, 128), bf16),
            shape((HEADS, 32, 256), f32),
            shape((HEADS, 32, 256), bf16),
        ),
        grid=(1,),
        in_specs=[SMEM]
        + [whole(*a.shape) for a in (dq, own, oth, seg)]
        + [whole(2, ROWS, 256), HBM],
        out_specs=(whole(HEADS, 192, 128), whole(HEADS, 32, 256), whole(HEADS, 32, 256)),
        scratch_shapes=[
            pltpu.VMEM((n, 256), bf16),
            pltpu.VMEM((32, 32, 256), f32),
            pltpu.VMEM(normed.shape, bf16),
            pltpu.VMEM((n, 128), f32),
            pltpu.VMEM((n, 128), f32),
            pltpu.SemaphoreType.DMA,
        ],
        compiler_params=limits(60),
        cost_estimate=cost(5),
        name="turn_back",
    )(core, dq, own, oth, seg, turns(), normed)


def pack_kernel(keep_ref, took_ref, out_ref):
    left = left_lanes((16, 128))
    for h in range(HEADS):
        both = keep_ref[h] + took_ref[h].astype(f32)
        k = both[:, 128:]
        out_ref[h, :32, :] = both[:, :128].astype(bf16)
        out_ref[h, 32:, :] = jnp.where(left, swapped(k[:16]), k[16:]).astype(bf16)


def pack_head(keep, took):
    return pl.pallas_call(
        pack_kernel,
        grid=(1,),
        out_shape=shape((HEADS, 48, 128), bf16),
        in_specs=[whole(*keep.shape), whole(*took.shape)],
        out_specs=whole(HEADS, 48, 128),
        compiler_params=limits(58),
        cost_estimate=cost(1),
        name="pack_head",
    )(keep, took)


def input_kernel(got_ref, w_ref, x_ref, gain_ref, dh_ref, out_ref, d_ref, acc_ref):
    step = pl.program_id(0)

    @pl.when(step == 0)
    def _():
        for h in range(HEADS):
            d_ref[h // 4, :, 128 * (h % 4) : 128 * (h % 4 + 1)] = got_ref[h, :ROWS, :]
        for p in range(HEADS // 2):
            both = unpack_pair(
                got_ref[2 * p, ROWS:192, :].astype(f32), got_ref[2 * p + 1, ROWS:192, :].astype(f32)
            )
            d_ref[4 + p // 4, :, 128 * (p % 4) : 128 * (p % 4 + 1)] = both.astype(bf16)
        acc_ref[...] = jnp.zeros_like(acc_ref)

    acc_ref[...] += dot_nt(w_ref[...], d_ref[step])

    @pl.when(step == pl.num_programs(0) - 1)
    def _():
        z, scale = norm_parts(x_ref[...].astype(f32))
        back = norm_back(acc_ref[...].T * gain_ref[...], z, scale)
        out_ref[...] = (dh_ref[...] + back).astype(bf16)


def input_back(got, w, x, gain, dh):
    n, width = x.shape
    return pl.pallas_call(
        input_kernel,
        grid=(6,),
        out_shape=shape((n, width), bf16),
        in_specs=[
            whole(*got.shape),
            pl.BlockSpec((width, 512), lambda i: (0, i)),
            whole(n, width),
            whole(1, width),
            whole(n, width),
        ],
        out_specs=whole(n, width),
        scratch_shapes=[pltpu.VMEM((6, n, 512), bf16), pltpu.VMEM((width, n), f32)],
        compiler_params=limits(32),
        cost_estimate=cost(4),
        name="input_back",
    )(got, w, x, gain, dh)


def rows_kernel(got_ref, out_ref):
    left = left_lanes((32, 128))
    half = left_lanes((16, 128))
    for p in range(HEADS // 2):
        even, odd = (got_ref[2 * p + i, :32, :].astype(f32) for i in range(2))
        even_k, odd_k = (got_ref[2 * p + i, 32:, :].astype(f32) for i in range(2))
        q = jnp.where(left, swapped(even), odd)
        v = jnp.where(left, even, swapped(odd))
        k = jnp.concatenate(
            [jnp.where(half, even_k, swapped(odd_k)), jnp.where(half, swapped(even_k), odd_k)]
        )
        for i, part in enumerate((q, k, v)):
            j = 8 * i + p
            out_ref[32 * (j // 2) : 32 * (j // 2 + 1), 128 * (j % 2) : 128 * (j % 2 + 1)] = part.astype(bf16)


def gather_rows(got):
    return pl.pallas_call(
        rows_kernel,
        out_shape=shape((384, 256), bf16),
        in_specs=[VMEM],
        out_specs=VMEM,
        compiler_params=limits(16),
        cost_estimate=cost(1),
        name="gather_rows",
    )(got)


def as_row(column):
    full = jnp.concatenate([column, jnp.zeros((ROWS - 32, 1), f32)])
    return jnp.broadcast_to(full, (ROWS, ROWS)).T[0:1]


def planes_kernel(plane_ref, h0, h1, h2, h3, r0, r1, r2, r3, spread_ref, pick_ref, wqkv_ref, win_ref, g1_ref, g2_ref,
                  qkv_ref, out_ref, in_ref, mlp_ref, norm1_ref, norm2_ref, held):
    pieces = (r0, r1, r2, r3)
    planes = [plane_ref[k] for k in range(4)]

    def total(refs, first):
        return sum(r[first : first + 32, :].astype(f32) for r in refs)

    norm = jnp.zeros((32, 1), f32)
    for j in range(12):
        cols = slice(256 * j, 256 * (j + 1))
        part = total((h0, h1, h2, h3), 32 * j)
        qkv_ref[:, cols] = part
        norm += jnp.sum(part * wqkv_ref[:, cols].astype(f32), axis=1, keepdims=True)
    norm1_ref[...] = as_row(norm / g1_ref[...])
    all_slots = [r[192:OUT_FIRST, :].astype(f32) for r in pieces]
    for j in range(4):
        cols = slice(256 * j, 256 * (j + 1))
        out_ref[:, cols] = total(pieces, OUT_FIRST + 32 * j)
        slot = slice(SLOT * j, SLOT * (j + 1))
        mlp_ref[:, cols] = sum(
            dot_tn(pick_ref[z], slots[slot].astype(bf16)) for z, slots in zip(planes, all_slots)
        )
    grads = jnp.zeros((256, SPAN), f32)
    for z, r in zip(planes, pieces):
        wide = jnp.concatenate([r[32 * j : 32 * (j + 1), :] for j in range(6)], axis=1)
        for k in range(8):
            held[32 * k : 32 * (k + 1), :] = wide[:, 8 * SLOT * k : 8 * SLOT * (k + 1)]
        grads += dot_nt(held[...], spread_ref[z])
    norm = jnp.zeros((32, 1), f32)
    for k in range(8):
        cols = slice(SPAN * k, SPAN * (k + 1))
        part = grads[32 * k : 32 * (k + 1)]
        in_ref[:, cols] = part
        norm += jnp.sum(part * win_ref[:, cols].astype(f32), axis=1, keepdims=True)
    norm2_ref[...] = as_row(norm / g2_ref[...])


def add_planes(plane, heads, parts, spread, pick, wqkv, win, gain_one, gain_two):
    return pl.pallas_call(
        planes_kernel,
        out_shape=(
            shape(wqkv.shape, f32),
            shape((32, 1024), f32),
            shape(win.shape, f32),
            shape((BLOCK, 1024), f32),
            shape((1, ROWS), f32),
            shape((1, ROWS), f32),
        ),
        in_specs=[SMEM] + [VMEM] * 14,
        out_specs=(VMEM,) * 6,
        scratch_shapes=[pltpu.VMEM((256, 8 * SLOT), bf16)],
        compiler_params=limits(24),
        cost_estimate=cost(5),
        name="add_planes",
    )(plane, *heads, *parts, spread, pick, wqkv, win, gain_one, gain_two)


def shift(value, axis, steps):
    count = lax.axis_size(axis)
    return lax.ppermute(value, axis, [(i, (i + steps) % count) for i in range(count)])


def both_ways(value, axis):
    first = [(2 * i + c, (2 * i + 2 - 4 * c) % 8 + c) for i in range(4) for c in range(2)]
    other = [(b, a) for a, b in first]
    near = lax.ppermute(value, (axis, "c"), first)
    return [value, near, lax.ppermute(value, (axis, "c"), other), lax.ppermute(near, (axis, "c"), first)]


def from_planes(value):
    return [value] + [shift(value, "z", k) for k in SHIFTS[1:]]


def back_to_planes(pieces):
    return [pieces[0]] + [shift(p, "z", -k) for p, k in zip(pieces[1:], SHIFTS[1:])]


def far(value, near, axis):
    half = value.shape[0] // 2
    behind, ahead = near
    return [value, behind, ahead, shift(behind[:half], axis, 1), shift(ahead[half:], axis, 3)]


def exchange(value, axes):
    return lax.all_to_all(value, axes, split_axis=0, concat_axis=0, tiled=True)


def shards(hidden_in, seg_start, norm1_gain, qkv_weight, out_weight, norm2_gain, in_weight,
           mlp_weight, out_cotangent):
    plane, core = lax.axis_index("z"), lax.axis_index("c")
    mine = (lax.axis_index("x"), lax.axis_index("y"))
    plane_id, core_id = plane.astype(jnp.int32)[None], core.astype(jnp.int32)[None]
    x_own = hidden_in[0]
    cot = out_cotangent[0]
    width = x_own.shape[1]
    rows = qkv_weight.shape[0]

    upper, lower = x_own[:64], x_own[64:]
    upper = [upper] + [shift(upper, "x", k) for k in SHIFTS[1:]]
    lower = [lower] + [shift(lower, "y", k) for k in SHIFTS[1:]]
    upper, lower = jnp.concatenate(upper), jnp.concatenate(lower)

    gains = jnp.pad(jnp.concatenate([norm1_gain, norm2_gain]), (0, HDIM)).astype(f32)[None]
    sent, wqkv = heads_out(qkv_weight, gains, seg_start)
    spread, pick = unit_places()
    bundle = bundle_out(plane_id, in_weight, spread, pick, mlp_weight, out_weight)
    upper, lower, sent = lax.optimization_barrier((upper, lower, sent))
    got = exchange(sent, XYC)
    pieces = both_ways(upper, "y") + both_ways(lower, "x")
    steps = (0, 1 - 2 * core, 2 * core - 1, 2)
    place = []
    for half in (0, 1):
        for outer in steps:
            for inner in SHIFTS:
                sx, sy = (inner, outer) if half == 0 else (outer, inner)
                place.append((((mine[0] - sx) % 4) * 4 + (mine[1] - sy) % 4) * 2 + half)
    place = jnp.stack([*place, core]).astype(jnp.int32)
    w_head = got.reshape(width, 256)
    gain_one = got[:, 0, 128:160].reshape(1, width).astype(f32)
    gain_two = got[:, 0, 160:192].reshape(1, width).astype(f32)
    high, rest = got[:, 1:3, 128:192].astype(jnp.int32), got[:, 3:5, 128:192].astype(jnp.int32)
    seg_all = (high * 64 + rest).reshape(HEADS, 2, ROWS)
    seg_own = jnp.where(core == 0, seg_all[:, 0], seg_all[:, 1]).reshape(-1)
    seg_oth = jnp.where(core == 0, seg_all[:, 1], seg_all[:, 0]).reshape(-1)
    pieces, seg_own, seg_oth, gain_one, gain_two, bundle = lax.optimization_barrier(
        (pieces, seg_own, seg_oth, gain_one, gain_two, bundle)
    )
    bundle = lax.all_gather(bundle, XYC, axis=0, tiled=False)


    normed_one, queries, keys = qkv(place, pieces, gain_one, w_head, seg_own[None])
    keys_oth = shift(keys, "c", 1)

    def bounds(seg, size):
        tiles = seg.reshape(-1, size)
        return tiles[:, 0], tiles[:, -1]

    (qlo, qhi), (olo, ohi), (tlo, thi) = bounds(seg_own, 256), bounds(seg_own, 1024), bounds(seg_oth, 1024)
    both_segs = jnp.stack([seg_own, seg_oth]).astype(f32)
    o_pack, o, lse = attn_fwd(
        256, 1024, 2, (qlo, qhi, jnp.minimum(olo, tlo), jnp.maximum(ohi, thi)),
        queries, keys, keys_oth, both_segs,
    )
    o_pack, cot = lax.optimization_barrier((o_pack, cot))
    cots = from_planes(cot)
    o_got = exchange(o_pack, XY)
    wqkv, o_got, cots = lax.optimization_barrier((wqkv, o_got, cots))
    wqkv = lax.all_gather(wqkv, XYC, axis=0, tiled=True)

    normed_two, middle, o_tok = proj(o_got, x_own, gain_two, bundle)
    act, dup, n_all, g_all, w_units, *d_parts = units(from_planes(normed_two), cots, bundle)
    d_parts = back_to_planes(d_parts)
    g_sum = unit_grads(act, dup, n_all, g_all)
    d_parts, g_sum = lax.optimization_barrier((d_parts, g_sum))
    do_pack, d_mid, d_attn = proj_back(d_parts, middle, gain_two, cot, bundle)
    do_got = exchange(do_pack, XY)
    act, d_attn = lax.optimization_barrier((act, d_attn))
    g_sum = out_grad(o_tok, d_attn, g_sum)
    out_parts = unit_out(act, w_units)
    do_got, out_parts = lax.optimization_barrier((do_got, out_parts))
    g_sum, wqkv = lax.optimization_barrier((g_sum, wqkv))
    g_sum = lax.psum_scatter(g_sum.reshape(8, 4 * BUNDLE, 256), YC, scatter_dimension=0, tiled=False)

    (qlo, qhi), (tlo, thi) = bounds(seg_own, 512), bounds(seg_oth, 512)
    ranges = (qlo, qhi, jnp.stack([qlo, tlo]), jnp.stack([qhi, thi]))
    dq, dk_own, dk_oth = attn_bwd(512, 4, 2, ranges, queries, keys, keys_oth, do_got, o, lse, both_segs)
    dk_oth, out_parts = lax.optimization_barrier((dk_oth, out_parts))
    out_parts = back_to_planes(out_parts)
    d_sent, keep, give = turn_back(core_id, dq, dk_own, shift(dk_oth, "c", 1), seg_own[None], normed_one)

    give, out_parts = lax.optimization_barrier((give, out_parts))
    g_head = pack_head(keep, shift(give, "c", 1))
    g_head, g_sum = lax.optimization_barrier((g_head, g_sum))
    g_head = exchange(g_head, XY)
    g_sum = lax.psum_scatter(g_sum.reshape(4, BUNDLE, 256), "x", scatter_dimension=0, tiled=False)
    g_head, d_sent = lax.optimization_barrier((g_head, d_sent))
    d_got = exchange(d_sent, XY)
    heads = gather_rows(g_head)

    heads, g_rows = from_planes(heads), from_planes(g_sum)
    input_grad = input_back(d_got, wqkv, x_own, gain_one, d_mid)
    hidden_out = (middle + sum(p.astype(f32) for p in out_parts)).astype(bf16)
    heads, g_rows, input_grad, hidden_out = lax.optimization_barrier(
        (heads, g_rows, input_grad, hidden_out)
    )
    g_qkv, g_out, g_in, g_mlp, grad_one, grad_two = add_planes(
        jnp.stack([(plane - k) % 4 for k in SHIFTS]).astype(jnp.int32), heads, g_rows, spread, pick,
        qkv_weight, in_weight,
        norm1_gain.astype(f32)[:, None], norm2_gain.astype(f32)[:, None],
    )
    return (
        hidden_out[None],
        input_grad[None],
        g_qkv,
        g_out,
        g_in,
        g_mlp,
        grad_one[0, :32],
        grad_two[0, :32],
    )


def solution(mesh):
    fine = Mesh(mesh.devices.reshape(4, 4, 4, 2), ("z", "x", "y", "c"))
    blk = ("x", "y", "c")
    return jax.shard_map(
        shards,
        mesh=fine,
        in_specs=(
            P("z", blk, None),
            P("z", blk),
            P(blk),
            P(blk, None),
            P(blk, None),
            P(blk),
            P(blk, None),
            P(blk, None),
            P("z", blk, None),
        ),
        out_specs=(
            P("z", blk, None),
            P("z", blk, None),
            P(blk, None),
            P(blk, None),
            P(blk, None),
            P(blk, None),
            P(blk),
            P(blk),
        ),
        check_vma=False,
    )
```
